32 devices in a mesh: atoms: 8 (over z, core), kvec: 4 (over y, x).
Axes of the slice: x: 2, y: 2, z: 4, core: 2. Of those that a mesh axis runs over, the one named last changes fastest.
Arguments:
- positions: float32 [3, 16384], P(None, 'atoms'), may hold values from 0 to 1
- feats: float32 [64, 16384], P(None, 'atoms'), may hold values from -6 to 6
- species: int32 [16384], P('atoms'), may hold values from 0 to 15
- pad_count: int32 [64], P('atoms'), may hold values from 128 to 256
- k_lattice: int32 [3, 1024], P(None, 'kvec'), may hold values from -12 to 13, as said below
- filter_width: float32 [64], replicated, may hold values from 2e-05 to 0.002
- w_charge: float32 [64, 64], replicated, may hold values from -0.75 to 0.75
- species_embed: float32 [64, 16], replicated, may hold values from -3 to 3
- w_out: float32 [64, 64], replicated, may hold values from -0.75 to 0.75
- grad_out: float32 [64, 16384], P(None, ('atoms', 'kvec')), may hold values from -6 to 6
Outputs:
- message: float32 [64, 16384], P(None, ('atoms', 'kvec'))
- grad_positions: float32 [3, 16384], P(None, ('atoms', 'kvec'))
- grad_feats: float32 [64, 16384], P(None, ('atoms', 'kvec'))
The draws below stay inside these ranges and needn't reach their ends.
Inputs may be any that keep to these rules, and one draw needn't show every extreme that they name: `k_lattice`: the 1024 columns are distinct nonzero integer vectors k with k[0] > 0, or k[0] = 0 and k[1] > 0, or k[0] = k[1] = 0 and k[2] > 0, and with squared length at most 169.
All inputs are finite; a program needn't handle non-finite values.
Results may differ from the reference program's by a relative error of at most 0.0003.
Values sent between devices are 32-bit elements; how exact they have to be, the bound alone decides.
No kernel may reach another device: no remote copies, remote signals or barrier semaphores. Data moves between devices by JAX's collectives and lax.ppermute only.
A program may use at most 64 MiB of HBM per device.

```python
import math
import jax
import jax.numpy as jnp
from jax import lax

C = 64
NSPEC = 16
NATOM = 16384
NBLK = 64
KVEC = 1024


def draw_k_lattice(key, part):
    key = jax.random.fold_in(key, 7)
    extremes = [[13, 0, 0], [0, 1, -12]]
    others = []
    for comp_one in range(-13, 14):
        for comp_two in range(-13, 14):
            for comp_three in range(-13, 14):
                upper = comp_one > 0 or (comp_one == 0 and comp_two > 0) or (comp_one == 0 and comp_two == 0 and (comp_three > 0))
                inside = comp_one * comp_one + comp_two * comp_two + comp_three * comp_three <= 169
                point = [comp_one, comp_two, comp_three]
                if upper and inside and (point not in extremes):
                    others.append(point)
    lattice_table = jnp.asarray(extremes + others, jnp.int32).T
    other_count = len(others)
    key_one, key_two = jax.random.split(key)
    shuffled = jax.random.permutation(key_one, other_count)[:KVEC - 2] + 2
    chosen = jnp.concatenate([jnp.arange(2, dtype=jnp.int32), shuffled.astype(jnp.int32)])
    chosen = jax.random.permutation(key_two, chosen)
    return jnp.take(lattice_table, chosen, axis=1)


def plant(entries, stream_key, smallest, top_value):
    extent = entries.shape
    place = [jax.random.randint(jax.random.fold_in(stream_key, axis), (), 0, extent[axis]) for axis in range(len(extent))]
    entries = entries.at[tuple(place)].set(smallest)
    longest = extent.index(max(extent))
    place[longest] = (place[longest] + 1) % extent[longest]
    return entries.at[tuple(place)].set(top_value)


def block_scale(rng, dims, cuts, least, top_value):
    def one(dim, parts):
        steps = jax.random.uniform(jax.random.fold_in(jax.random.fold_in(rng, 6), dim), (parts,), jnp.float32, least / len(cuts), top_value / len(cuts))
        return jnp.repeat(jnp.exp(steps), dims[dim] // parts).reshape((-1,) + (1,) * (len(dims) - dim - 1))

    loudness = one(*cuts[0])
    for cut in cuts[1:]:
        loudness = loudness * one(*cut)
    return loudness


def noise(stream_key, dims, spread, limit, cuts=(), held_as=jnp.bfloat16):
    loudness = block_scale(stream_key, dims, cuts, -0.22, 0.18) if cuts else 1.0
    entries = jax.random.normal(stream_key, dims, jnp.float32) * spread * loudness
    return jnp.minimum(jnp.maximum(entries, -limit), limit).astype(held_as)


def setup_inputs(seed: int = 0) -> dict:
    arg_keys = jax.random.split(jax.random.key(seed), 11)
    positions = jnp.clip(1.0 * jax.random.uniform(arg_keys[0], (3, NATOM), jnp.float32) ** block_scale(arg_keys[0], (3, NATOM), ((1, 8),), -0.2, 0.2), 0.0, 1.0)
    feats = noise(arg_keys[1], (C, NATOM), 1.0, 6.0, ((1, 8),), jnp.float32)
    species = plant(jax.random.randint(arg_keys[2], (NATOM,), 0, NSPEC), jax.random.fold_in(arg_keys[2], 1), 0, NSPEC - 1).astype(jnp.int32)
    pad_count = plant(jax.random.randint(arg_keys[3], (NBLK,), 128, 257), jax.random.fold_in(arg_keys[3], 1), 128, 256).astype(jnp.int32)
    k_lattice = draw_k_lattice(jax.random.fold_in(arg_keys[10], 71), 0)
    filter_width = jnp.clip(jnp.exp(jax.random.uniform(arg_keys[5], (C,), jnp.float32, math.log(1.9999999494757503e-05), math.log(0.002))), 1.9999999494757503e-05, 0.002)
    w_charge = noise(arg_keys[6], (C, C), C ** -0.5, 0.75, (), jnp.float32)
    species_embed = noise(arg_keys[7], (C, NSPEC), 0.5, 3.0, (), jnp.float32)
    w_out = noise(arg_keys[8], (C, C), C ** -0.5, 0.75, (), jnp.float32)
    grad_out = noise(arg_keys[9], (C, NATOM), 1.0, 6.0, ((1, 32),), jnp.float32)
    return {"positions": positions, "feats": feats, "species": species, "pad_count": pad_count, "k_lattice": k_lattice, "filter_width": filter_width, "w_charge": w_charge, "species_embed": species_embed, "w_out": w_out, "grad_out": grad_out}


exact = lax.Precision.HIGHEST
two_pi = 2.0 * math.pi

def reference(positions, feats, species, pad_count, k_lattice, filter_width, w_charge, species_embed, w_out, grad_out):
    block = 2048
    block_count = NATOM // block
    valid_mask = (jnp.arange(NATOM) % 256 < jnp.repeat(pad_count, 256)).astype(jnp.float32)
    charges = valid_mask[None, :] * (jnp.dot(w_charge.T, feats, precision=exact) + species_embed[:, species])
    wave_vec = two_pi * k_lattice.astype(jnp.float32)
    k_square = lax.optimization_barrier(jnp.sum(wave_vec * wave_vec, axis=0))
    filter_gain = jnp.exp(-k_square[:, None] * filter_width[None, :]) * 40.0 / (k_square[:, None] + 40.0) / math.sqrt(NATOM)

    def blocks(array):
        return array.reshape(array.shape[0], block_count, block).transpose(1, 0, 2)

    def unblock(array):
        return array.transpose(1, 0, 2).reshape(array.shape[1], NATOM)
    pos_blocks = blocks(positions)
    charge_blocks = blocks(charges)
    mask_blocks = valid_mask.reshape(block_count, block)
    cot_blocks = blocks(grad_out)

    def trig(pos_block):
        phase = jnp.dot(pos_block.T, wave_vec, precision=exact)
        return (jnp.cos(phase), jnp.sin(phase))

    def pass_one(carry, items):
        pos_block, charge_block = items
        cos_tile, sine_tile = trig(pos_block)
        part_cos = jnp.einsum('aj,ca->jc', cos_tile, charge_block, precision=exact)
        part_sin = jnp.einsum('aj,ca->jc', sine_tile, charge_block, precision=exact)
        return ((carry[0] + part_cos, carry[1] + part_sin), jnp.float32(0.0))
    zero_kc = jnp.zeros((KVEC, C), jnp.float32)
    (sf_cos, sf_sin), _ = lax.scan(pass_one, (zero_kc, zero_kc), (pos_blocks, charge_blocks))
    h_cos = filter_gain * sf_cos
    h_sin = filter_gain * sf_sin

    def pass_two(carry, items):
        pos_block, mask_block, cot_block = items
        cos_tile, sine_tile = trig(pos_block)
        field_out = mask_block[None, :] * (jnp.einsum('aj,jc->ca', cos_tile, h_cos, precision=exact) + jnp.einsum('aj,jc->ca', sine_tile, h_sin, precision=exact))
        message = jnp.dot(w_out.T, field_out, precision=exact)
        adjoint = mask_block[None, :] * jnp.dot(w_out, cot_block, precision=exact)
        part_cos = jnp.einsum('aj,ca->jc', cos_tile, adjoint, precision=exact)
        part_sin = jnp.einsum('aj,ca->jc', sine_tile, adjoint, precision=exact)
        return ((carry[0] + part_cos, carry[1] + part_sin), (message, adjoint))
    (e_cos, e_sin), (message_blocks, adjoint_blocks) = lax.scan(pass_two, (zero_kc, zero_kc), (pos_blocks, mask_blocks, cot_blocks))
    b_cos = filter_gain * e_cos
    b_sin = filter_gain * e_sin

    def pass_three(carry, items):
        pos_block, charge_block, mask_block, adjoint = items
        cos_tile, sine_tile = trig(pos_block)
        charge_grad = jnp.einsum('aj,jc->ca', cos_tile, b_cos, precision=exact) + jnp.einsum('aj,jc->ca', sine_tile, b_sin, precision=exact)
        feat_grad = jnp.dot(w_charge, mask_block[None, :] * charge_grad, precision=exact)
        along_sin = jnp.einsum('ca,jc->aj', adjoint, h_sin, precision=exact) + jnp.einsum('ca,jc->aj', charge_block, b_sin, precision=exact)
        along_cos = jnp.einsum('ca,jc->aj', adjoint, h_cos, precision=exact) + jnp.einsum('ca,jc->aj', charge_block, b_cos, precision=exact)
        dphase = cos_tile * along_sin - sine_tile * along_cos
        force_part = jnp.einsum('xj,aj->xa', wave_vec, dphase, precision=exact)
        return (carry, (force_part, feat_grad))
    _, (force_blocks, feat_blocks) = lax.scan(pass_three, jnp.float32(0.0), (pos_blocks, charge_blocks, mask_blocks, adjoint_blocks))
    return (unblock(message_blocks), unblock(force_blocks), unblock(feat_blocks))
```

```python
import functools
import math

import jax
import jax.numpy as jnp
from jax import lax
from jax.experimental import pallas as pl
from jax.experimental.pallas import tpu as pltpu
from jax.sharding import PartitionSpec as P

F32, BF16 = jnp.float32, jnp.bfloat16
HALF_SIN = (4.442867755889893, -7.307443618774414, 3.594788074493408, -0.7843740582466125)
HALF_COS = (1.4142135381698608, -6.978850841522217, 5.7394609451293945, -1.8835630416870117, 0.31069818139076233)
VMEM = pl.BlockSpec(memory_space=pltpu.VMEM)
SMEM = pl.BlockSpec(memory_space=pltpu.SMEM)
ANY = pl.BlockSpec(memory_space=pl.ANY)
PARAMS = pltpu.CompilerParams(vmem_limit_bytes=32 * 2**20)
NN, NT, TN = ((1,), (0,)), ((1,), (1,)), ((0,), (0,))


def halves(value):
    high = value.astype(BF16)
    return high, (value - high.astype(F32)).astype(BF16)


def dot16(left, right, dims):
    return lax.dot_general(left, right, (dims, ((), ())), preferred_element_type=F32)


def dot3(left, right, dims):
    left_high, left_low = halves(left)
    right_high, right_low = halves(right)
    return (
        dot16(left_high, right_high, dims)
        + dot16(left_low, right_high, dims)
        + dot16(left_high, right_low, dims)
    )


def horner(terms, square):
    total = terms[-1] * square + terms[-2]
    for term in terms[-3::-1]:
        total = total * square + term
    return total


def trig(columns, rows):
    turns = columns[0] * rows[0] + columns[1] * rows[1] + columns[2] * rows[2]
    turns = turns - jnp.round(turns)
    square = turns * turns
    half_sin = horner(HALF_SIN, square) * turns
    return 1.0 - half_sin * half_sin, half_sin * horner(HALF_COS, square)


def trig_blocks(k_ref, pos_ref, first, high_low, full=None):
    vectors, atoms = high_low[0].shape
    step = 32
    width = min(256, atoms)
    per_body = max(1, 2048 // atoms)
    per_body = min(per_body, vectors // step)

    def body(block, _):
        for inner in range(per_body):
            here = pl.ds(pl.multiple_of((block * per_body + inner) * step, step), step)
            columns = [k_ref[here, x : x + 1] for x in range(3)]
            for chunk in range(atoms // width):
                lanes = pl.ds(chunk * width, width)
                start = chunk * width if first is None else pl.multiple_of(first + chunk * width, 128)
                rows = [pos_ref[x : x + 1, pl.ds(start, width)] for x in range(3)]
                cos, sin = trig(columns, rows)
                high_low[0][here, lanes], high_low[1][here, lanes] = halves(cos)
                high_low[2][here, lanes], high_low[3][here, lanes] = halves(sin)
                if full is not None:
                    full[0][here, lanes], full[1][here, lanes] = cos, sin
        return 0

    lax.fori_loop(0, vectors // (step * per_body), body, 0)


def tile_kernel(pos_ref, k_ref, cos_high, cos_low, sin_high, sin_low, k_column):
    k_column[:, 0:3] = k_ref[...].astype(F32).T
    trig_blocks(k_column, pos_ref, None, (cos_high, cos_low, sin_high, sin_low))


def sums_kernel(
    here_ref, pad_ref, cos_high, cos_low, sin_high, sin_low, feats_ref, species_ref, w_charge_ref, embed_ref, w_out_ref,
    *rest, groups,
):
    cotangents = rest[:groups]
    keep_ref, send_ref, own_ref, mask_ref, both, total = rest[-6:]
    channels, atoms = feats_ref.shape
    share = cotangents[0].shape[1]
    place, group = here_ref[0], here_ref[1]
    embed_high, embed_low = halves(embed_ref[...])
    for block in range(atoms // 256):
        lanes = slice(block * 256, (block + 1) * 256)
        mask = (lax.broadcasted_iota(jnp.int32, (1, 256), 1) < pad_ref[block]).astype(F32)
        mask_ref[:, lanes] = mask
        species_at = lax.broadcasted_iota(jnp.int32, (embed_ref.shape[0], 256), 0)
        one_hot = (species_at == species_ref[:, lanes]).astype(BF16)
        both[0:channels, lanes] = mask * (
            dot3(w_charge_ref[...], feats_ref[:, lanes], TN)
            + dot16(embed_high, one_hot, TN)
            + dot16(embed_low, one_hot, TN)
        )
    for offset, cotangent in enumerate(cotangents):
        lanes = pl.ds(pl.multiple_of((group ^ offset) * share, share), share)
        adjoint = mask_ref[:, lanes] * dot3(w_out_ref[...], cotangent[...], NN)
        both[channels:, lanes] = adjoint
        if offset == 0:
            own_ref[0:channels, :] = adjoint
            own_ref[channels : 2 * channels, :] = both[0:channels, lanes]
            own_ref[2 * channels :, :] = jnp.broadcast_to(mask_ref[:, lanes], (8, share))
    high, low = halves(both[...])
    pair = jnp.concatenate([high, low], axis=0)
    for part, (tile_high, tile_low) in enumerate(((cos_high, cos_low), (sin_high, sin_low))):
        wide = dot16(tile_high[...], pair, NT)
        total[part] = (
            wide[:, : 2 * channels] + wide[:, 2 * channels :] + dot16(tile_low[...], high, NT)
        )
    rows = keep_ref.shape[1]
    core = place & 1
    for flip, out in enumerate((keep_ref, send_ref)):
        start = pl.multiple_of((core ^ flip) * rows, rows)
        for part in range(2):
            out[part] = total[part, pl.ds(start, rows), :]


def gain_kernel(here_ref, width_ref, k_ref, gain_ref, *, atom_total):
    rows = gain_ref.shape[0]
    start = pl.multiple_of((here_ref[0] & 1) * rows, rows)
    waves = [2.0 * math.pi * k_ref[pl.ds(start, rows), x : x + 1] for x in range(3)]
    square = waves[0] * waves[0] + waves[1] * waves[1] + waves[2] * waves[2]
    gain = jnp.exp(-square * width_ref[...]) * 40.0 / (square + 40.0) / math.sqrt(atom_total)
    gain_ref[...] = jnp.concatenate([gain, gain], axis=1)


def wave_kernel(here_ref, pos_ref, lattice_ref, after_ref, cos, sin, cos_high, cos_low, sin_high, sin_low, k_ref, k_column):
    rows = lattice_ref.shape[1] // 2
    k_column[:, 0:3] = lattice_ref[...].astype(F32).T
    for flip in range(2):
        start = pl.multiple_of(((here_ref[0] & 1) ^ flip) * rows, rows)
        k_ref[flip * rows : (flip + 1) * rows, :] = k_column[pl.ds(start, rows), :]
    first = here_ref[1] * cos.shape[1]
    trig_blocks(k_ref, pos_ref, first, (cos_high, cos_low, sin_high, sin_low), (cos, sin))


def coefficient_stack(near_ref, far_ref, part):
    high, low = halves(jnp.concatenate([near_ref[part], far_ref[part]], axis=0))
    return jnp.concatenate([high, low, high], axis=1)


def own_stack(own_ref, channels):
    high, low = halves(own_ref[0 : 2 * channels, :])
    return jnp.concatenate([high, high, low], axis=0)


def add_field(stack, tile_high, tile_low):
    width = stack.shape[1] // 3
    wide = dot16(stack[:, : 2 * width], tile_high, TN)
    return wide[:width] + wide[width:] + dot16(stack[:, :width], tile_low, TN)


def add_force(sums, rows, get):
    step = 16
    for block in range(rows // step):
        cos, sin, along_cos, along_sin, columns = get(block * step, step)
        slope = cos * along_sin - sin * along_cos
        for x in range(3):
            term = columns[:, x : x + 1] * slope
            sums[x] = sums[x] + (term[0:8] + term[8:16])
    return sums


def own_field_kernel(
    here_ref, cos_high, cos_low, sin_high, sin_low, k_ref, own_ref, near_ref, far_ref,
    field_ref, sums_ref, k_column, along, *tiles,
):
    share = own_ref.shape[1]
    rows = near_ref.shape[1]
    channels = near_ref.shape[2] // 2
    lanes = pl.ds(pl.multiple_of(here_ref[1] * share, share), share)
    for flip in range(2):
        here = pl.ds(pl.multiple_of(((here_ref[0] & 1) ^ flip) * rows, rows), rows)
        to = slice(flip * rows, (flip + 1) * rows)
        k_column[to, :] = k_ref[here, :]
        for tile, source in zip(tiles, (cos_high, cos_low, sin_high, sin_low)):
            tile[to, :] = source[here, lanes]
    other = own_stack(own_ref, channels)
    stacks = [coefficient_stack(near_ref, far_ref, part) for part in range(2)]
    for part in range(2):
        along[part] = dot16(stacks[part], other, NN)
    field_ref[...] = add_field(stacks[0], tiles[0][...], tiles[1][...]) + add_field(
        stacks[1], tiles[2][...], tiles[3][...]
    )

    def get(first, step):
        at = slice(first, first + step)
        cos = tiles[0][at, :].astype(F32) + tiles[1][at, :].astype(F32)
        sin = tiles[2][at, :].astype(F32) + tiles[3][at, :].astype(F32)
        return cos, sin, along[0, at, :], along[1, at, :], k_column[at, 0:3]

    sums = add_force([jnp.zeros((8, share), F32)] * 3, 2 * rows, get)
    for x in range(3):
        sums_ref[8 * x : 8 * x + 8, :] = sums[x]


def field_kernel(own_ref, w_out_ref, w_charge_ref, field_ref, sums_ref, *rest, groups):
    *waves, message_ref, force_ref, grad_ref, along = rest
    waves, coefs = waves[: 7 * groups], waves[7 * groups :]
    channels = w_out_ref.shape[0]
    share = own_ref.shape[1]
    rows = 2 * coefs[0].shape[1]
    other = own_stack(own_ref, channels)
    parts = [[coefficient_stack(coefs[2 * g], coefs[2 * g + 1], part) for g in range(groups)] for part in range(2)]
    for part in range(2):
        along[part] = dot16(jnp.concatenate(parts[part], axis=0), other, NN)
    field = field_ref[...]
    sums = [sums_ref[8 * x : 8 * x + 8, :] for x in range(3)]
    for g in range(groups):
        cos, sin, cos_high, cos_low, sin_high, sin_low, k_ref = waves[7 * g : 7 * g + 7]
        field += add_field(parts[0][g], cos_high[...], cos_low[...])
        field += add_field(parts[1][g], sin_high[...], sin_low[...])
    field = own_ref[2 * channels : 2 * channels + 1, :] * field
    message_ref[...] = dot3(w_out_ref[...], field[:channels], TN)
    grad_ref[...] = dot3(w_charge_ref[...], field[channels:], NN)
    for g in range(groups):
        cos, sin, _, _, _, _, k_ref = waves[7 * g : 7 * g + 7]

        def get(first, step):
            at = slice(first, first + step)
            there = slice(g * rows + first, g * rows + first + step)
            return cos[at, :], sin[at, :], along[0, there, :], along[1, there, :], k_ref[at, 0:3]

        sums = add_force(sums, rows, get)
    for x in range(3):
        force_ref[x : x + 1, :] = 2.0 * math.pi * jnp.sum(sums[x], axis=0, keepdims=True)


def swap(value, axis, offset):
    size = lax.axis_size(axis)
    return lax.ppermute(value, axis, [(place, place ^ offset) for place in range(size)])


def cost(work):
    return pl.CostEstimate(flops=work, bytes_accessed=0, transcendentals=0)


def on_device(
    positions, feats, species, pad_count, k_lattice, filter_width, w_charge, species_embed, w_out, grad_out,
):
    atom_count, group_count = lax.axis_size("atoms"), lax.axis_size("kvec")
    channels, atoms = feats.shape
    share = grad_out.shape[1]
    vectors = k_lattice.shape[1]
    half = vectors // 2
    both = 2 * channels
    here = jnp.stack([lax.axis_index("atoms"), lax.axis_index("kvec")]).astype(jnp.int32)
    f32 = lambda *shape: jax.ShapeDtypeStruct(shape, F32)
    bf16 = lambda *shape: jax.ShapeDtypeStruct(shape, BF16)

    cotangents = [grad_out] + [swap(grad_out, "kvec", m) for m in range(1, group_count)]
    lattices = [k_lattice] + [swap(k_lattice, "kvec", m) for m in range(1, group_count)]

    *tiles, k_column = pl.pallas_call(
        tile_kernel,
        out_shape=[bf16(vectors, atoms)] * 4 + [f32(vectors, 128)],
        in_specs=[VMEM] * 2,
        out_specs=[VMEM] * 5,
        compiler_params=PARAMS,
        cost_estimate=cost(9000 * vectors * atoms),
        name="waves_of_own_vectors",
    )(positions, k_lattice)

    keep, send, own = pl.pallas_call(
        functools.partial(sums_kernel, groups=group_count),
        out_shape=[f32(2, half, both), f32(2, half, both), f32(both + 8, share)],
        in_specs=[SMEM, SMEM] + [VMEM] * (9 + group_count) + [ANY] * (group_count - 1),
        out_specs=[VMEM] * 3,
        scratch_shapes=[
            pltpu.VMEM((1, atoms), F32), pltpu.VMEM((both, atoms), F32), pltpu.VMEM((2, vectors, both), F32),
        ],
        compiler_params=PARAMS,
        cost_estimate=cost(100 * vectors * atoms * channels),
        name="structure_sums",
    )(
        here, pad_count, *tiles, feats, species.reshape(1, atoms), w_charge, species_embed.T, w_out,
        *cotangents, *lattices[1:],
    )

    gain = pl.pallas_call(
        functools.partial(gain_kernel, atom_total=atoms * atom_count),
        out_shape=f32(half, both),
        in_specs=[SMEM, VMEM, VMEM],
        out_specs=VMEM,
        compiler_params=PARAMS,
        cost_estimate=cost(9000 * half * both),
        name="filter_gain",
    )(here, filter_width.reshape(1, channels), k_column)

    def waves_of(lattice, after):
        return pl.pallas_call(
            wave_kernel,
            out_shape=[f32(vectors, share)] * 2 + [bf16(vectors, share)] * 4 + [f32(vectors, 128)],
            in_specs=[SMEM, VMEM, VMEM, ANY],
            out_specs=[VMEM] * 7,
            scratch_shapes=[pltpu.VMEM((vectors, 128), F32)],
            compiler_params=PARAMS,
            cost_estimate=cost(9000 * vectors * share),
            name="waves_of_own_atoms",
        )(here, positions, lattice, after)

    total = keep + swap(send, "atoms", 1)
    waves = []
    offset, made = 2, 1
    while offset < atom_count:
        arrived = swap(total, "atoms", offset)
        last = offset * 2 >= atom_count
        count = group_count - made if last else 1
        beside = [waves_of(lattices[m], total) for m in range(made, min(made + count, group_count))]
        made += len(beside)
        arrived, beside = lax.optimization_barrier((arrived, beside))
        for tiles_made in beside:
            waves += tiles_made
        total = total + arrived
        offset *= 2
    near = gain[None] * total
    plane = [swap(near, "kvec", m) for m in range(1, group_count)]
    field, sums = pl.pallas_call(
        own_field_kernel,
        out_shape=[f32(both, share), f32(24, share)],
        in_specs=[SMEM] + [VMEM] * 8,
        out_specs=[VMEM] * 2,
        scratch_shapes=[pltpu.VMEM((vectors, 128), F32), pltpu.VMEM((2, vectors, share), F32)]
        + [pltpu.VMEM((vectors, share), BF16)] * 4,
        compiler_params=PARAMS,
        cost_estimate=cost(120 * vectors * share * channels),
        name="fields_of_own_vectors",
    )(here, *tiles, k_column, own, near, swap(near, "atoms", 1))
    plane, field = lax.optimization_barrier((plane, field))
    coefs = []
    for part in plane:
        coefs += [part, swap(part, "atoms", 1)]

    return tuple(
        pl.pallas_call(
            functools.partial(field_kernel, groups=group_count - 1),
            out_shape=[f32(channels, share), f32(3, share), f32(channels, share)],
            in_specs=[VMEM] * (5 + 9 * (group_count - 1)),
            out_specs=[VMEM] * 3,
            scratch_shapes=[pltpu.VMEM((2, (group_count - 1) * vectors, share), F32)],
            compiler_params=PARAMS,
            cost_estimate=cost(300 * vectors * share * channels),
            name="fields_and_forces",
        )(own, w_out, w_charge, field, sums, *waves, *coefs)
    )


def solution(mesh):
    shared = P(None, ("atoms", "kvec"))
    placed = (
        P(None, "atoms"), P(None, "atoms"), P("atoms"), P("atoms"), P(None, "kvec"),
        P(), P(), P(), P(), shared,
    )
    return jax.shard_map(
        on_device, mesh=mesh, in_specs=placed, out_specs=(shared, shared, shared), check_vma=False
    )
```

```python
import functools
import math

import jax
import jax.numpy as jnp
from jax import lax
from jax.experimental import pallas as pl
from jax.experimental.pallas import tpu as pltpu
from jax.sharding import PartitionSpec as P

F32, BF16 = jnp.float32, jnp.bfloat16
HALF_SIN = (4.442867755889893, -7.307443618774414, 3.594788074493408, -0.7843740582466125)
HALF_COS = (1.4142135381698608, -6.978850841522217, 5.7394609451293945, -1.8835630416870117, 0.31069818139076233)
VMEM = pl.BlockSpec(memory_space=pltpu.VMEM)
SMEM = pl.BlockSpec(memory_space=pltpu.SMEM)
ANY = pl.BlockSpec(memory_space=pl.ANY)
PARAMS = pltpu.CompilerParams(vmem_limit_bytes=32 * 2**20)
NN, NT, TN = ((1,), (0,)), ((1,), (1,)), ((0,), (0,))


def halves(value):
    high = value.astype(BF16)
    return high, (value - high.astype(F32)).astype(BF16)


def dot16(left, right, dims):
    return lax.dot_general(left, right, (dims, ((), ())), preferred_element_type=F32)


def dot3(left, right, dims):
    left_high, left_low = halves(left)
    right_high, right_low = halves(right)
    return (
        dot16(left_high, right_high, dims)
        + dot16(left_low, right_high, dims)
        + dot16(left_high, right_low, dims)
    )


def horner(terms, square):
    total = terms[-1] * square + terms[-2]
    for term in terms[-3::-1]:
        total = total * square + term
    return total


def trig(columns, rows):
    turns = columns[0] * rows[0] + columns[1] * rows[1] + columns[2] * rows[2]
    turns = turns - jnp.round(turns)
    square = turns * turns
    half_sin = horner(HALF_SIN, square) * turns
    return 1.0 - half_sin * half_sin, half_sin * horner(HALF_COS, square)


def trig_blocks(k_ref, pos_ref, first, high_low, full=None):
    vectors, atoms = high_low[0].shape
    step = 32
    width = min(256, atoms)
    per_body = max(1, 2048 // atoms)
    per_body = min(per_body, vectors // step)

    def body(block, _):
        for inner in range(per_body):
            here = pl.ds(pl.multiple_of((block * per_body + inner) * step, step), step)
            columns = [k_ref[here, x : x + 1] for x in range(3)]
            for chunk in range(atoms // width):
                lanes = pl.ds(chunk * width, width)
                start = chunk * width if first is None else pl.multiple_of(first + chunk * width, 128)
                rows = [pos_ref[x : x + 1, pl.ds(start, width)] for x in range(3)]
                cos, sin = trig(columns, rows)
                high_low[0][here, lanes], high_low[1][here, lanes] = halves(cos)
                high_low[2][here, lanes], high_low[3][here, lanes] = halves(sin)
                if full is not None:
                    full[0][here, lanes], full[1][here, lanes] = cos, sin
        return 0

    lax.fori_loop(0, vectors // (step * per_body), body, 0)


def lattice_rows(packed, channels, vectors):
    share = packed.shape[1]
    width = min(share, vectors)
    chunks = [packed[channels + 3 * n : channels + 3 * n + 3, 0:width] for n in range(-(-vectors // share))]
    return jnp.concatenate(chunks, axis=1)


def tile_kernel(pos_ref, k_ref, cos_high, cos_low, sin_high, sin_low, k_column):
    k_column[:, 0:3] = k_ref[...].T
    trig_blocks(k_column, pos_ref, None, (cos_high, cos_low, sin_high, sin_low))


def sums_kernel(
    here_ref, pad_ref, cos_high, cos_low, sin_high, sin_low, feats_ref, species_ref, w_charge_ref, embed_ref, w_out_ref,
    *rest, groups,
):
    cotangents = rest[:groups]
    keep_ref, send_ref, own_ref, mask_ref, both, total = rest[-6:]
    channels, atoms = feats_ref.shape
    share = cotangents[0].shape[1]
    place, group = here_ref[0], here_ref[1]
    embed_high, embed_low = halves(embed_ref[...])
    for block in range(atoms // 256):
        lanes = slice(block * 256, (block + 1) * 256)
        mask = (lax.broadcasted_iota(jnp.int32, (1, 256), 1) < pad_ref[block]).astype(F32)
        mask_ref[:, lanes] = mask
        species_at = lax.broadcasted_iota(jnp.int32, (embed_ref.shape[0], 256), 0)
        one_hot = (species_at == species_ref[:, lanes]).astype(BF16)
        both[0:channels, lanes] = mask * (
            dot3(w_charge_ref[...], feats_ref[:, lanes], TN)
            + dot16(embed_high, one_hot, TN)
            + dot16(embed_low, one_hot, TN)
        )
    for offset, cotangent in enumerate(cotangents):
        lanes = pl.ds(pl.multiple_of((group ^ offset) * share, share), share)
        adjoint = mask_ref[:, lanes] * dot3(w_out_ref[...], cotangent[0:channels, :], NN)
        both[channels:, lanes] = adjoint
        if offset == 0:
            own_ref[0:channels, :] = adjoint
            own_ref[channels : 2 * channels, :] = both[0:channels, lanes]
            own_ref[2 * channels :, :] = jnp.broadcast_to(mask_ref[:, lanes], (8, share))
    high, low = halves(both[...])
    pair = jnp.concatenate([high, low], axis=0)
    for part, (tile_high, tile_low) in enumerate(((cos_high, cos_low), (sin_high, sin_low))):
        wide = dot16(tile_high[...], pair, NT)
        total[part] = (
            wide[:, : 2 * channels] + wide[:, 2 * channels :] + dot16(tile_low[...], high, NT)
        )
    rows = keep_ref.shape[2]
    for offset in range(keep_ref.shape[0]):
        for flip, out in enumerate((keep_ref, send_ref)):
            start = pl.multiple_of((place ^ (2 * offset + flip)) * rows, rows)
            for part in range(2):
                out[offset, part] = total[part, pl.ds(start, rows), :]


def wave_kernel(here_ref, pos_ref, packed_ref, width_ref, after_ref, *rest, atom_total, rows):
    *gain_ref, cos, sin, cos_high, cos_low, sin_high, sin_low, k_ref, k_column = rest
    vectors = cos.shape[0]
    k_column[:, 0:3] = lattice_rows(packed_ref, width_ref.shape[1], vectors).T
    count = vectors // rows
    for piece in range(count):
        start = pl.multiple_of((here_ref[0] ^ piece) * rows, rows)
        to = ((piece % 2) * (count // 2) + piece // 2) * rows
        k_ref[to : to + rows, :] = k_column[pl.ds(start, rows), :]
    if gain_ref:
        waves = [2.0 * math.pi * k_ref[0:rows, x : x + 1] for x in range(3)]
        square = waves[0] * waves[0] + waves[1] * waves[1] + waves[2] * waves[2]
        gain = jnp.exp(-square * width_ref[...]) * 40.0 / (square + 40.0) / math.sqrt(atom_total)
        gain_ref[0][...] = jnp.concatenate([gain, gain], axis=1)
    first = here_ref[1] * cos.shape[1]
    trig_blocks(k_ref, pos_ref, first, (cos_high, cos_low, sin_high, sin_low), (cos, sin))


def coefficient_stack(near_ref, far_ref, part):
    flat = (near_ref.shape[0] * near_ref.shape[2], near_ref.shape[3])
    high, low = halves(jnp.concatenate([near_ref[:, part].reshape(flat), far_ref[:, part].reshape(flat)], axis=0))
    return jnp.concatenate([high, low, high], axis=1)


def own_stack(own_ref, channels):
    high, low = halves(own_ref[0 : 2 * channels, :])
    return jnp.concatenate([high, high, low], axis=0)


def add_field(stack, tile_high, tile_low):
    width = stack.shape[1] // 3
    wide = dot16(stack[:, : 2 * width], tile_high, TN)
    return wide[:width] + wide[width:] + dot16(stack[:, :width], tile_low, TN)


def add_force(sums, wave, along, first):
    step = 16
    cos, sin, _, _, _, _, k_ref = wave
    for start in range(0, cos.shape[0], step):
        here = slice(start, start + step)
        there = slice(first + start, first + start + step)
        slope = cos[here, :] * along[1, there, :] - sin[here, :] * along[0, there, :]
        for x in range(3):
            term = k_ref[here, x : x + 1] * slope
            sums[x] = sums[x] + (term[0:8] + term[8:16])
    return sums


def fields(own_ref, waves, coefs, channels, along, field, sums):
    other = own_stack(own_ref, channels)
    parts = [
        [coefficient_stack(near, far, part) for near, far in zip(coefs[::2], coefs[1::2])] for part in range(2)
    ]
    for part in range(2):
        along[part] = dot16(jnp.concatenate(parts[part], axis=0), other, NN)
    waves = [waves[at : at + 7] for at in range(0, len(waves), 7)]
    for group, wave in enumerate(waves):
        _, _, cos_high, cos_low, sin_high, sin_low, _ = wave
        for part, high, low in ((parts[0], cos_high, cos_low), (parts[1], sin_high, sin_low)):
            added = add_field(part[group], high[...], low[...])
            field = added if field is None else field + added
    for group, wave in enumerate(waves):
        sums = add_force(sums, wave, along, group * wave[0].shape[0])
    return field, sums


def own_field_kernel(own_ref, *rest):
    *waves, near_ref, far_ref, field_ref, sums_ref, along = rest
    share = own_ref.shape[1]
    field, sums = fields(
        own_ref, waves, [near_ref, far_ref], near_ref.shape[3] // 2, along, None, [jnp.zeros((8, share), F32)] * 3
    )
    field_ref[...] = field
    for x in range(3):
        sums_ref[8 * x : 8 * x + 8, :] = sums[x]


def field_kernel(own_ref, w_out_ref, w_charge_ref, field_ref, sums_ref, *rest, groups):
    *waves, message_ref, force_ref, grad_ref, along = rest
    waves, coefs = waves[: 7 * groups], waves[7 * groups :]
    channels = w_out_ref.shape[0]
    sums = [sums_ref[8 * x : 8 * x + 8, :] for x in range(3)]
    field, sums = fields(own_ref, waves, coefs, channels, along, field_ref[...], sums)
    field = own_ref[2 * channels : 2 * channels + 1, :] * field
    message_ref[...] = dot3(w_out_ref[...], field[:channels], TN)
    grad_ref[...] = dot3(w_charge_ref[...], field[channels:], NN)
    for x in range(3):
        force_ref[x : x + 1, :] = 2.0 * math.pi * jnp.sum(sums[x], axis=0, keepdims=True)


def swap(value, axis, offset):
    size = lax.axis_size(axis)
    return lax.ppermute(value, axis, [(place, place ^ offset) for place in range(size)])


def cost(work):
    return pl.CostEstimate(flops=work, bytes_accessed=0, transcendentals=0)


def on_device(
    positions, feats, species, pad_count, k_lattice, filter_width, w_charge, species_embed, w_out, grad_out,
):
    atom_count, group_count = lax.axis_size("atoms"), lax.axis_size("kvec")
    channels, atoms = feats.shape
    share = grad_out.shape[1]
    vectors = k_lattice.shape[1]
    rows = vectors // atom_count
    depth = atom_count // 2
    both = 2 * channels
    here = jnp.stack([lax.axis_index("atoms"), lax.axis_index("kvec")]).astype(jnp.int32)
    f32 = lambda *shape: jax.ShapeDtypeStruct(shape, F32)
    bf16 = lambda *shape: jax.ShapeDtypeStruct(shape, BF16)

    chunks = -(-vectors // share)
    below = -(-3 * chunks // 8) * 8
    packed = jnp.pad(grad_out, ((0, below), (0, 0)))
    lattice = k_lattice.astype(F32)
    for n in range(chunks):
        chunk = lattice[:, n * share : (n + 1) * share]
        first = channels + 3 * n
        packed += jnp.pad(chunk, ((first, channels + below - first - 3), (0, share - chunk.shape[1])))
    packed = [packed] + [swap(packed, "kvec", m) for m in range(1, group_count)]

    *tiles, _ = pl.pallas_call(
        tile_kernel,
        out_shape=[bf16(vectors, atoms)] * 4 + [f32(vectors, 128)],
        in_specs=[VMEM] * 2,
        out_specs=[VMEM] * 5,
        compiler_params=PARAMS,
        cost_estimate=cost(9000 * vectors * atoms),
        name="waves_of_own_vectors",
    )(positions, lattice)

    piece = f32(depth, 2, rows, both)
    keep, send, own = pl.pallas_call(
        functools.partial(sums_kernel, groups=group_count),
        out_shape=[piece, piece, f32(both + 8, share)],
        in_specs=[SMEM, SMEM] + [VMEM] * (9 + group_count),
        out_specs=[VMEM] * 3,
        scratch_shapes=[
            pltpu.VMEM((1, atoms), F32), pltpu.VMEM((both, atoms), F32), pltpu.VMEM((2, vectors, both), F32),
        ],
        compiler_params=PARAMS,
        cost_estimate=cost(100 * vectors * atoms * channels),
        name="structure_sums",
    )(here, pad_count, *tiles, feats, species.reshape(1, atoms), w_charge, species_embed.T, w_out, *packed)

    wave_shapes = [f32(vectors, share)] * 2 + [bf16(vectors, share)] * 4 + [f32(vectors, 128)]

    def waves_of(group, after):
        shapes = ([f32(rows, both)] if group == 0 else []) + wave_shapes
        return pl.pallas_call(
            functools.partial(wave_kernel, atom_total=atoms * atom_count, rows=rows),
            out_shape=shapes,
            in_specs=[SMEM, VMEM, VMEM, VMEM, ANY],
            out_specs=[VMEM] * len(shapes),
            scratch_shapes=[pltpu.VMEM((vectors, 128), F32)],
            compiler_params=PARAMS,
            cost_estimate=cost(9000 * vectors * share),
            name="waves_of_own_atoms",
        )(here, positions, packed[group], filter_width.reshape(1, channels), after)

    arrived = swap(send, "atoms", 1)
    gain, *own_waves = waves_of(0, send)
    arrived, gain = lax.optimization_barrier((arrived, gain))
    half = keep + arrived

    arrived = [swap(half[offset], "atoms", 2 * offset) for offset in range(1, depth)]
    waves = waves_of(1, half)
    arrived, waves = lax.optimization_barrier((arrived, waves))
    total = half[0]
    for part in arrived:
        total = total + part
    total = gain[None] * total

    arrived = [swap(total, "atoms", 2 * offset) for offset in range(1, depth)]
    more = waves_of(2, total)
    arrived, more = lax.optimization_barrier((arrived, more))
    waves = waves + more
    near = jnp.stack([total] + arrived)

    plane = [swap(near, "kvec", m) for m in range(1, group_count)]
    field, sums = pl.pallas_call(
        own_field_kernel,
        out_shape=[f32(both, share), f32(24, share)],
        in_specs=[VMEM] * 10,
        out_specs=[VMEM] * 2,
        scratch_shapes=[pltpu.VMEM((2, vectors, share), F32)],
        compiler_params=PARAMS,
        cost_estimate=cost(120 * vectors * share * channels),
        name="fields_of_own_vectors",
    )(own, *own_waves, near, swap(near, "atoms", 1))
    for group in range(3, group_count):
        waves = waves + waves_of(group, near)
    coefs = []
    for part in plane:
        part, field, waves = lax.optimization_barrier((part, field, waves))
        coefs += [part, swap(part, "atoms", 1)]

    return tuple(
        pl.pallas_call(
            functools.partial(field_kernel, groups=group_count - 1),
            out_shape=[f32(channels, share), f32(3, share), f32(channels, share)],
            in_specs=[VMEM] * (5 + 9 * (group_count - 1)),
            out_specs=[VMEM] * 3,
            scratch_shapes=[pltpu.VMEM((2, (group_count - 1) * vectors, share), F32)],
            compiler_params=PARAMS,
            cost_estimate=cost(300 * vectors * share * channels),
            name="fields_and_forces",
        )(own, w_out, w_charge, field, sums, *waves, *coefs)
    )


def solution(mesh):
    shared = P(None, ("atoms", "kvec"))
    placed = (
        P(None, "atoms"), P(None, "atoms"), P("atoms"), P("atoms"), P(None, "kvec"),
        P(), P(), P(), P(), shared,
    )
    return jax.shard_map(
        on_device, mesh=mesh, in_specs=placed, out_specs=(shared, shared, shared), check_vma=False
    )
```

```python
import functools
import math

import jax
import jax.numpy as jnp
from jax import lax
from jax.experimental import pallas as pl
from jax.experimental.pallas import tpu as pltpu
from jax.sharding import PartitionSpec as P

F32, BF16 = jnp.float32, jnp.bfloat16
HALF_SIN = (4.442867755889893, -7.307443618774414, 3.594788074493408, -0.7843740582466125)
HALF_COS = (1.4142135381698608, -6.978850841522217, 5.7394609451293945, -1.8835630416870117, 0.31069818139076233)
VMEM = pl.BlockSpec(memory_space=pltpu.VMEM)
ANY = pl.BlockSpec(memory_space=pl.ANY)
PARAMS = pltpu.CompilerParams(vmem_limit_bytes=32 * 2**20)
NN, NT, TN = ((1,), (0,)), ((1,), (1,)), ((0,), (0,))


def halves(value):
    high = value.astype(BF16)
    return high, (value - high.astype(F32)).astype(BF16)


def dot16(left, right, dims):
    return lax.dot_general(left, right, (dims, ((), ())), preferred_element_type=F32)


def dot3(left, right, dims):
    left_high, left_low = halves(left)
    right_high, right_low = halves(right)
    return (
        dot16(left_high, right_high, dims)
        + dot16(left_low, right_high, dims)
        + dot16(left_high, right_low, dims)
    )


def horner(terms, square):
    total = terms[-1] * square + terms[-2]
    for term in terms[-3::-1]:
        total = total * square + term
    return total


def trig(columns, rows):
    turns = columns[0] * rows[0] + columns[1] * rows[1] + columns[2] * rows[2]
    turns = turns - jnp.round(turns)
    square = turns * turns
    half_sin = horner(HALF_SIN, square) * turns
    return 1.0 - half_sin * half_sin, half_sin * horner(HALF_COS, square)


def trig_blocks(k_ref, pos_ref, first, high_low, full=None):
    vectors, atoms = high_low[0].shape
    step = 32
    width = min(256, atoms)
    per_body = max(1, 2048 // atoms)
    per_body = min(per_body, vectors // step)

    def body(block, _):
        for inner in range(per_body):
            here = pl.ds(pl.multiple_of((block * per_body + inner) * step, step), step)
            columns = [k_ref[here, x : x + 1] for x in range(3)]
            for chunk in range(atoms // width):
                lanes = pl.ds(chunk * width, width)
                start = chunk * width if first is None else pl.multiple_of(first + chunk * width, 128)
                rows = [pos_ref[x : x + 1, pl.ds(start, width)] for x in range(3)]
                cos, sin = trig(columns, rows)
                high_low[0][here, lanes], high_low[1][here, lanes] = halves(cos)
                high_low[2][here, lanes], high_low[3][here, lanes] = halves(sin)
                if full is not None:
                    full[0][here, lanes], full[1][here, lanes] = cos, sin
        return 0

    lax.fori_loop(0, vectors // (step * per_body), body, 0)


def lattice_rows(packed, channels, vectors):
    share = packed.shape[1]
    width = min(share, vectors)
    chunks = [packed[channels + 3 * n : channels + 3 * n + 3, 0:width] for n in range(-(-vectors // share))]
    return jnp.concatenate(chunks, axis=1)


def tile_kernel(pos_ref, packed_ref, cos_high, cos_low, sin_high, sin_low, k_column, *, channels, vectors, first):
    rows = cos_high.shape[0]
    k_column[:, 0:3] = lattice_rows(packed_ref, channels, vectors)[:, first : first + rows].T
    trig_blocks(k_column, pos_ref, None, (cos_high, cos_low, sin_high, sin_low))


def group_offset(label, groups):
    if groups != 4 or label in (0, 3):
        return label
    return jnp.where(lax.axis_index("atoms") % 2 == 0, label, 3 - label)


def sums_kernel(pad_ref, feats_ref, species_ref, w_charge_ref, embed_ref, w_out_ref, *rest, groups):
    tiles, packed = rest[:8], rest[8 : 8 + groups]
    keep_ref, send_ref, own_ref, mask_ref, both, total = rest[8 + groups :]
    channels, atoms = feats_ref.shape
    share = packed[0].shape[1]
    group = lax.axis_index("kvec")
    embed_high, embed_low = halves(embed_ref[...])
    for block in range(atoms // 256):
        lanes = slice(block * 256, (block + 1) * 256)
        used = pad_ref[0:1, block : block + 1]
        mask = (lax.broadcasted_iota(jnp.int32, (1, 256), 1) < used).astype(F32)
        mask_ref[:, lanes] = mask
        species_at = lax.broadcasted_iota(jnp.int32, (embed_ref.shape[0], 256), 0)
        one_hot = (species_at == species_ref[:, lanes]).astype(BF16)
        both[0:channels, lanes] = mask * (
            dot3(w_charge_ref[...], feats_ref[:, lanes], TN)
            + dot16(embed_high, one_hot, TN)
            + dot16(embed_low, one_hot, TN)
        )
    for label, cotangent in enumerate(packed):
        lanes = pl.ds(pl.multiple_of((group ^ group_offset(label, groups)) * share, share), share)
        adjoint = mask_ref[:, lanes] * dot3(w_out_ref[...], cotangent[0:channels, :], NN)
        both[channels:, lanes] = adjoint
        if label == 0:
            own_ref[0:channels, :] = adjoint
            own_ref[channels : 2 * channels, :] = both[0:channels, lanes]
            own_ref[2 * channels :, :] = jnp.broadcast_to(mask_ref[:, lanes], (8, share))
    high, low = halves(both[...])
    pair = jnp.concatenate([high, low], axis=0)
    tiles_high = jnp.concatenate([tiles[n][...] for n in (0, 4, 2, 6)], axis=0)
    tiles_low = jnp.concatenate([tiles[n][...] for n in (1, 5, 3, 7)], axis=0)
    wide = dot16(tiles_high, pair, NT)
    total[...] = wide[:, : 2 * channels] + wide[:, 2 * channels :] + dot16(tiles_low, high, NT)
    rows = keep_ref.shape[1]
    core = lax.axis_index("atoms") % 2
    for flip, out in enumerate((keep_ref, send_ref)):
        for part in range(2):
            start = pl.multiple_of(2 * rows * part + (core ^ flip) * rows, rows)
            out[part] = total[pl.ds(start, rows), :]


def wave_kernel(pos_ref, packed_ref, width_ref, after_ref, *rest, atom_total):
    *gain_ref, cos, sin, cos_high, cos_low, sin_high, sin_low, k_ref, k_column = rest
    vectors = cos.shape[0]
    rows = vectors // 2
    core = lax.axis_index("atoms") % 2
    k_column[:, 0:3] = lattice_rows(packed_ref, width_ref.shape[1], vectors).T
    for flip in range(2):
        start = pl.multiple_of((core ^ flip) * rows, rows)
        k_ref[flip * rows : (flip + 1) * rows, :] = k_column[pl.ds(start, rows), :]
    if gain_ref:
        waves = [2.0 * math.pi * k_ref[0:rows, x : x + 1] for x in range(3)]
        square = waves[0] * waves[0] + waves[1] * waves[1] + waves[2] * waves[2]
        gain = jnp.exp(-square * width_ref[...]) * 40.0 / (square + 40.0) / math.sqrt(atom_total)
        gain_ref[0][...] = jnp.concatenate([gain, gain], axis=1)
    first = lax.axis_index("kvec") * cos.shape[1]
    trig_blocks(k_ref, pos_ref, first, (cos_high, cos_low, sin_high, sin_low), (cos, sin))


def coefficient_stack(near_ref, far_ref, part):
    high, low = halves(jnp.concatenate([near_ref[part], far_ref[part]], axis=0))
    return jnp.concatenate([high, low, high], axis=1)


def own_stack(own_ref, channels):
    high, low = halves(own_ref[0 : 2 * channels, :])
    return jnp.concatenate([high, high, low], axis=0)


def add_field(stack, tile_high, tile_low):
    width = stack.shape[1] // 3
    wide = dot16(stack[:, : 2 * width], tile_high, TN)
    return wide[:width] + wide[width:] + dot16(stack[:, :width], tile_low, TN)


def add_force(sums, wave, along, first):
    step = 16
    cos, sin, _, _, _, _, k_ref = wave
    for start in range(0, cos.shape[0], step):
        here = slice(start, start + step)
        there = slice(first + start, first + start + step)
        slope = cos[here, :] * along[1, there, :] - sin[here, :] * along[0, there, :]
        for x in range(3):
            term = k_ref[here, x : x + 1] * slope
            sums[x] = sums[x] + (term[0:8] + term[8:16])
    return sums


def fields(own_ref, waves, coefs, channels, along, field, sums):
    other = own_stack(own_ref, channels)
    parts = [
        [coefficient_stack(near, far, part) for near, far in zip(coefs[::2], coefs[1::2])] for part in range(2)
    ]
    for part in range(2):
        along[part] = dot16(jnp.concatenate(parts[part], axis=0), other, NN)
    waves = [waves[at : at + 7] for at in range(0, len(waves), 7)]
    for group, wave in enumerate(waves):
        _, _, cos_high, cos_low, sin_high, sin_low, _ = wave
        for part, high, low in ((parts[0], cos_high, cos_low), (parts[1], sin_high, sin_low)):
            added = add_field(part[group], high[...], low[...])
            field = added if field is None else field + added
    for group, wave in enumerate(waves):
        sums = add_force(sums, wave, along, group * wave[0].shape[0])
    return field, sums


def partial_field_kernel(own_ref, *rest, groups, first):
    waves, coefs, before = rest[: 7 * groups], rest[7 * groups : 9 * groups], rest[9 * groups : -3]
    field_ref, sums_ref, along = rest[-3:]
    share = own_ref.shape[1]
    if first:
        field, sums = None, [jnp.zeros((8, share), F32)] * 3
    else:
        field, sums = before[0][...], [before[1][8 * x : 8 * x + 8, :] for x in range(3)]
    field, sums = fields(own_ref, waves, coefs, coefs[0].shape[2] // 2, along, field, sums)
    field_ref[...] = field
    for x in range(3):
        sums_ref[8 * x : 8 * x + 8, :] = sums[x]


def field_kernel(own_ref, w_out_ref, w_charge_ref, *rest):
    *waves, near_ref, far_ref, field_ref, sums_ref, message_ref, force_ref, grad_ref, along = rest
    channels = w_out_ref.shape[0]
    sums = [sums_ref[8 * x : 8 * x + 8, :] for x in range(3)]
    field, sums = fields(own_ref, waves, [near_ref, far_ref], channels, along, field_ref[...], sums)
    field = own_ref[2 * channels : 2 * channels + 1, :] * field
    message_ref[...] = dot3(w_out_ref[...], field[:channels], TN)
    grad_ref[...] = dot3(w_charge_ref[...], field[channels:], NN)
    for x in range(3):
        force_ref[x : x + 1, :] = 2.0 * math.pi * jnp.sum(sums[x], axis=0, keepdims=True)


def swap(value, axis, offset):
    size = lax.axis_size(axis)
    return lax.ppermute(value, axis, [(place, place ^ offset) for place in range(size)])


def swap_by_core(value, even, odd):
    groups = lax.axis_size("kvec")
    pairs = []
    for place in range(lax.axis_size("atoms")):
        for group in range(groups):
            other = group ^ (odd if place % 2 else even)
            pairs.append((place * groups + group, place * groups + other))
    return lax.ppermute(value, ("atoms", "kvec"), pairs)


def cost(work):
    return pl.CostEstimate(flops=work, bytes_accessed=0, transcendentals=0)


def on_device(
    positions, feats, species, pad_count, k_lattice, filter_width, w_charge, species_embed, w_out, grad_out,
):
    atom_count, group_count = lax.axis_size("atoms"), lax.axis_size("kvec")
    channels, atoms = feats.shape
    share = grad_out.shape[1]
    vectors = k_lattice.shape[1]
    half = vectors // 2
    both = 2 * channels
    four = group_count == 4
    f32 = lambda *shape: jax.ShapeDtypeStruct(shape, F32)
    bf16 = lambda *shape: jax.ShapeDtypeStruct(shape, BF16)

    def first_planes(value):
        if four:
            return [swap_by_core(value, 1, 2), swap_by_core(value, 2, 1)]
        return [swap(value, "kvec", m) for m in range(1, group_count)]

    chunks = -(-vectors // share)
    below = -(-3 * chunks // 8) * 8
    packed = jnp.pad(grad_out, ((0, below), (0, 0)))
    for n in range(chunks):
        chunk = k_lattice[:, n * share : (n + 1) * share]
        first = channels + 3 * n
        packed += jnp.pad(chunk, ((first, channels + below - first - 3), (0, share - chunk.shape[1]))).astype(F32)

    def tiles_of(part):
        made = pl.pallas_call(
            functools.partial(tile_kernel, channels=channels, vectors=vectors, first=part * half),
            out_shape=[bf16(half, atoms)] * 4,
            in_specs=[VMEM] * 2,
            out_specs=[VMEM] * 4,
            scratch_shapes=[pltpu.VMEM((half, 128), F32)],
            compiler_params=PARAMS,
            cost_estimate=cost(9000 * half * atoms),
            name="waves_of_own_vectors",
        )(positions, packed)
        return list(made)

    arrived = first_planes(packed)
    tiles = tiles_of(0)
    arrived[0], tiles = lax.optimization_barrier((arrived[0], tiles))
    if four:
        arrived.append(swap_by_core(arrived[0], 2, 1))
    tiles = tiles + tiles_of(1)
    packed = [packed] + arrived

    keep, send, own = pl.pallas_call(
        functools.partial(sums_kernel, groups=group_count),
        out_shape=[f32(2, half, both), f32(2, half, both), f32(both + 8, share)],
        in_specs=[VMEM] * (14 + group_count),
        out_specs=[VMEM] * 3,
        scratch_shapes=[
            pltpu.VMEM((1, atoms), F32), pltpu.VMEM((both, atoms), F32), pltpu.VMEM((2 * vectors, both), F32),
        ],
        compiler_params=PARAMS,
        cost_estimate=cost(100 * vectors * atoms * channels),
        name="structure_sums",
    )(
        pad_count.reshape(1, -1), feats, species.reshape(1, atoms), w_charge, species_embed.T, w_out,
        *tiles, *packed,
    )

    wave_shapes = [f32(vectors, share)] * 2 + [bf16(vectors, share)] * 4 + [f32(vectors, 128)]

    def waves_of(group, after):
        shapes = ([f32(half, both)] if group == 0 else []) + wave_shapes
        made = pl.pallas_call(
            functools.partial(wave_kernel, atom_total=atoms * atom_count),
            out_shape=shapes,
            in_specs=[VMEM, VMEM, VMEM, ANY],
            out_specs=[VMEM] * len(shapes),
            scratch_shapes=[pltpu.VMEM((vectors, 128), F32)],
            compiler_params=PARAMS,
            cost_estimate=cost(9000 * vectors * share),
            name="waves_of_own_atoms",
        )(positions, packed[group], filter_width.reshape(1, channels), after)
        return list(made)

    arrived = swap(send, "atoms", 1)
    gain, *own_waves = waves_of(0, send)
    arrived, gain = lax.optimization_barrier((arrived, gain))
    total = keep + arrived
    waves, made = [], 1
    steps = [2 << n for n in range((atom_count // 2).bit_length() - 1)]
    for near_step, far_step in zip(steps, steps[::-1]):
        pairs = [(place, place ^ (far_step if place % 2 else near_step)) for place in range(atom_count)]
        arrived = lax.ppermute(total, "atoms", pairs)
        count = group_count - made if near_step == steps[-1] else 1
        beside = []
        for group in range(made, min(made + count, group_count)):
            beside = beside + waves_of(group, total)
            made += 1
        arrived, beside = lax.optimization_barrier((arrived, beside))
        waves += beside
        total = total + arrived
    near = gain[None] * total

    def partial_fields(group_waves, coefs, before):
        groups = len(coefs) // 2
        return pl.pallas_call(
            functools.partial(partial_field_kernel, groups=groups, first=not before),
            out_shape=[f32(both, share), f32(24, share)],
            in_specs=[VMEM] * (1 + 9 * groups + len(before)),
            out_specs=[VMEM] * 2,
            scratch_shapes=[pltpu.VMEM((2, groups * vectors, share), F32)],
            compiler_params=PARAMS,
            cost_estimate=cost(120 * groups * vectors * share * channels),
            name="fields_of_some_groups",
        )(own, *group_waves, *coefs, *before)

    plane = first_planes(near)
    fields_so_far = partial_fields(own_waves, [near, swap(near, "atoms", 1)], [])
    plane[0], fields_so_far = lax.optimization_barrier((plane[0], fields_so_far))
    if four:
        last = swap_by_core(plane[0], 2, 1)
        plane = lax.optimization_barrier(plane)
        far = [swap(plane[1], "atoms", 1), swap(plane[0], "atoms", 1)]
    else:
        last = plane.pop()
        far = [swap(part, "atoms", 1) for part in plane]
    coefs = [part for pair in zip(plane, far) for part in pair]
    fields_so_far = partial_fields(waves[:-7], coefs, fields_so_far)
    last, fields_so_far = lax.optimization_barrier((last, fields_so_far))

    return tuple(
        pl.pallas_call(
            field_kernel,
            out_shape=[f32(channels, share), f32(3, share), f32(channels, share)],
            in_specs=[VMEM] * 14,
            out_specs=[VMEM] * 3,
            scratch_shapes=[pltpu.VMEM((2, vectors, share), F32)],
            compiler_params=PARAMS,
            cost_estimate=cost(120 * vectors * share * channels),
            name="fields_and_forces",
        )(own, w_out, w_charge, *waves[-7:], last, swap(last, "atoms", 1), *fields_so_far)
    )


def solution(mesh):
    shared = P(None, ("atoms", "kvec"))
    placed = (
        P(None, "atoms"), P(None, "atoms"), P("atoms"), P("atoms"), P(None, "kvec"),
        P(), P(), P(), P(), shared,
    )
    return jax.shard_map(
        on_device, mesh=mesh, in_specs=placed, out_specs=(shared, shared, shared), check_vma=False
    )
```

```python
import functools
import math

import jax
import jax.numpy as jnp
from jax import lax
from jax.experimental import pallas as pl
from jax.experimental.pallas import tpu as pltpu
from jax.sharding import PartitionSpec as P

F32, BF16 = jnp.float32, jnp.bfloat16
HALF_SIN = (4.442867755889893, -7.307443618774414, 3.594788074493408, -0.7843740582466125)
HALF_COS = (1.4142135381698608, -6.978850841522217, 5.7394609451293945, -1.8835630416870117, 0.31069818139076233)
VMEM = pl.BlockSpec(memory_space=pltpu.VMEM)
ANY = pl.BlockSpec(memory_space=pl.ANY)
PARAMS = pltpu.CompilerParams(vmem_limit_bytes=32 * 2**20)
NN, NT, TN = ((1,), (0,)), ((1,), (1,)), ((0,), (0,))


def halves(value):
    high = value.astype(BF16)
    return high, (value - high.astype(F32)).astype(BF16)


def dot16(left, right, dims):
    return lax.dot_general(left, right, (dims, ((), ())), preferred_element_type=F32)


def dot3(left, right, dims):
    left_high, left_low = halves(left)
    right_high, right_low = halves(right)
    return (
        dot16(left_high, right_high, dims)
        + dot16(left_low, right_high, dims)
        + dot16(left_high, right_low, dims)
    )


def horner(terms, square):
    total = terms[-1] * square + terms[-2]
    for term in terms[-3::-1]:
        total = total * square + term
    return total


def trig(columns, rows):
    turns = columns[0] * rows[0] + columns[1] * rows[1] + columns[2] * rows[2]
    turns = turns - jnp.round(turns)
    square = turns * turns
    half_sin = horner(HALF_SIN, square) * turns
    return 1.0 - half_sin * half_sin, half_sin * horner(HALF_COS, square)


def trig_blocks(k_ref, pos_ref, first, high_low, full=None):
    vectors, atoms = high_low[0].shape
    step = 32
    width = min(256, atoms)
    per_body = max(1, 2048 // atoms)
    per_body = min(per_body, vectors // step)

    def body(block, _):
        for inner in range(per_body):
            here = pl.ds(pl.multiple_of((block * per_body + inner) * step, step), step)
            columns = [k_ref[here, x : x + 1] for x in range(3)]
            for chunk in range(atoms // width):
                lanes = pl.ds(chunk * width, width)
                start = chunk * width if first is None else pl.multiple_of(first + chunk * width, 128)
                rows = [pos_ref[x : x + 1, pl.ds(start, width)] for x in range(3)]
                cos, sin = trig(columns, rows)
                high_low[0][here, lanes], high_low[1][here, lanes] = halves(cos)
                high_low[2][here, lanes], high_low[3][here, lanes] = halves(sin)
                if full is not None:
                    full[0][here, lanes], full[1][here, lanes] = cos, sin
        return 0

    lax.fori_loop(0, vectors // (step * per_body), body, 0)


def tile_kernel(pos_ref, lattice_ref, high_ref, low_ref, k_column, *, first):
    rows = k_column.shape[0]
    k_column[:, 0:3] = lattice_ref[:, first : first + rows].astype(F32).T
    cos, sin = pl.ds(0, rows), pl.ds(rows, rows)
    trig_blocks(k_column, pos_ref, None, (high_ref.at[cos], low_ref.at[cos], high_ref.at[sin], low_ref.at[sin]))


def sum_over_atoms(tiles, lanes, value):
    count = value.shape[0]
    high, low = halves(value)
    tiles_high = jnp.concatenate([tile[:, lanes] for tile in tiles[::2]], axis=0)
    tiles_low = jnp.concatenate([tile[:, lanes] for tile in tiles[1::2]], axis=0)
    wide = dot16(tiles_high, jnp.concatenate([high, low], axis=0), NT)
    return wide[:, :count] + wide[:, count:] + dot16(tiles_low, high, NT)


def arranged(sums):
    rows = sums.shape[0] // 4
    parts = [sums[n * rows : (n + 1) * rows] for n in range(4)]
    return jnp.concatenate([jnp.concatenate(parts[:2], axis=1), jnp.concatenate(parts[2:], axis=1)], axis=0)


def split_by_core(total, keep_ref, send_ref):
    rows = keep_ref.shape[0]
    core = lax.axis_index("atoms") % 2
    for flip, out in enumerate((keep_ref, send_ref)):
        out[...] = total[pl.ds(pl.multiple_of((core ^ flip) * rows, rows), rows), :]


def halves_of_atoms(groups, atoms):
    side = lax.axis_index("kvec") // (groups // 2)
    span = atoms // 2
    return [pl.ds(pl.multiple_of(at * span, span), span) for at in (side, 1 - side)]


def adjoint_of(cotangent_ref, offset, mask_ref, w_out_ref):
    share = cotangent_ref.shape[1]
    lanes = pl.ds(pl.multiple_of((lax.axis_index("kvec") ^ offset) * share, share), share)
    return lanes, mask_ref[:, lanes] * dot3(w_out_ref[...], cotangent_ref[...], NN)


def charge_kernel(pad_ref, feats_ref, species_ref, w_charge_ref, embed_ref, w_out_ref, *rest, groups):
    tiles, cotangents = rest[:4], rest[4 : 4 + groups // 2]
    keep_ref, send_ref, own_ref, mask_ref, part_ref, both, total = rest[4 + groups // 2 :]
    channels, atoms = feats_ref.shape
    embed_high, embed_low = halves(embed_ref[...])
    for block in range(atoms // 256):
        lanes = slice(block * 256, (block + 1) * 256)
        used = pad_ref[0:1, block : block + 1]
        mask = (lax.broadcasted_iota(jnp.int32, (1, 256), 1) < used).astype(F32)
        mask_ref[:, lanes] = mask
        species_at = lax.broadcasted_iota(jnp.int32, (embed_ref.shape[0], 256), 0)
        one_hot = (species_at == species_ref[:, lanes]).astype(BF16)
        both[0:channels, lanes] = mask * (
            dot3(w_charge_ref[...], feats_ref[:, lanes], TN)
            + dot16(embed_high, one_hot, TN)
            + dot16(embed_low, one_hot, TN)
        )
    for offset, cotangent in enumerate(cotangents):
        lanes, adjoint = adjoint_of(cotangent, offset, mask_ref, w_out_ref)
        both[channels:, lanes] = adjoint
        if offset == 0:
            own_ref[0:channels, :] = adjoint
            own_ref[channels : 2 * channels, :] = both[0:channels, lanes]
            own_ref[2 * channels :, :] = jnp.broadcast_to(mask_ref[:, lanes], (8, adjoint.shape[1]))
    near, far = halves_of_atoms(groups, atoms)
    sums = sum_over_atoms(tiles, near, both[:, near])
    total[...] = arranged(sums[:, :channels] + sum_over_atoms(tiles, far, both[0:channels, far]))
    split_by_core(total, keep_ref, send_ref)
    part_ref[...] = arranged(sums[:, channels:])


def adjoint_kernel(mask_ref, w_out_ref, part_ref, *rest, groups):
    tiles, cotangents = rest[:4], rest[4 : 4 + groups // 2]
    keep_ref, send_ref, adjoint_ref, total = rest[4 + groups // 2 :]
    for offset, cotangent in enumerate(cotangents):
        lanes, adjoint = adjoint_of(cotangent, groups // 2 + offset, mask_ref, w_out_ref)
        adjoint_ref[:, lanes] = adjoint
    _, far = halves_of_atoms(groups, adjoint_ref.shape[1])
    total[...] = part_ref[...] + arranged(sum_over_atoms(tiles, far, adjoint_ref[:, far]))
    split_by_core(total, keep_ref, send_ref)


def wave_kernel(pos_ref, lattice_ref, width_ref, after_ref, *rest, atom_total):
    *gain_ref, cos, sin, cos_high, cos_low, sin_high, sin_low, k_ref, k_column = rest
    vectors = cos.shape[0]
    rows = vectors // 2
    core = lax.axis_index("atoms") % 2
    k_column[:, 0:3] = lattice_ref[...].astype(F32).T
    for flip in range(2):
        start = pl.multiple_of((core ^ flip) * rows, rows)
        k_ref[flip * rows : (flip + 1) * rows, :] = k_column[pl.ds(start, rows), :]
    if gain_ref:
        waves = [2.0 * math.pi * k_ref[0:rows, x : x + 1] for x in range(3)]
        square = waves[0] * waves[0] + waves[1] * waves[1] + waves[2] * waves[2]
        gain = jnp.exp(-square * width_ref[...]) * 40.0 / (square + 40.0) / math.sqrt(atom_total)
        gain_ref[0][...] = jnp.concatenate([gain, gain], axis=1)
    first = lax.axis_index("kvec") * cos.shape[1]
    trig_blocks(k_ref, pos_ref, first, (cos_high, cos_low, sin_high, sin_low), (cos, sin))


def coefficient_stack(near_ref, far_ref, part):
    channels = near_ref.shape[2] // 2
    lanes = slice(part * channels, (part + 1) * channels)
    sides = [jnp.concatenate([side[0, :, lanes], side[1, :, lanes]], axis=1) for side in (near_ref, far_ref)]
    high, low = halves(jnp.concatenate(sides, axis=0))
    return jnp.concatenate([high, low, high], axis=1)


def own_stack(own_ref, channels):
    high, low = halves(own_ref[0 : 2 * channels, :])
    return jnp.concatenate([high, high, low], axis=0)


def add_field(stack, tile_high, tile_low):
    width = stack.shape[1] // 3
    wide = dot16(stack[:, : 2 * width], tile_high, TN)
    return wide[:width] + wide[width:] + dot16(stack[:, :width], tile_low, TN)


def add_force(sums, wave, along, first):
    step = 16
    cos, sin, _, _, _, _, k_ref = wave
    for start in range(0, cos.shape[0], step):
        here = slice(start, start + step)
        there = slice(first + start, first + start + step)
        slope = cos[here, :] * along[1, there, :] - sin[here, :] * along[0, there, :]
        for x in range(3):
            term = k_ref[here, x : x + 1] * slope
            sums[x] = sums[x] + (term[0:8] + term[8:16])
    return sums


def fields(own_ref, waves, coefs, channels, along, field, sums):
    other = own_stack(own_ref, channels)
    coefs = [coefs[at : at + 2] for at in range(0, len(coefs), 2)]
    parts = [[coefficient_stack(*pair, part) for pair in coefs] for part in range(2)]
    for part in range(2):
        along[part] = dot16(jnp.concatenate(parts[part], axis=0), other, NN)
    waves = [waves[at : at + 7] for at in range(0, len(waves), 7)]
    for group, wave in enumerate(waves):
        _, _, cos_high, cos_low, sin_high, sin_low, _ = wave
        for part, high, low in ((parts[0], cos_high, cos_low), (parts[1], sin_high, sin_low)):
            added = add_field(part[group], high[...], low[...])
            field = added if field is None else field + added
    for group, wave in enumerate(waves):
        sums = add_force(sums, wave, along, group * wave[0].shape[0])
    return field, sums


def partial_field_kernel(own_ref, *rest, groups, first):
    waves, coefs, before = rest[: 7 * groups], rest[7 * groups : 9 * groups], rest[9 * groups : -3]
    field_ref, sums_ref, along = rest[-3:]
    share = own_ref.shape[1]
    if first:
        field, sums = None, [jnp.zeros((8, share), F32)] * 3
    else:
        field, sums = before[0][...], [before[1][8 * x : 8 * x + 8, :] for x in range(3)]
    field, sums = fields(own_ref, waves, coefs, coefs[0].shape[2] // 2, along, field, sums)
    field_ref[...] = field
    for x in range(3):
        sums_ref[8 * x : 8 * x + 8, :] = sums[x]


def field_kernel(own_ref, w_out_ref, w_charge_ref, *rest, groups):
    waves, coefs = rest[: 7 * groups], rest[7 * groups : 9 * groups]
    field_ref, sums_ref, message_ref, force_ref, grad_ref, along = rest[9 * groups :]
    channels = w_out_ref.shape[0]
    sums = [sums_ref[8 * x : 8 * x + 8, :] for x in range(3)]
    field, sums = fields(own_ref, waves, coefs, channels, along, field_ref[...], sums)
    field = own_ref[2 * channels : 2 * channels + 1, :] * field
    message_ref[...] = dot3(w_out_ref[...], field[:channels], TN)
    grad_ref[...] = dot3(w_charge_ref[...], field[channels:], NN)
    for x in range(3):
        force_ref[x : x + 1, :] = 2.0 * math.pi * jnp.sum(sums[x], axis=0, keepdims=True)


def swap(value, axis, offset):
    size = lax.axis_size(axis)
    return lax.ppermute(value, axis, [(place, place ^ offset) for place in range(size)])


def swap_along_z(value, even, odd):
    pairs = [(place, place ^ (odd if place % 2 else even)) for place in range(lax.axis_size("atoms"))]
    return lax.ppermute(value, "atoms", pairs)


def cost(work):
    return pl.CostEstimate(flops=work, bytes_accessed=0, transcendentals=0)


def on_device(
    positions, feats, species, pad_count, k_lattice, filter_width, w_charge, species_embed, w_out, grad_out,
):
    atom_count, group_count = lax.axis_size("atoms"), lax.axis_size("kvec")
    channels, atoms = feats.shape
    share = grad_out.shape[1]
    vectors = k_lattice.shape[1]
    half = vectors // 2
    both = 2 * channels
    f32 = lambda *shape: jax.ShapeDtypeStruct(shape, F32)
    bf16 = lambda *shape: jax.ShapeDtypeStruct(shape, BF16)

    def planes(value):
        return [swap(value, "kvec", m) for m in range(group_count - 1, 0, -1)][::-1]

    cotangents = [grad_out] + planes(grad_out)

    tiles = []
    for part in range(2):
        tiles += pl.pallas_call(
            functools.partial(tile_kernel, first=part * half),
            out_shape=[bf16(vectors, atoms)] * 2,
            in_specs=[VMEM] * 2,
            out_specs=[VMEM] * 2,
            scratch_shapes=[pltpu.VMEM((half, 128), F32)],
            compiler_params=PARAMS,
            cost_estimate=cost(9000 * half * atoms),
            name="waves_of_own_vectors",
        )(positions, k_lattice)

    middle = group_count // 2
    keep_h, send_h, own, mask, part = pl.pallas_call(
        functools.partial(charge_kernel, groups=group_count),
        out_shape=[f32(half, both)] * 2 + [f32(both + 8, share), f32(1, atoms), f32(vectors, both)],
        in_specs=[VMEM] * (10 + middle),
        out_specs=[VMEM] * 5,
        scratch_shapes=[pltpu.VMEM((both, atoms), F32), pltpu.VMEM((vectors, both), F32)],
        compiler_params=PARAMS,
        cost_estimate=cost(60 * vectors * atoms * channels),
        name="charge_sums",
    )(
        pad_count.reshape(1, -1), feats, species.reshape(1, atoms), w_charge, species_embed.T, w_out,
        *tiles, *cotangents[:middle],
    )

    wave_shapes = [f32(vectors, share)] * 2 + [bf16(vectors, share)] * 4 + [f32(vectors, 128)]

    def waves_of(group, after):
        shapes = ([f32(half, both)] if group == 0 else []) + wave_shapes
        made = pl.pallas_call(
            functools.partial(wave_kernel, atom_total=atoms * atom_count),
            out_shape=shapes,
            in_specs=[VMEM, VMEM, VMEM, ANY],
            out_specs=[VMEM] * len(shapes),
            scratch_shapes=[pltpu.VMEM((vectors, 128), F32)],
            compiler_params=PARAMS,
            cost_estimate=cost(20 * vectors * share),
            name="waves_of_own_atoms",
        )(positions, lattices[group], filter_width.reshape(1, channels), after)
        return list(made)

    arrived_h = swap(send_h, "atoms", 1)
    keep_b, send_b = pl.pallas_call(
        functools.partial(adjoint_kernel, groups=group_count),
        out_shape=[f32(half, both)] * 2,
        in_specs=[VMEM] * (7 + middle),
        out_specs=[VMEM] * 2,
        scratch_shapes=[pltpu.VMEM((channels, atoms), F32), pltpu.VMEM((vectors, both), F32)],
        compiler_params=PARAMS,
        cost_estimate=cost(60 * vectors * atoms * channels),
        name="adjoint_sums",
    )(mask, w_out, part, *tiles, *cotangents[middle:])

    arrived_h, send_b = lax.optimization_barrier((arrived_h, send_b))
    arrived_b = swap(send_b, "atoms", 1)
    sum_h = keep_h + arrived_h
    steps = [2 << n for n in range((atom_count // 2).bit_length() - 1)]
    next_h = swap_along_z(sum_h, steps[0], steps[-1])
    arrived_b, sum_h = lax.optimization_barrier((arrived_b, sum_h))
    sum_b = keep_b + arrived_b
    next_b = swap_along_z(sum_b, steps[0], steps[-1])

    next_h, next_b = lax.optimization_barrier((next_h, next_b))
    total = jnp.stack([sum_h + next_h, sum_b + next_b])
    lattices, waves = [k_lattice], []
    for step in zip(steps[1:], steps[-2::-1]):
        arrived = swap_along_z(total, *step)
        if not waves:
            gain, *made = waves_of(0, total)
            held, made = lax.optimization_barrier((k_lattice, made))
            lattices += planes(held)
            waves = [made, waves_of(1, total)]
            arrived, gain, waves, lattices = lax.optimization_barrier((arrived, gain, waves, lattices))
        total = total + arrived
    near = gain[None] * total
    plane = {0: near}
    for group in range(group_count - 1, 0, -1):
        plane[group] = swap(near, "kvec", group)
    waves += [waves_of(group, near) for group in range(2, group_count)]
    far = {0: swap(near, "atoms", 1)}

    def partial_fields(groups, before):
        count = len(groups)
        coefs = [part[g] for g in groups for part in (plane, far)]
        group_waves = [wave for g in groups for wave in waves[g]]
        return pl.pallas_call(
            functools.partial(partial_field_kernel, groups=count, first=not before),
            out_shape=[f32(both, share), f32(24, share)],
            in_specs=[VMEM] * (1 + 9 * count + len(before)),
            out_specs=[VMEM] * 2,
            scratch_shapes=[pltpu.VMEM((2, count * vectors, share), F32)],
            compiler_params=PARAMS,
            cost_estimate=cost(count * vectors * share),
            name="fields_of_some_groups",
        )(own, *group_waves, *coefs, *before)

    fields_so_far = partial_fields([0], [])
    waves, fields_so_far = lax.optimization_barrier((waves, fields_so_far))
    for group in range(group_count - 1, 0, -1):
        plane[group], fields_so_far = lax.optimization_barrier((plane[group], fields_so_far))
        far[group] = swap(plane[group], "atoms", 1)
    late = [2, 1] if group_count > 3 else [1]
    fields_so_far = partial_fields(list(range(group_count - 1, len(late), -1)), fields_so_far)
    late_operands = [wave for g in late for wave in waves[g]] + [part[g] for g in late for part in (plane, far)]

    return tuple(
        pl.pallas_call(
            functools.partial(field_kernel, groups=len(late)),
            out_shape=[f32(channels, share), f32(3, share), f32(channels, share)],
            in_specs=[VMEM] * (5 + 9 * len(late)),
            out_specs=[VMEM] * 3,
            scratch_shapes=[pltpu.VMEM((2, len(late) * vectors, share), F32)],
            compiler_params=PARAMS,
            cost_estimate=cost(vectors * share),
            name="fields_and_forces",
        )(
            own, w_out, w_charge, *late_operands, *fields_so_far
        )
    )


def solution(mesh):
    shared = P(None, ("atoms", "kvec"))
    placed = (
        P(None, "atoms"), P(None, "atoms"), P("atoms"), P("atoms"), P(None, "kvec"),
        P(), P(), P(), P(), shared,
    )
    return jax.shard_map(
        on_device, mesh=mesh, in_specs=placed, out_specs=(shared, shared, shared), check_vma=False
    )
```

```python
import functools
import math

import jax
import jax.numpy as jnp
from jax import lax
from jax.experimental import pallas as pl
from jax.experimental.pallas import tpu as pltpu
from jax.sharding import PartitionSpec as P

F32, BF16 = jnp.float32, jnp.bfloat16
HALF_SIN = (4.442867755889893, -7.307443618774414, 3.594788074493408, -0.7843740582466125)
HALF_COS = (1.4142135381698608, -6.978850841522217, 5.7394609451293945, -1.8835630416870117, 0.31069818139076233)
VMEM = pl.BlockSpec(memory_space=pltpu.VMEM)
ANY = pl.BlockSpec(memory_space=pl.ANY)
PARAMS = pltpu.CompilerParams(vmem_limit_bytes=32 * 2**20)
NN, NT, TN = ((1,), (0,)), ((1,), (1,)), ((0,), (0,))


def halves(value):
    high = value.astype(BF16)
    return high, (value - high.astype(F32)).astype(BF16)


def dot16(left, right, dims):
    return lax.dot_general(left, right, (dims, ((), ())), preferred_element_type=F32)


def dot3(left, right, dims):
    left_high, left_low = halves(left)
    right_high, right_low = halves(right)
    return (
        dot16(left_high, right_high, dims)
        + dot16(left_low, right_high, dims)
        + dot16(left_high, right_low, dims)
    )


def horner(terms, square):
    total = terms[-1] * square + terms[-2]
    for term in terms[-3::-1]:
        total = total * square + term
    return total


def trig(columns, rows):
    turns = columns[0] * rows[0] + columns[1] * rows[1] + columns[2] * rows[2]
    turns = turns - jnp.round(turns)
    square = turns * turns
    half_sin = horner(HALF_SIN, square) * turns
    return 1.0 - half_sin * half_sin, half_sin * horner(HALF_COS, square)


def trig_blocks(k_ref, pos_ref, first, high_low, full=None):
    vectors, atoms = high_low[0].shape
    step = 32
    width = min(256, atoms)
    per_body = max(1, 2048 // atoms)
    per_body = min(per_body, vectors // step)

    def body(block, _):
        for inner in range(per_body):
            here = pl.ds(pl.multiple_of((block * per_body + inner) * step, step), step)
            columns = [k_ref[here, x : x + 1] for x in range(3)]
            for chunk in range(atoms // width):
                lanes = pl.ds(chunk * width, width)
                start = chunk * width if first is None else pl.multiple_of(first + chunk * width, 128)
                rows = [pos_ref[x : x + 1, pl.ds(start, width)] for x in range(3)]
                cos, sin = trig(columns, rows)
                high_low[0][here, lanes], high_low[1][here, lanes] = halves(cos)
                high_low[2][here, lanes], high_low[3][here, lanes] = halves(sin)
                if full is not None:
                    full[0][here, lanes], full[1][here, lanes] = cos, sin
        return 0

    lax.fori_loop(0, vectors // (step * per_body), body, 0)


def lattice_rows(packed, channels, vectors):
    share = packed.shape[1]
    width = min(share, vectors)
    chunks = [packed[channels + 3 * n : channels + 3 * n + 3, 0:width] for n in range(-(-vectors // share))]
    return jnp.concatenate(chunks, axis=1)


def tile_kernel(pos_ref, packed_ref, high_ref, low_ref, k_column, *, channels, vectors, first):
    rows = k_column.shape[0]
    k_column[:, 0:3] = lattice_rows(packed_ref, channels, vectors)[:, first : first + rows].T
    cos, sin = pl.ds(0, rows), pl.ds(rows, rows)
    trig_blocks(k_column, pos_ref, None, (high_ref.at[cos], low_ref.at[cos], high_ref.at[sin], low_ref.at[sin]))


def sum_over_atoms(tiles, lanes, value):
    count = value.shape[0]
    high, low = halves(value)
    tiles_high = jnp.concatenate([tile[:, lanes] for tile in tiles[::2]], axis=0)
    tiles_low = jnp.concatenate([tile[:, lanes] for tile in tiles[1::2]], axis=0)
    wide = dot16(tiles_high, jnp.concatenate([high, low], axis=0), NT)
    return wide[:, :count] + wide[:, count:] + dot16(tiles_low, high, NT)


def arranged(sums):
    rows = sums.shape[0] // 4
    parts = [sums[n * rows : (n + 1) * rows] for n in range(4)]
    return jnp.concatenate([jnp.concatenate(parts[:2], axis=1), jnp.concatenate(parts[2:], axis=1)], axis=0)


def split_by_core(total, keep_ref, send_ref):
    rows = keep_ref.shape[0]
    core = lax.axis_index("atoms") % 2
    for flip, out in enumerate((keep_ref, send_ref)):
        out[...] = total[pl.ds(pl.multiple_of((core ^ flip) * rows, rows), rows), :]


def halves_of_atoms(groups, atoms):
    side = lax.axis_index("kvec") // (groups // 2)
    span = atoms // 2
    return [pl.ds(pl.multiple_of(at * span, span), span) for at in (side, 1 - side)]


def adjoint_of(cotangent_ref, offset, mask_ref, w_out_ref):
    share = cotangent_ref.shape[1]
    lanes = pl.ds(pl.multiple_of((lax.axis_index("kvec") ^ offset) * share, share), share)
    return lanes, mask_ref[:, lanes] * dot3(w_out_ref[...], cotangent_ref[0 : w_out_ref.shape[0], :], NN)


def charge_kernel(pad_ref, feats_ref, species_ref, w_charge_ref, embed_ref, w_out_ref, *rest, groups):
    tiles, cotangents = rest[:4], rest[4 : 4 + groups // 2]
    keep_ref, send_ref, own_ref, mask_ref, part_ref, both, total = rest[4 + groups // 2 :]
    channels, atoms = feats_ref.shape
    embed_high, embed_low = halves(embed_ref[...])
    for block in range(atoms // 256):
        lanes = slice(block * 256, (block + 1) * 256)
        used = pad_ref[0:1, block : block + 1]
        mask = (lax.broadcasted_iota(jnp.int32, (1, 256), 1) < used).astype(F32)
        mask_ref[:, lanes] = mask
        species_at = lax.broadcasted_iota(jnp.int32, (embed_ref.shape[0], 256), 0)
        one_hot = (species_at == species_ref[:, lanes]).astype(BF16)
        both[0:channels, lanes] = mask * (
            dot3(w_charge_ref[...], feats_ref[:, lanes], TN)
            + dot16(embed_high, one_hot, TN)
            + dot16(embed_low, one_hot, TN)
        )
    for offset, cotangent in enumerate(cotangents):
        lanes, adjoint = adjoint_of(cotangent, offset, mask_ref, w_out_ref)
        both[channels:, lanes] = adjoint
        if offset == 0:
            own_ref[0:channels, :] = adjoint
            own_ref[channels : 2 * channels, :] = both[0:channels, lanes]
            own_ref[2 * channels :, :] = jnp.broadcast_to(mask_ref[:, lanes], (8, adjoint.shape[1]))
    near, far = halves_of_atoms(groups, atoms)
    sums = sum_over_atoms(tiles, near, both[:, near])
    total[...] = arranged(sums[:, :channels] + sum_over_atoms(tiles, far, both[0:channels, far]))
    split_by_core(total, keep_ref, send_ref)
    part_ref[...] = arranged(sums[:, channels:])


def adjoint_kernel(mask_ref, w_out_ref, part_ref, *rest, groups):
    tiles, cotangents = rest[:4], rest[4 : 4 + groups // 2]
    keep_ref, send_ref, adjoint_ref, total = rest[4 + groups // 2 :]
    for offset, cotangent in enumerate(cotangents):
        lanes, adjoint = adjoint_of(cotangent, groups // 2 + offset, mask_ref, w_out_ref)
        adjoint_ref[:, lanes] = adjoint
    _, far = halves_of_atoms(groups, adjoint_ref.shape[1])
    total[...] = part_ref[...] + arranged(sum_over_atoms(tiles, far, adjoint_ref[:, far]))
    split_by_core(total, keep_ref, send_ref)


def wave_kernel(pos_ref, packed_ref, width_ref, after_ref, *rest, atom_total):
    *gain_ref, cos, sin, cos_high, cos_low, sin_high, sin_low, k_ref, k_column = rest
    vectors = cos.shape[0]
    rows = vectors // 2
    core = lax.axis_index("atoms") % 2
    k_column[:, 0:3] = lattice_rows(packed_ref, width_ref.shape[1], vectors).T
    for flip in range(2):
        start = pl.multiple_of((core ^ flip) * rows, rows)
        k_ref[flip * rows : (flip + 1) * rows, :] = k_column[pl.ds(start, rows), :]
    if gain_ref:
        waves = [2.0 * math.pi * k_ref[0:rows, x : x + 1] for x in range(3)]
        square = waves[0] * waves[0] + waves[1] * waves[1] + waves[2] * waves[2]
        gain = jnp.exp(-square * width_ref[...]) * 40.0 / (square + 40.0) / math.sqrt(atom_total)
        gain_ref[0][...] = jnp.concatenate([gain, gain], axis=1)
    first = lax.axis_index("kvec") * cos.shape[1]
    trig_blocks(k_ref, pos_ref, first, (cos_high, cos_low, sin_high, sin_low), (cos, sin))


def coefficient_stack(sides, part):
    channels = sides[0].shape[2] // 2
    lanes = slice(part * channels, (part + 1) * channels)
    rows = [jnp.concatenate([side[0, :, lanes], side[1, :, lanes]], axis=1) for side in sides]
    high, low = halves(jnp.concatenate(rows, axis=0))
    return jnp.concatenate([high, low, high], axis=1)


def own_stack(own_ref, channels):
    high, low = halves(own_ref[0 : 2 * channels, :])
    return jnp.concatenate([high, high, low], axis=0)


def add_field(stack, tile_high, tile_low):
    width = stack.shape[1] // 3
    wide = dot16(stack[:, : 2 * width], tile_high, TN)
    return wide[:width] + wide[width:] + dot16(stack[:, :width], tile_low, TN)


def add_force(sums, wave, along, rows, first):
    step = 16
    cos, sin, _, _, _, _, k_ref = wave
    for start in range(0, rows.stop - rows.start, step):
        here = slice(rows.start + start, rows.start + start + step)
        there = slice(first + start, first + start + step)
        slope = cos[here, :] * along[1, there, :] - sin[here, :] * along[0, there, :]
        for x in range(3):
            term = k_ref[here, x : x + 1] * slope
            sums[x] = sums[x] + (term[0:8] + term[8:16])
    return sums


def fields(own_ref, refs, layout, channels, along, field, sums):
    entries = []
    for count, first in layout:
        wave, sides, refs = refs[:7], refs[7 : 7 + count], refs[7 + count :]
        rows = sides[0].shape[1]
        entries.append((wave, sides, slice(first * rows, (first + count) * rows)))
    other = own_stack(own_ref, channels)
    stacks = [[coefficient_stack(sides, part) for _, sides, _ in entries] for part in range(2)]
    for part in range(2):
        along[part] = dot16(jnp.concatenate(stacks[part], axis=0), other, NN)
    for at, (wave, _, rows) in enumerate(entries):
        _, _, cos_high, cos_low, sin_high, sin_low, _ = wave
        for part, high, low in ((0, cos_high, cos_low), (1, sin_high, sin_low)):
            added = add_field(stacks[part][at], high[rows, :], low[rows, :])
            field = added if field is None else field + added
    first = 0
    for wave, _, rows in entries:
        sums = add_force(sums, wave, along, rows, first)
        first += rows.stop - rows.start
    return field, sums


def partial_field_kernel(own_ref, *rest, layout, first):
    refs, field_ref, sums_ref, along = rest[:-3], *rest[-3:]
    share = own_ref.shape[1]
    if first:
        field, sums = None, [jnp.zeros((8, share), F32)] * 3
    else:
        refs, before = refs[:-2], refs[-2:]
        field, sums = before[0][...], [before[1][8 * x : 8 * x + 8, :] for x in range(3)]
    field, sums = fields(own_ref, refs, layout, field_ref.shape[0] // 2, along, field, sums)
    field_ref[...] = field
    for x in range(3):
        sums_ref[8 * x : 8 * x + 8, :] = sums[x]


def field_kernel(own_ref, w_out_ref, w_charge_ref, *rest, layout):
    refs, field_ref, sums_ref, message_ref, force_ref, grad_ref, along = rest[:-6], *rest[-6:]
    channels = w_out_ref.shape[0]
    sums = [sums_ref[8 * x : 8 * x + 8, :] for x in range(3)]
    field, sums = fields(own_ref, refs, layout, channels, along, field_ref[...], sums)
    field = own_ref[2 * channels : 2 * channels + 1, :] * field
    message_ref[...] = dot3(w_out_ref[...], field[:channels], TN)
    grad_ref[...] = dot3(w_charge_ref[...], field[channels:], NN)
    for x in range(3):
        force_ref[x : x + 1, :] = 2.0 * math.pi * jnp.sum(sums[x], axis=0, keepdims=True)


def swap(value, axis, offset):
    size = lax.axis_size(axis)
    return lax.ppermute(value, axis, [(place, place ^ offset) for place in range(size)])


def swap_along_z(value, even, odd):
    pairs = [(place, place ^ (odd if place % 2 else even)) for place in range(lax.axis_size("atoms"))]
    return lax.ppermute(value, "atoms", pairs)


def cost(work):
    return pl.CostEstimate(flops=work, bytes_accessed=0, transcendentals=0)


def on_device(
    positions, feats, species, pad_count, k_lattice, filter_width, w_charge, species_embed, w_out, grad_out,
):
    atom_count, group_count = lax.axis_size("atoms"), lax.axis_size("kvec")
    channels, atoms = feats.shape
    share = grad_out.shape[1]
    vectors = k_lattice.shape[1]
    half = vectors // 2
    both = 2 * channels
    f32 = lambda *shape: jax.ShapeDtypeStruct(shape, F32)
    bf16 = lambda *shape: jax.ShapeDtypeStruct(shape, BF16)

    def planes(value):
        return [swap(value, "kvec", m) for m in range(group_count - 1, 0, -1)][::-1]

    chunks = -(-vectors // share)
    below = -(-3 * chunks // 8) * 8
    packed = jnp.pad(grad_out, ((0, below), (0, 0)))
    for n in range(chunks):
        chunk = k_lattice[:, n * share : (n + 1) * share]
        first = channels + 3 * n
        packed += jnp.pad(chunk, ((first, channels + below - first - 3), (0, share - chunk.shape[1]))).astype(F32)

    packed = [packed] + planes(packed)

    tiles = []
    for part in range(2):
        tiles += pl.pallas_call(
            functools.partial(tile_kernel, channels=channels, vectors=vectors, first=part * half),
            out_shape=[bf16(vectors, atoms)] * 2,
            in_specs=[VMEM] * 2,
            out_specs=[VMEM] * 2,
            scratch_shapes=[pltpu.VMEM((half, 128), F32)],
            compiler_params=PARAMS,
            cost_estimate=cost(9000 * half * atoms),
            name="waves_of_own_vectors",
        )(positions, packed[0])

    middle = group_count // 2
    keep_h, send_h, own, mask, part = pl.pallas_call(
        functools.partial(charge_kernel, groups=group_count),
        out_shape=[f32(half, both)] * 2 + [f32(both + 8, share), f32(1, atoms), f32(vectors, both)],
        in_specs=[VMEM] * (10 + middle),
        out_specs=[VMEM] * 5,
        scratch_shapes=[pltpu.VMEM((both, atoms), F32), pltpu.VMEM((vectors, both), F32)],
        compiler_params=PARAMS,
        cost_estimate=cost(60 * vectors * atoms * channels),
        name="charge_sums",
    )(
        pad_count.reshape(1, -1), feats, species.reshape(1, atoms), w_charge, species_embed.T, w_out,
        *tiles, *packed[:middle],
    )

    wave_shapes = [f32(vectors, share)] * 2 + [bf16(vectors, share)] * 4 + [f32(vectors, 128)]

    def waves_of(group, after):
        shapes = ([f32(half, both)] if group == 0 else []) + wave_shapes
        made = pl.pallas_call(
            functools.partial(wave_kernel, atom_total=atoms * atom_count),
            out_shape=shapes,
            in_specs=[VMEM, VMEM, VMEM, ANY],
            out_specs=[VMEM] * len(shapes),
            scratch_shapes=[pltpu.VMEM((vectors, 128), F32)],
            compiler_params=PARAMS,
            cost_estimate=cost(20 * vectors * share),
            name="waves_of_own_atoms",
        )(positions, packed[group], filter_width.reshape(1, channels), after)
        return list(made)

    arrived_h = swap(send_h, "atoms", 1)
    keep_b, send_b = pl.pallas_call(
        functools.partial(adjoint_kernel, groups=group_count),
        out_shape=[f32(half, both)] * 2,
        in_specs=[VMEM] * (7 + middle),
        out_specs=[VMEM] * 2,
        scratch_shapes=[pltpu.VMEM((channels, atoms), F32), pltpu.VMEM((vectors, both), F32)],
        compiler_params=PARAMS,
        cost_estimate=cost(60 * vectors * atoms * channels),
        name="adjoint_sums",
    )(mask, w_out, part, *tiles, *packed[middle:])

    arrived_h, send_b = lax.optimization_barrier((arrived_h, send_b))
    arrived_b = swap(send_b, "atoms", 1)
    sum_h = keep_h + arrived_h
    steps = [2 << n for n in range((atom_count // 2).bit_length() - 1)]
    next_h = swap_along_z(sum_h, steps[0], steps[-1])
    arrived_b, sum_h = lax.optimization_barrier((arrived_b, sum_h))
    sum_b = keep_b + arrived_b
    next_b = swap_along_z(sum_b, steps[0], steps[-1])

    def more_waves(count, after):
        return [waves_of(group, after) for group in range(len(waves), min(len(waves) + count, group_count))]

    waves = []
    beside = more_waves(2, sum_b)
    next_h, next_b, beside = lax.optimization_barrier((next_h, next_b, beside))
    waves += beside
    total = jnp.stack([sum_h + next_h, sum_b + next_b])
    for at, step in enumerate(zip(steps[1:], steps[-2::-1])):
        arrived = swap_along_z(total, *step)
        beside = more_waves(group_count if at + 2 == len(steps) else 1, total)
        arrived, beside = lax.optimization_barrier((arrived, beside))
        waves += beside
        total = total + arrived
    gain, *waves[0] = waves[0]
    near = gain[None] * total
    plane = {0: near}
    for group in range(group_count - 1, 0, -1):
        plane[group] = swap(near, "kvec", group)
    far = {0: swap(near, "atoms", 1)}

    def operands_of(parts):
        sides = [[plane[group], far.get(group)][first : first + count] for group, count, first in parts]
        return [ref for part, side in zip(parts, sides) for ref in list(waves[part[0]]) + side]

    def field_sizes(parts):
        layout = tuple(part[1:] for part in parts)
        return layout, pltpu.VMEM((2, sum(count for count, _ in layout) * half, share), F32)

    def partial_fields(parts, before):
        layout, scratch = field_sizes(parts)
        operands = [own, *operands_of(parts), *before]
        return pl.pallas_call(
            functools.partial(partial_field_kernel, layout=layout, first=not before),
            out_shape=[f32(both, share), f32(24, share)],
            in_specs=[VMEM] * len(operands),
            out_specs=[VMEM] * 2,
            scratch_shapes=[scratch],
            compiler_params=PARAMS,
            cost_estimate=cost(vectors * share),
            name="fields_of_some_groups",
        )(*operands)

    fields_so_far = partial_fields([(0, 2, 0)], [])
    for group in range(group_count - 1, 0, -1):
        plane[group], fields_so_far = lax.optimization_barrier((plane[group], fields_so_far))
        far[group] = swap(plane[group], "atoms", 1)
    late = [2, 1] if group_count > 3 else [1]
    parts = [(group, 2, 0) for group in range(group_count - 1, len(late), -1)] + [(group, 1, 0) for group in late]
    fields_so_far = partial_fields(parts, fields_so_far)

    parts = [(group, 1, 1) for group in late]
    layout, scratch = field_sizes(parts)
    operands = [own, w_out, w_charge, *operands_of(parts), *fields_so_far]
    return tuple(
        pl.pallas_call(
            functools.partial(field_kernel, layout=layout),
            out_shape=[f32(channels, share), f32(3, share), f32(channels, share)],
            in_specs=[VMEM] * len(operands),
            out_specs=[VMEM] * 3,
            scratch_shapes=[scratch],
            compiler_params=PARAMS,
            cost_estimate=cost(vectors * share),
            name="fields_and_forces",
        )(*operands)
    )


def solution(mesh):
    shared = P(None, ("atoms", "kvec"))
    placed = (
        P(None, "atoms"), P(None, "atoms"), P("atoms"), P("atoms"), P(None, "kvec"),
        P(), P(), P(), P(), shared,
    )
    return jax.shard_map(
        on_device, mesh=mesh, in_specs=placed, out_specs=(shared, shared, shared), check_vma=False
    )
```

```python
import functools
import math

import jax
import jax.numpy as jnp
from jax import lax
from jax.experimental import pallas as pl
from jax.experimental.pallas import tpu as pltpu
from jax.sharding import PartitionSpec as P

F32, BF16 = jnp.float32, jnp.bfloat16
HALF_SIN = (4.442867755889893, -7.307443618774414, 3.594788074493408, -0.7843740582466125)
HALF_COS = (1.4142135381698608, -6.978850841522217, 5.7394609451293945, -1.8835630416870117, 0.31069818139076233)
VMEM = pl.BlockSpec(memory_space=pltpu.VMEM)
ANY = pl.BlockSpec(memory_space=pl.ANY)
PARAMS = pltpu.CompilerParams(vmem_limit_bytes=32 * 2**20)
NN, NT, TN = ((1,), (0,)), ((1,), (1,)), ((0,), (0,))


def halves(value):
    high = value.astype(BF16)
    return high, (value - high.astype(F32)).astype(BF16)


def dot16(left, right, dims):
    return lax.dot_general(left, right, (dims, ((), ())), preferred_element_type=F32)


def dot3(left, right, dims):
    left_high, left_low = halves(left)
    right_high, right_low = halves(right)
    return (
        dot16(left_high, right_high, dims)
        + dot16(left_low, right_high, dims)
        + dot16(left_high, right_low, dims)
    )


def horner(terms, square):
    total = terms[-1] * square + terms[-2]
    for term in terms[-3::-1]:
        total = total * square + term
    return total


def trig(columns, rows):
    turns = columns[0] * rows[0] + columns[1] * rows[1] + columns[2] * rows[2]
    turns = turns - jnp.round(turns)
    square = turns * turns
    half_sin = horner(HALF_SIN, square) * turns
    return 1.0 - half_sin * half_sin, half_sin * horner(HALF_COS, square)


def trig_blocks(k_ref, pos_ref, first, high_low, full=None):
    vectors, atoms = high_low[0].shape
    step = 32
    width = min(256, atoms)
    per_body = max(1, 2048 // atoms)
    per_body = min(per_body, vectors // step)

    def body(block, _):
        for inner in range(per_body):
            here = pl.ds(pl.multiple_of((block * per_body + inner) * step, step), step)
            columns = [k_ref[here, x : x + 1] for x in range(3)]
            for chunk in range(atoms // width):
                lanes = pl.ds(chunk * width, width)
                start = chunk * width if first is None else pl.multiple_of(first + chunk * width, 128)
                rows = [pos_ref[x : x + 1, pl.ds(start, width)] for x in range(3)]
                cos, sin = trig(columns, rows)
                high_low[0][here, lanes], high_low[1][here, lanes] = halves(cos)
                high_low[2][here, lanes], high_low[3][here, lanes] = halves(sin)
                if full is not None:
                    full[0][here, lanes], full[1][here, lanes] = cos, sin
        return 0

    lax.fori_loop(0, vectors // (step * per_body), body, 0)


def lattice_rows(packed, channels, vectors):
    share = packed.shape[1]
    width = min(share, vectors)
    chunks = [packed[channels + 3 * n : channels + 3 * n + 3, 0:width] for n in range(-(-vectors // share))]
    return jnp.concatenate(chunks, axis=1)


def tile_kernel(pos_ref, packed_ref, high_ref, low_ref, k_column, *, channels, vectors, first):
    rows = k_column.shape[0]
    k_column[:, 0:3] = lattice_rows(packed_ref, channels, vectors)[:, first : first + rows].T
    cos, sin = pl.ds(0, rows), pl.ds(rows, rows)
    trig_blocks(k_column, pos_ref, None, (high_ref.at[cos], low_ref.at[cos], high_ref.at[sin], low_ref.at[sin]))


def sum_over_atoms(tiles, lanes, value):
    count = value.shape[0]
    high, low = halves(value)
    tiles_high = jnp.concatenate([tile[:, lanes] for tile in tiles[::2]], axis=0)
    tiles_low = jnp.concatenate([tile[:, lanes] for tile in tiles[1::2]], axis=0)
    wide = dot16(tiles_high, jnp.concatenate([high, low], axis=0), NT)
    return wide[:, :count] + wide[:, count:] + dot16(tiles_low, high, NT)


def arranged(sums):
    rows = sums.shape[0] // 4
    parts = [sums[n * rows : (n + 1) * rows] for n in range(4)]
    return jnp.concatenate([jnp.concatenate(parts[:2], axis=1), jnp.concatenate(parts[2:], axis=1)], axis=0)


def split_by_core(total, keep_ref, send_ref):
    rows = keep_ref.shape[0]
    core = lax.axis_index("atoms") % 2
    for flip, out in enumerate((keep_ref, send_ref)):
        out[...] = total[pl.ds(pl.multiple_of((core ^ flip) * rows, rows), rows), :]


def halves_of_atoms(groups, atoms):
    side = lax.axis_index("kvec") // (groups // 2)
    span = atoms // 2
    return [pl.ds(pl.multiple_of(at * span, span), span) for at in (side, 1 - side)]


def adjoint_of(cotangent_ref, offset, mask_ref, w_out_ref):
    share = cotangent_ref.shape[1]
    lanes = pl.ds(pl.multiple_of((lax.axis_index("kvec") ^ offset) * share, share), share)
    return lanes, mask_ref[:, lanes] * dot3(w_out_ref[...], cotangent_ref[0 : w_out_ref.shape[0], :], NN)


def charge_kernel(pad_ref, feats_ref, species_ref, w_charge_ref, embed_ref, w_out_ref, *rest, groups):
    tiles, cotangents = rest[:4], rest[4 : 4 + groups // 2]
    keep_ref, send_ref, own_ref, mask_ref, part_ref, both, total = rest[4 + groups // 2 :]
    channels, atoms = feats_ref.shape
    embed_high, embed_low = halves(embed_ref[...])
    for block in range(atoms // 256):
        lanes = slice(block * 256, (block + 1) * 256)
        used = pad_ref[0:1, block : block + 1]
        mask = (lax.broadcasted_iota(jnp.int32, (1, 256), 1) < used).astype(F32)
        mask_ref[:, lanes] = mask
        species_at = lax.broadcasted_iota(jnp.int32, (embed_ref.shape[0], 256), 0)
        one_hot = (species_at == species_ref[:, lanes]).astype(BF16)
        both[0:channels, lanes] = mask * (
            dot3(w_charge_ref[...], feats_ref[:, lanes], TN)
            + dot16(embed_high, one_hot, TN)
            + dot16(embed_low, one_hot, TN)
        )
    for offset, cotangent in enumerate(cotangents):
        lanes, adjoint = adjoint_of(cotangent, offset, mask_ref, w_out_ref)
        both[channels:, lanes] = adjoint
        if offset == 0:
            own_ref[0:channels, :] = adjoint
            own_ref[channels : 2 * channels, :] = both[0:channels, lanes]
            own_ref[2 * channels :, :] = jnp.broadcast_to(mask_ref[:, lanes], (8, adjoint.shape[1]))
    near, far = halves_of_atoms(groups, atoms)
    sums = sum_over_atoms(tiles, near, both[:, near])
    total[...] = arranged(sums[:, :channels] + sum_over_atoms(tiles, far, both[0:channels, far]))
    split_by_core(total, keep_ref, send_ref)
    part_ref[...] = arranged(sums[:, channels:])


def adjoint_kernel(mask_ref, w_out_ref, part_ref, *rest, groups):
    tiles, cotangents = rest[:4], rest[4 : 4 + groups // 2]
    keep_ref, send_ref, adjoint_ref, total = rest[4 + groups // 2 :]
    for offset, cotangent in enumerate(cotangents):
        lanes, adjoint = adjoint_of(cotangent, groups // 2 + offset, mask_ref, w_out_ref)
        adjoint_ref[:, lanes] = adjoint
    _, far = halves_of_atoms(groups, adjoint_ref.shape[1])
    total[...] = part_ref[...] + arranged(sum_over_atoms(tiles, far, adjoint_ref[:, far]))
    split_by_core(total, keep_ref, send_ref)


def wave_kernel(pos_ref, packed_ref, width_ref, after_ref, *rest, atom_total):
    *gain_ref, cos, sin, cos_high, cos_low, sin_high, sin_low, k_ref, k_column = rest
    vectors = cos.shape[0]
    rows = vectors // 2
    core = lax.axis_index("atoms") % 2
    k_column[:, 0:3] = lattice_rows(packed_ref, width_ref.shape[1], vectors).T
    for flip in range(2):
        start = pl.multiple_of((core ^ flip) * rows, rows)
        k_ref[flip * rows : (flip + 1) * rows, :] = k_column[pl.ds(start, rows), :]
    if gain_ref:
        waves = [2.0 * math.pi * k_ref[0:rows, x : x + 1] for x in range(3)]
        square = waves[0] * waves[0] + waves[1] * waves[1] + waves[2] * waves[2]
        gain = jnp.exp(-square * width_ref[...]) * 40.0 / (square + 40.0) / math.sqrt(atom_total)
        gain_ref[0][...] = jnp.concatenate([gain, gain], axis=1)
    first = lax.axis_index("kvec") * cos.shape[1]
    trig_blocks(k_ref, pos_ref, first, (cos_high, cos_low, sin_high, sin_low), (cos, sin))


def coefficient_stack(sides, part):
    channels = sides[0].shape[2] // 2
    lanes = slice(part * channels, (part + 1) * channels)
    rows = [jnp.concatenate([side[0, :, lanes], side[1, :, lanes]], axis=1) for side in sides]
    high, low = halves(jnp.concatenate(rows, axis=0))
    return jnp.concatenate([high, low, high], axis=1)


def own_stack(own_ref, channels):
    high, low = halves(own_ref[0 : 2 * channels, :])
    return jnp.concatenate([high, high, low], axis=0)


def add_field(stack, tile_high, tile_low):
    width = stack.shape[1] // 3
    wide = dot16(stack[:, : 2 * width], tile_high, TN)
    return wide[:width] + wide[width:] + dot16(stack[:, :width], tile_low, TN)


def add_force(sums, wave, along, rows, first):
    step = 16
    cos, sin, _, _, _, _, k_ref = wave
    for start in range(0, rows.stop - rows.start, step):
        here = slice(rows.start + start, rows.start + start + step)
        there = slice(first + start, first + start + step)
        slope = cos[here, :] * along[1, there, :] - sin[here, :] * along[0, there, :]
        for x in range(3):
            term = k_ref[here, x : x + 1] * slope
            sums[x] = sums[x] + (term[0:8] + term[8:16])
    return sums


def fields(own_ref, refs, layout, channels, along, field, sums):
    entries = []
    for count, first in layout:
        wave, sides, refs = refs[:7], refs[7 : 7 + count], refs[7 + count :]
        rows = sides[0].shape[1]
        entries.append((wave, sides, slice(first * rows, (first + count) * rows)))
    other = own_stack(own_ref, channels)
    stacks = [[coefficient_stack(sides, part) for _, sides, _ in entries] for part in range(2)]
    for part in range(2):
        along[part] = dot16(jnp.concatenate(stacks[part], axis=0), other, NN)
    for at, (wave, _, rows) in enumerate(entries):
        _, _, cos_high, cos_low, sin_high, sin_low, _ = wave
        for part, high, low in ((0, cos_high, cos_low), (1, sin_high, sin_low)):
            added = add_field(stacks[part][at], high[rows, :], low[rows, :])
            field = added if field is None else field + added
    first = 0
    for wave, _, rows in entries:
        sums = add_force(sums, wave, along, rows, first)
        first += rows.stop - rows.start
    return field, sums


def partial_field_kernel(own_ref, *rest, layout, first):
    refs, field_ref, sums_ref, along = rest[:-3], *rest[-3:]
    share = own_ref.shape[1]
    if first:
        field, sums = None, [jnp.zeros((8, share), F32)] * 3
    else:
        refs, before = refs[:-2], refs[-2:]
        field, sums = before[0][...], [before[1][8 * x : 8 * x + 8, :] for x in range(3)]
    field, sums = fields(own_ref, refs, layout, field_ref.shape[0] // 2, along, field, sums)
    field_ref[...] = field
    for x in range(3):
        sums_ref[8 * x : 8 * x + 8, :] = sums[x]


def field_kernel(own_ref, w_out_ref, w_charge_ref, *rest, layout):
    refs, field_ref, sums_ref, message_ref, force_ref, grad_ref, along = rest[:-6], *rest[-6:]
    channels = w_out_ref.shape[0]
    sums = [sums_ref[8 * x : 8 * x + 8, :] for x in range(3)]
    field, sums = fields(own_ref, refs, layout, channels, along, field_ref[...], sums)
    field = own_ref[2 * channels : 2 * channels + 1, :] * field
    message_ref[...] = dot3(w_out_ref[...], field[:channels], TN)
    grad_ref[...] = dot3(w_charge_ref[...], field[channels:], NN)
    for x in range(3):
        force_ref[x : x + 1, :] = 2.0 * math.pi * jnp.sum(sums[x], axis=0, keepdims=True)


def swap(value, axis, offset):
    size = lax.axis_size(axis)
    return lax.ppermute(value, axis, [(place, place ^ offset) for place in range(size)])


def swap_along_z(value, even, odd):
    pairs = [(place, place ^ (odd if place % 2 else even)) for place in range(lax.axis_size("atoms"))]
    return lax.ppermute(value, "atoms", pairs)


def cost(work):
    return pl.CostEstimate(flops=work, bytes_accessed=0, transcendentals=0)


def on_device(
    positions, feats, species, pad_count, k_lattice, filter_width, w_charge, species_embed, w_out, grad_out,
):
    atom_count, group_count = lax.axis_size("atoms"), lax.axis_size("kvec")
    channels, atoms = feats.shape
    share = grad_out.shape[1]
    vectors = k_lattice.shape[1]
    half = vectors // 2
    both = 2 * channels
    f32 = lambda *shape: jax.ShapeDtypeStruct(shape, F32)
    bf16 = lambda *shape: jax.ShapeDtypeStruct(shape, BF16)

    def planes(value):
        return [swap(value, "kvec", m) for m in range(group_count - 1, 0, -1)][::-1]

    chunks = -(-vectors // share)
    below = -(-3 * chunks // 8) * 8
    packed = jnp.pad(grad_out, ((0, below), (0, 0)))
    for n in range(chunks):
        chunk = k_lattice[:, n * share : (n + 1) * share]
        first = channels + 3 * n
        packed += jnp.pad(chunk, ((first, channels + below - first - 3), (0, share - chunk.shape[1]))).astype(F32)

    packed = [packed] + planes(packed)

    tiles = []
    for part in range(2):
        tiles += pl.pallas_call(
            functools.partial(tile_kernel, channels=channels, vectors=vectors, first=part * half),
            out_shape=[bf16(vectors, atoms)] * 2,
            in_specs=[VMEM] * 2,
            out_specs=[VMEM] * 2,
            scratch_shapes=[pltpu.VMEM((half, 128), F32)],
            compiler_params=PARAMS,
            cost_estimate=cost(9000 * half * atoms),
            name="waves_of_own_vectors",
        )(positions, packed[0])

    middle = group_count // 2
    keep_h, send_h, own, mask, part = pl.pallas_call(
        functools.partial(charge_kernel, groups=group_count),
        out_shape=[f32(half, both)] * 2 + [f32(both + 8, share), f32(1, atoms), f32(vectors, both)],
        in_specs=[VMEM] * (10 + middle),
        out_specs=[VMEM] * 5,
        scratch_shapes=[pltpu.VMEM((both, atoms), F32), pltpu.VMEM((vectors, both), F32)],
        compiler_params=PARAMS,
        cost_estimate=cost(60 * vectors * atoms * channels),
        name="charge_sums",
    )(
        pad_count.reshape(1, -1), feats, species.reshape(1, atoms), w_charge, species_embed.T, w_out,
        *tiles, *packed[:middle],
    )

    wave_shapes = [f32(vectors, share)] * 2 + [bf16(vectors, share)] * 4 + [f32(vectors, 128)]

    def waves_of(group, after):
        shapes = ([f32(half, both)] if group == 0 else []) + wave_shapes
        made = pl.pallas_call(
            functools.partial(wave_kernel, atom_total=atoms * atom_count),
            out_shape=shapes,
            in_specs=[VMEM, VMEM, VMEM, ANY],
            out_specs=[VMEM] * len(shapes),
            scratch_shapes=[pltpu.VMEM((vectors, 128), F32)],
            compiler_params=PARAMS,
            cost_estimate=cost(20 * vectors * share),
            name="waves_of_own_atoms",
        )(positions, packed[group], filter_width.reshape(1, channels), after)
        return list(made)

    arrived_h = swap(send_h, "atoms", 1)
    keep_b, send_b = pl.pallas_call(
        functools.partial(adjoint_kernel, groups=group_count),
        out_shape=[f32(half, both)] * 2,
        in_specs=[VMEM] * (7 + middle),
        out_specs=[VMEM] * 2,
        scratch_shapes=[pltpu.VMEM((channels, atoms), F32), pltpu.VMEM((vectors, both), F32)],
        compiler_params=PARAMS,
        cost_estimate=cost(60 * vectors * atoms * channels),
        name="adjoint_sums",
    )(mask, w_out, part, *tiles, *packed[middle:])

    arrived_h, send_b = lax.optimization_barrier((arrived_h, send_b))
    arrived_b = swap(send_b, "atoms", 1)
    sum_h = keep_h + arrived_h
    steps = [2 << n for n in range((atom_count // 2).bit_length() - 1)]
    next_h = swap_along_z(sum_h, steps[0], steps[-1])
    arrived_b, sum_h = lax.optimization_barrier((arrived_b, sum_h))
    sum_b = keep_b + arrived_b
    next_b = swap_along_z(sum_b, steps[0], steps[-1])

    def more_waves(count, after):
        return [waves_of(group, after) for group in range(len(waves), min(len(waves) + count, group_count))]

    waves = []
    beside = more_waves(2, sum_b)
    next_h, next_b, beside = lax.optimization_barrier((next_h, next_b, beside))
    waves += beside
    total = jnp.stack([sum_h + next_h, sum_b + next_b])
    for at, step in enumerate(zip(steps[1:], steps[-2::-1])):
        arrived = swap_along_z(total, *step)
        beside = more_waves(group_count if at + 2 == len(steps) else 1, total)
        arrived, beside = lax.optimization_barrier((arrived, beside))
        waves += beside
        total = total + arrived
    gain, *waves[0] = waves[0]
    near = gain[None] * total
    plane = {0: near}
    for group in range(group_count - 1, 0, -1):
        plane[group] = swap(near, "kvec", group)
    far = {}

    def operands_of(parts):
        sides = [[plane[group], far.get(group)][first : first + count] for group, count, first in parts]
        return [ref for part, side in zip(parts, sides) for ref in list(waves[part[0]]) + side]

    def field_sizes(parts):
        layout = tuple(part[1:] for part in parts)
        return layout, pltpu.VMEM((2, sum(count for count, _ in layout) * half, share), F32)

    def partial_fields(parts, before):
        layout, scratch = field_sizes(parts)
        operands = [own, *operands_of(parts), *before]
        return pl.pallas_call(
            functools.partial(partial_field_kernel, layout=layout, first=not before),
            out_shape=[f32(both, share), f32(24, share)],
            in_specs=[VMEM] * len(operands),
            out_specs=[VMEM] * 2,
            scratch_shapes=[scratch],
            compiler_params=PARAMS,
            cost_estimate=cost(vectors * share),
            name="fields_of_some_groups",
        )(*operands)

    fields_so_far = partial_fields([(0, 1, 0)], [])
    late = [2, 1] if group_count > 3 else [1]
    early = [group for group in range(group_count - 1, 0, -1) if group not in late]
    for group in early:
        plane[group], near, fields_so_far = lax.optimization_barrier((plane[group], near, fields_so_far))
        if not far:
            far[0] = swap(near, "atoms", 1)
        far[group] = swap(plane[group], "atoms", 1)
    fields_so_far = partial_fields([(0, 1, 1)] + [(group, 1, 0) for group in early], fields_so_far)
    for group in late:
        plane[group], fields_so_far = lax.optimization_barrier((plane[group], fields_so_far))
        far[group] = swap(plane[group], "atoms", 1)
    parts = [(group, 1, 1) for group in early] + [(group, 1, 0) for group in late]
    fields_so_far = partial_fields(parts, fields_so_far)

    parts = [(group, 1, 1) for group in late]
    layout, scratch = field_sizes(parts)
    operands = [own, w_out, w_charge, *operands_of(parts), *fields_so_far]
    return tuple(
        pl.pallas_call(
            functools.partial(field_kernel, layout=layout),
            out_shape=[f32(channels, share), f32(3, share), f32(channels, share)],
            in_specs=[VMEM] * len(operands),
            out_specs=[VMEM] * 3,
            scratch_shapes=[scratch],
            compiler_params=PARAMS,
            cost_estimate=cost(vectors * share),
            name="fields_and_forces",
        )(*operands)
    )


def solution(mesh):
    shared = P(None, ("atoms", "kvec"))
    placed = (
        P(None, "atoms"), P(None, "atoms"), P("atoms"), P("atoms"), P(None, "kvec"),
        P(), P(), P(), P(), shared,
    )
    return jax.shard_map(
        on_device, mesh=mesh, in_specs=placed, out_specs=(shared, shared, shared), check_vma=False
    )
```

```python
import functools
import math

import jax
import jax.numpy as jnp
from jax import lax
from jax.experimental import pallas as pl
from jax.experimental.pallas import tpu as pltpu
from jax.sharding import PartitionSpec as P

F32, BF16 = jnp.float32, jnp.bfloat16
HALF_SIN = (4.442867755889893, -7.307443618774414, 3.594788074493408, -0.7843740582466125)
HALF_COS = (1.4142135381698608, -6.978850841522217, 5.7394609451293945, -1.8835630416870117, 0.31069818139076233)
VMEM = pl.BlockSpec(memory_space=pltpu.VMEM)
ANY = pl.BlockSpec(memory_space=pl.ANY)
PARAMS = pltpu.CompilerParams(vmem_limit_bytes=32 * 2**20)
NN, NT, TN = ((1,), (0,)), ((1,), (1,)), ((0,), (0,))


def halves(value):
    high = value.astype(BF16)
    return high, (value - high.astype(F32)).astype(BF16)


def dot16(left, right, dims):
    return lax.dot_general(left, right, (dims, ((), ())), preferred_element_type=F32)


def dot3(left, right, dims):
    left_high, left_low = halves(left)
    right_high, right_low = halves(right)
    return (
        dot16(left_high, right_high, dims)
        + dot16(left_low, right_high, dims)
        + dot16(left_high, right_low, dims)
    )


def horner(terms, square):
    total = terms[-1] * square + terms[-2]
    for term in terms[-3::-1]:
        total = total * square + term
    return total


def trig(columns, rows):
    turns = columns[0] * rows[0] + columns[1] * rows[1] + columns[2] * rows[2]
    turns = turns - jnp.round(turns)
    square = turns * turns
    half_sin = horner(HALF_SIN, square) * turns
    return 1.0 - half_sin * half_sin, half_sin * horner(HALF_COS, square)


def trig_blocks(k_ref, pos_ref, first, high_low, full=None):
    vectors, atoms = high_low[0].shape
    step = 32
    width = min(256, atoms)
    per_body = max(1, 2048 // atoms)
    per_body = min(per_body, vectors // step)

    def body(block, _):
        for inner in range(per_body):
            here = pl.ds(pl.multiple_of((block * per_body + inner) * step, step), step)
            columns = [k_ref[here, x : x + 1] for x in range(3)]
            for chunk in range(atoms // width):
                lanes = pl.ds(chunk * width, width)
                start = chunk * width if first is None else pl.multiple_of(first + chunk * width, 128)
                rows = [pos_ref[x : x + 1, pl.ds(start, width)] for x in range(3)]
                cos, sin = trig(columns, rows)
                high_low[0][here, lanes], high_low[1][here, lanes] = halves(cos)
                high_low[2][here, lanes], high_low[3][here, lanes] = halves(sin)
                if full is not None:
                    full[0][here, lanes], full[1][here, lanes] = cos, sin
        return 0

    lax.fori_loop(0, vectors // (step * per_body), body, 0)


def lattice_rows(packed, channels, vectors):
    share = packed.shape[1]
    width = min(share, vectors)
    chunks = [packed[channels + 3 * n : channels + 3 * n + 3, 0:width] for n in range(-(-vectors // share))]
    return jnp.concatenate(chunks, axis=1)


def tile_kernel(pos_ref, packed_ref, high_ref, low_ref, k_column, *, channels, vectors, first):
    rows = k_column.shape[0]
    k_column[:, 0:3] = lattice_rows(packed_ref, channels, vectors)[:, first : first + rows].T
    cos, sin = pl.ds(0, rows), pl.ds(rows, rows)
    trig_blocks(k_column, pos_ref, None, (high_ref.at[cos], low_ref.at[cos], high_ref.at[sin], low_ref.at[sin]))


def sum_over_atoms(tiles, lanes, value):
    count = value.shape[0]
    high, low = halves(value)
    tiles_high = jnp.concatenate([tile[:, lanes] for tile in tiles[::2]], axis=0)
    tiles_low = jnp.concatenate([tile[:, lanes] for tile in tiles[1::2]], axis=0)
    wide = dot16(tiles_high, jnp.concatenate([high, low], axis=0), NT)
    return wide[:, :count] + wide[:, count:] + dot16(tiles_low, high, NT)


def arranged(sums):
    rows = sums.shape[0] // 4
    parts = [sums[n * rows : (n + 1) * rows] for n in range(4)]
    return jnp.concatenate([jnp.concatenate(parts[:2], axis=1), jnp.concatenate(parts[2:], axis=1)], axis=0)


def split_by_core(total, keep_ref, send_ref):
    rows = keep_ref.shape[0]
    core = lax.axis_index("atoms") % 2
    for flip, out in enumerate((keep_ref, send_ref)):
        out[...] = total[pl.ds(pl.multiple_of((core ^ flip) * rows, rows), rows), :]


def halves_of_atoms(groups, atoms):
    side = lax.axis_index("kvec") // (groups // 2)
    span = atoms // 2
    return [pl.ds(pl.multiple_of(at * span, span), span) for at in (side, 1 - side)]


def adjoint_of(cotangent_ref, offset, mask_ref, w_out_ref):
    share = cotangent_ref.shape[1]
    lanes = pl.ds(pl.multiple_of((lax.axis_index("kvec") ^ offset) * share, share), share)
    return lanes, mask_ref[:, lanes] * dot3(w_out_ref[...], cotangent_ref[0 : w_out_ref.shape[0], :], NN)


def charge_kernel(pad_ref, feats_ref, species_ref, w_charge_ref, embed_ref, w_out_ref, *rest, groups):
    tiles, cotangents = rest[:4], rest[4 : 4 + groups // 2]
    keep_ref, send_ref, own_ref, mask_ref, part_ref, both, total = rest[4 + groups // 2 :]
    channels, atoms = feats_ref.shape
    embed_high, embed_low = halves(embed_ref[...])
    for block in range(atoms // 256):
        lanes = slice(block * 256, (block + 1) * 256)
        used = pad_ref[0:1, block : block + 1]
        mask = (lax.broadcasted_iota(jnp.int32, (1, 256), 1) < used).astype(F32)
        mask_ref[:, lanes] = mask
        species_at = lax.broadcasted_iota(jnp.int32, (embed_ref.shape[0], 256), 0)
        one_hot = (species_at == species_ref[:, lanes]).astype(BF16)
        both[0:channels, lanes] = mask * (
            dot3(w_charge_ref[...], feats_ref[:, lanes], TN)
            + dot16(embed_high, one_hot, TN)
            + dot16(embed_low, one_hot, TN)
        )
    for offset, cotangent in enumerate(cotangents):
        lanes, adjoint = adjoint_of(cotangent, offset, mask_ref, w_out_ref)
        both[channels:, lanes] = adjoint
        if offset == 0:
            own_ref[0:channels, :] = adjoint
            own_ref[channels : 2 * channels, :] = both[0:channels, lanes]
            own_ref[2 * channels :, :] = jnp.broadcast_to(mask_ref[:, lanes], (8, adjoint.shape[1]))
    near, far = halves_of_atoms(groups, atoms)
    sums = sum_over_atoms(tiles, near, both[:, near])
    total[...] = arranged(sums[:, :channels] + sum_over_atoms(tiles, far, both[0:channels, far]))
    split_by_core(total, keep_ref, send_ref)
    part_ref[...] = arranged(sums[:, channels:])


def adjoint_kernel(mask_ref, w_out_ref, part_ref, *rest, groups):
    tiles, cotangents = rest[:4], rest[4 : 4 + groups // 2]
    keep_ref, send_ref, adjoint_ref, total = rest[4 + groups // 2 :]
    for offset, cotangent in enumerate(cotangents):
        lanes, adjoint = adjoint_of(cotangent, groups // 2 + offset, mask_ref, w_out_ref)
        adjoint_ref[:, lanes] = adjoint
    _, far = halves_of_atoms(groups, adjoint_ref.shape[1])
    total[...] = part_ref[...] + arranged(sum_over_atoms(tiles, far, adjoint_ref[:, far]))
    split_by_core(total, keep_ref, send_ref)


def wave_kernel(pos_ref, packed_ref, width_ref, after_ref, *rest, atom_total):
    *gain_ref, cos, sin, cos_high, cos_low, sin_high, sin_low, k_ref, k_column = rest
    vectors = cos.shape[0]
    rows = vectors // 2
    core = lax.axis_index("atoms") % 2
    k_column[:, 0:3] = lattice_rows(packed_ref, width_ref.shape[1], vectors).T
    for flip in range(2):
        start = pl.multiple_of((core ^ flip) * rows, rows)
        k_ref[flip * rows : (flip + 1) * rows, :] = k_column[pl.ds(start, rows), :]
    if gain_ref:
        waves = [2.0 * math.pi * k_ref[0:rows, x : x + 1] for x in range(3)]
        square = waves[0] * waves[0] + waves[1] * waves[1] + waves[2] * waves[2]
        gain = jnp.exp(-square * width_ref[...]) * 40.0 / (square + 40.0) / math.sqrt(atom_total)
        gain_ref[0][...] = jnp.concatenate([gain, gain], axis=1)
    first = lax.axis_index("kvec") * cos.shape[1]
    trig_blocks(k_ref, pos_ref, first, (cos_high, cos_low, sin_high, sin_low), (cos, sin))


def coefficient_stack(sides, part):
    channels = sides[0].shape[2] // 2
    lanes = slice(part * channels, (part + 1) * channels)
    rows = [jnp.concatenate([side[0, :, lanes], side[1, :, lanes]], axis=1) for side in sides]
    high, low = halves(jnp.concatenate(rows, axis=0))
    return jnp.concatenate([high, low, high], axis=1)


def own_stack(own_ref, channels):
    high, low = halves(own_ref[0 : 2 * channels, :])
    return jnp.concatenate([high, high, low], axis=0)


def add_field(stack, tile_high, tile_low):
    width = stack.shape[1] // 3
    wide = dot16(stack[:, : 2 * width], tile_high, TN)
    return wide[:width] + wide[width:] + dot16(stack[:, :width], tile_low, TN)


def add_force(sums, wave, along, rows, first):
    step = 16
    cos, sin, _, _, _, _, k_ref = wave
    for start in range(0, rows.stop - rows.start, step):
        here = slice(rows.start + start, rows.start + start + step)
        there = slice(first + start, first + start + step)
        slope = cos[here, :] * along[1, there, :] - sin[here, :] * along[0, there, :]
        for x in range(3):
            term = k_ref[here, x : x + 1] * slope
            sums[x] = sums[x] + (term[0:8] + term[8:16])
    return sums


def fields(own_ref, refs, layout, channels, along, field, sums):
    entries = []
    for count, first in layout:
        wave, sides, refs = refs[:7], refs[7 : 7 + count], refs[7 + count :]
        rows = sides[0].shape[1]
        entries.append((wave, sides, slice(first * rows, (first + count) * rows)))
    other = own_stack(own_ref, channels)
    stacks = [[coefficient_stack(sides, part) for _, sides, _ in entries] for part in range(2)]
    for part in range(2):
        along[part] = dot16(jnp.concatenate(stacks[part], axis=0), other, NN)
    for at, (wave, _, rows) in enumerate(entries):
        _, _, cos_high, cos_low, sin_high, sin_low, _ = wave
        for part, high, low in ((0, cos_high, cos_low), (1, sin_high, sin_low)):
            added = add_field(stacks[part][at], high[rows, :], low[rows, :])
            field = added if field is None else field + added
    first = 0
    for wave, _, rows in entries:
        sums = add_force(sums, wave, along, rows, first)
        first += rows.stop - rows.start
    return field, sums


def partial_field_kernel(own_ref, *rest, layout, first):
    refs, field_ref, sums_ref, along = rest[:-3], *rest[-3:]
    share = own_ref.shape[1]
    if first:
        field, sums = None, [jnp.zeros((8, share), F32)] * 3
    else:
        refs, before = refs[:-2], refs[-2:]
        field, sums = before[0][...], [before[1][8 * x : 8 * x + 8, :] for x in range(3)]
    field, sums = fields(own_ref, refs, layout, field_ref.shape[0] // 2, along, field, sums)
    field_ref[...] = field
    for x in range(3):
        sums_ref[8 * x : 8 * x + 8, :] = sums[x]


def field_kernel(own_ref, w_out_ref, w_charge_ref, *rest, layout):
    refs, field_ref, sums_ref, message_ref, force_ref, grad_ref, along = rest[:-6], *rest[-6:]
    channels = w_out_ref.shape[0]
    sums = [sums_ref[8 * x : 8 * x + 8, :] for x in range(3)]
    field, sums = fields(own_ref, refs, layout, channels, along, field_ref[...], sums)
    field = own_ref[2 * channels : 2 * channels + 1, :] * field
    message_ref[...] = dot3(w_out_ref[...], field[:channels], TN)
    grad_ref[...] = dot3(w_charge_ref[...], field[channels:], NN)
    for x in range(3):
        force_ref[x : x + 1, :] = 2.0 * math.pi * jnp.sum(sums[x], axis=0, keepdims=True)


def swap(value, axis, offset):
    size = lax.axis_size(axis)
    return lax.ppermute(value, axis, [(place, place ^ offset) for place in range(size)])


def swap_along_z(value, even, odd):
    pairs = [(place, place ^ (odd if place % 2 else even)) for place in range(lax.axis_size("atoms"))]
    return lax.ppermute(value, "atoms", pairs)


def cost(work):
    return pl.CostEstimate(flops=work, bytes_accessed=0, transcendentals=0)


def on_device(
    positions, feats, species, pad_count, k_lattice, filter_width, w_charge, species_embed, w_out, grad_out,
):
    atom_count, group_count = lax.axis_size("atoms"), lax.axis_size("kvec")
    channels, atoms = feats.shape
    share = grad_out.shape[1]
    vectors = k_lattice.shape[1]
    half = vectors // 2
    both = 2 * channels
    f32 = lambda *shape: jax.ShapeDtypeStruct(shape, F32)
    bf16 = lambda *shape: jax.ShapeDtypeStruct(shape, BF16)

    def planes(value):
        return [swap(value, "kvec", m) for m in range(group_count - 1, 0, -1)][::-1]

    chunks = -(-vectors // share)
    below = -(-3 * chunks // 8) * 8
    packed = jnp.pad(grad_out, ((0, below), (0, 0)))
    for n in range(chunks):
        chunk = k_lattice[:, n * share : (n + 1) * share]
        first = channels + 3 * n
        packed += jnp.pad(chunk, ((first, channels + below - first - 3), (0, share - chunk.shape[1]))).astype(F32)

    packed = [packed] + planes(packed)

    tiles = []
    for part in range(2):
        tiles += pl.pallas_call(
            functools.partial(tile_kernel, channels=channels, vectors=vectors, first=part * half),
            out_shape=[bf16(vectors, atoms)] * 2,
            in_specs=[VMEM] * 2,
            out_specs=[VMEM] * 2,
            scratch_shapes=[pltpu.VMEM((half, 128), F32)],
            compiler_params=PARAMS,
            cost_estimate=cost(9000 * half * atoms),
            name="waves_of_own_vectors",
        )(positions, packed[0])

    middle = group_count // 2
    keep_h, send_h, own, mask, part = pl.pallas_call(
        functools.partial(charge_kernel, groups=group_count),
        out_shape=[f32(half, both)] * 2 + [f32(both + 8, share), f32(1, atoms), f32(vectors, both)],
        in_specs=[VMEM] * (10 + middle),
        out_specs=[VMEM] * 5,
        scratch_shapes=[pltpu.VMEM((both, atoms), F32), pltpu.VMEM((vectors, both), F32)],
        compiler_params=PARAMS,
        cost_estimate=cost(60 * vectors * atoms * channels),
        name="charge_sums",
    )(
        pad_count.reshape(1, -1), feats, species.reshape(1, atoms), w_charge, species_embed.T, w_out,
        *tiles, *packed[:middle],
    )

    wave_shapes = [f32(vectors, share)] * 2 + [bf16(vectors, share)] * 4 + [f32(vectors, 128)]

    def waves_of(group, after):
        shapes = ([f32(half, both)] if group == 0 else []) + wave_shapes
        made = pl.pallas_call(
            functools.partial(wave_kernel, atom_total=atoms * atom_count),
            out_shape=shapes,
            in_specs=[VMEM, VMEM, VMEM, ANY],
            out_specs=[VMEM] * len(shapes),
            scratch_shapes=[pltpu.VMEM((vectors, 128), F32)],
            compiler_params=PARAMS,
            cost_estimate=cost(20 * vectors * share),
            name="waves_of_own_atoms",
        )(positions, packed[group], filter_width.reshape(1, channels), after)
        return list(made)

    arrived_h = swap(send_h, "atoms", 1)
    keep_b, send_b = pl.pallas_call(
        functools.partial(adjoint_kernel, groups=group_count),
        out_shape=[f32(half, both)] * 2,
        in_specs=[VMEM] * (7 + middle),
        out_specs=[VMEM] * 2,
        scratch_shapes=[pltpu.VMEM((channels, atoms), F32), pltpu.VMEM((vectors, both), F32)],
        compiler_params=PARAMS,
        cost_estimate=cost(60 * vectors * atoms * channels),
        name="adjoint_sums",
    )(mask, w_out, part, *tiles, *packed[middle:])

    arrived_h, send_b = lax.optimization_barrier((arrived_h, send_b))
    arrived_b = swap(send_b, "atoms", 1)
    sum_h = keep_h + arrived_h
    steps = [2 << n for n in range((atom_count // 2).bit_length() - 1)]
    next_h = swap_along_z(sum_h, steps[0], steps[-1])
    arrived_b, sum_h = lax.optimization_barrier((arrived_b, sum_h))
    sum_b = keep_b + arrived_b
    next_b = swap_along_z(sum_b, steps[0], steps[-1])

    def more_waves(count, after):
        return [waves_of(group, after) for group in range(len(waves), min(len(waves) + count, group_count))]

    waves = []
    beside = more_waves(2, sum_b)
    next_h, next_b, beside = lax.optimization_barrier((next_h, next_b, beside))
    waves += beside
    total = jnp.stack([sum_h + next_h, sum_b + next_b])
    for at, step in enumerate(zip(steps[1:], steps[-2::-1])):
        arrived = swap_along_z(total, *step)
        beside = more_waves(group_count if at + 2 == len(steps) else 1, total)
        arrived, beside = lax.optimization_barrier((arrived, beside))
        waves += beside
        total = total + arrived
    gain, *waves[0] = waves[0]
    near = gain[None] * total
    plane = {0: near}
    for group in range(group_count - 1, 0, -1):
        plane[group] = swap(near, "kvec", group)
    far = {}

    def operands_of(parts):
        sides = [[plane[group], far.get(group)][first : first + count] for group, count, first in parts]
        return [ref for part, side in zip(parts, sides) for ref in list(waves[part[0]]) + side]

    def field_sizes(parts):
        layout = tuple(part[1:] for part in parts)
        return layout, pltpu.VMEM((2, sum(count for count, _ in layout) * half, share), F32)

    def partial_fields(parts, before):
        layout, scratch = field_sizes(parts)
        operands = [own, *operands_of(parts), *before]
        return pl.pallas_call(
            functools.partial(partial_field_kernel, layout=layout, first=not before),
            out_shape=[f32(both, share), f32(24, share)],
            in_specs=[VMEM] * len(operands),
            out_specs=[VMEM] * 2,
            scratch_shapes=[scratch],
            compiler_params=PARAMS,
            cost_estimate=cost(vectors * share),
            name="fields_of_some_groups",
        )(*operands)

    fields_so_far = partial_fields([(0, 1, 0)], [])
    late = [2, 1] if group_count > 3 else [1]
    early = [group for group in range(group_count - 1, 0, -1) if group not in late]
    for group in early:
        plane[group], near, fields_so_far = lax.optimization_barrier((plane[group], near, fields_so_far))
        if not far:
            far[0] = swap(near, "atoms", 1)
        far[group] = swap(plane[group], "atoms", 1)
    fields_so_far = partial_fields([(group, 1, 0) for group in early], fields_so_far)
    for group in late:
        plane[group], fields_so_far = lax.optimization_barrier((plane[group], fields_so_far))
        far[group] = swap(plane[group], "atoms", 1)
    parts = [(group, 1, 1) for group in [0] + early] + [(group, 1, 0) for group in late]
    fields_so_far = partial_fields(parts, fields_so_far)

    parts = [(group, 1, 1) for group in late]
    layout, scratch = field_sizes(parts)
    operands = [own, w_out, w_charge, *operands_of(parts), *fields_so_far]
    return tuple(
        pl.pallas_call(
            functools.partial(field_kernel, layout=layout),
            out_shape=[f32(channels, share), f32(3, share), f32(channels, share)],
            in_specs=[VMEM] * len(operands),
            out_specs=[VMEM] * 3,
            scratch_shapes=[scratch],
            compiler_params=PARAMS,
            cost_estimate=cost(vectors * share),
            name="fields_and_forces",
        )(*operands)
    )


def solution(mesh):
    shared = P(None, ("atoms", "kvec"))
    placed = (
        P(None, "atoms"), P(None, "atoms"), P("atoms"), P("atoms"), P(None, "kvec"),
        P(), P(), P(), P(), shared,
    )
    return jax.shard_map(
        on_device, mesh=mesh, in_specs=placed, out_specs=(shared, shared, shared), check_vma=False
    )
```

```python
import functools
import math

import jax
import jax.numpy as jnp
from jax import lax
from jax.experimental import pallas as pl
from jax.experimental.pallas import tpu as pltpu
from jax.sharding import PartitionSpec as P

F32, BF16 = jnp.float32, jnp.bfloat16
HALF_SIN = (4.442867755889893, -7.307443618774414, 3.594788074493408, -0.7843740582466125)
HALF_COS = (1.4142135381698608, -6.978850841522217, 5.7394609451293945, -1.8835630416870117, 0.31069818139076233)
VMEM = pl.BlockSpec(memory_space=pltpu.VMEM)
ANY = pl.BlockSpec(memory_space=pl.ANY)
PARAMS = pltpu.CompilerParams(vmem_limit_bytes=32 * 2**20)
NN, NT, TN = ((1,), (0,)), ((1,), (1,)), ((0,), (0,))


def halves(value):
    high = value.astype(BF16)
    return high, (value - high.astype(F32)).astype(BF16)


def dot16(left, right, dims):
    return lax.dot_general(left, right, (dims, ((), ())), preferred_element_type=F32)


def dot3(left, right, dims):
    left_high, left_low = halves(left)
    right_high, right_low = halves(right)
    return (
        dot16(left_high, right_high, dims)
        + dot16(left_low, right_high, dims)
        + dot16(left_high, right_low, dims)
    )


def horner(terms, square):
    total = terms[-1] * square + terms[-2]
    for term in terms[-3::-1]:
        total = total * square + term
    return total


def trig(columns, rows):
    turns = columns[0] * rows[0] + columns[1] * rows[1] + columns[2] * rows[2]
    turns = turns - jnp.round(turns)
    square = turns * turns
    half_sin = horner(HALF_SIN, square) * turns
    return 1.0 - half_sin * half_sin, half_sin * horner(HALF_COS, square)


def trig_blocks(k_ref, pos_ref, first, high_low, full=None):
    vectors, atoms = high_low[0].shape
    step = 32
    width = min(256, atoms)
    per_body = max(1, 2048 // atoms)
    per_body = min(per_body, vectors // step)

    def body(block, _):
        for inner in range(per_body):
            here = pl.ds(pl.multiple_of((block * per_body + inner) * step, step), step)
            columns = [k_ref[here, x : x + 1] for x in range(3)]
            for chunk in range(atoms // width):
                lanes = pl.ds(chunk * width, width)
                start = chunk * width if first is None else pl.multiple_of(first + chunk * width, 128)
                rows = [pos_ref[x : x + 1, pl.ds(start, width)] for x in range(3)]
                cos, sin = trig(columns, rows)
                high_low[0][here, lanes], high_low[1][here, lanes] = halves(cos)
                high_low[2][here, lanes], high_low[3][here, lanes] = halves(sin)
                if full is not None:
                    full[0][here, lanes], full[1][here, lanes] = cos, sin
        return 0

    lax.fori_loop(0, vectors // (step * per_body), body, 0)


def lattice_rows(packed, channels, vectors):
    share = packed.shape[1]
    width = min(share, vectors)
    chunks = [packed[channels + 3 * n : channels + 3 * n + 3, 0:width] for n in range(-(-vectors // share))]
    return jnp.concatenate(chunks, axis=1)


def tile_kernel(pos_ref, packed_ref, high_ref, low_ref, k_column, *, channels, vectors, first):
    rows = k_column.shape[0]
    k_column[:, 0:3] = lattice_rows(packed_ref, channels, vectors)[:, first : first + rows].T
    cos, sin = pl.ds(0, rows), pl.ds(rows, rows)
    trig_blocks(k_column, pos_ref, None, (high_ref.at[cos], low_ref.at[cos], high_ref.at[sin], low_ref.at[sin]))


def sum_over_atoms(tiles, lanes, value):
    count = value.shape[0]
    high, low = halves(value)
    tiles_high = jnp.concatenate([tile[:, lanes] for tile in tiles[::2]], axis=0)
    tiles_low = jnp.concatenate([tile[:, lanes] for tile in tiles[1::2]], axis=0)
    wide = dot16(tiles_high, jnp.concatenate([high, low], axis=0), NT)
    return wide[:, :count] + wide[:, count:] + dot16(tiles_low, high, NT)


def arranged(sums):
    rows = sums.shape[0] // 4
    parts = [sums[n * rows : (n + 1) * rows] for n in range(4)]
    return jnp.concatenate([jnp.concatenate(parts[:2], axis=1), jnp.concatenate(parts[2:], axis=1)], axis=0)


def split_by_core(total, keep_ref, send_ref):
    rows = keep_ref.shape[0]
    core = lax.axis_index("atoms") % 2
    for flip, out in enumerate((keep_ref, send_ref)):
        out[...] = total[pl.ds(pl.multiple_of((core ^ flip) * rows, rows), rows), :]


def halves_of_atoms(groups, atoms):
    side = lax.axis_index("kvec") // (groups // 2)
    span = atoms // 2
    return [pl.ds(pl.multiple_of(at * span, span), span) for at in (side, 1 - side)]


def adjoint_of(cotangent_ref, offset, mask_ref, w_out_ref):
    share = cotangent_ref.shape[1]
    lanes = pl.ds(pl.multiple_of((lax.axis_index("kvec") ^ offset) * share, share), share)
    return lanes, mask_ref[:, lanes] * dot3(w_out_ref[...], cotangent_ref[0 : w_out_ref.shape[0], :], NN)


def charge_kernel(pad_ref, feats_ref, species_ref, w_charge_ref, embed_ref, w_out_ref, *rest, groups):
    tiles, cotangents = rest[:4], rest[4 : 4 + groups // 2]
    keep_ref, send_ref, own_ref, mask_ref, part_ref, both, total = rest[4 + groups // 2 :]
    channels, atoms = feats_ref.shape
    embed_high, embed_low = halves(embed_ref[...])
    for block in range(atoms // 256):
        lanes = slice(block * 256, (block + 1) * 256)
        used = pad_ref[0:1, block : block + 1]
        mask = (lax.broadcasted_iota(jnp.int32, (1, 256), 1) < used).astype(F32)
        mask_ref[:, lanes] = mask
        species_at = lax.broadcasted_iota(jnp.int32, (embed_ref.shape[0], 256), 0)
        one_hot = (species_at == species_ref[:, lanes]).astype(BF16)
        both[0:channels, lanes] = mask * (
            dot3(w_charge_ref[...], feats_ref[:, lanes], TN)
            + dot16(embed_high, one_hot, TN)
            + dot16(embed_low, one_hot, TN)
        )
    for offset, cotangent in enumerate(cotangents):
        lanes, adjoint = adjoint_of(cotangent, offset, mask_ref, w_out_ref)
        both[channels:, lanes] = adjoint
        if offset == 0:
            own_ref[0:channels, :] = adjoint
            own_ref[channels : 2 * channels, :] = both[0:channels, lanes]
            own_ref[2 * channels :, :] = jnp.broadcast_to(mask_ref[:, lanes], (8, adjoint.shape[1]))
    near, far = halves_of_atoms(groups, atoms)
    sums = sum_over_atoms(tiles, near, both[:, near])
    total[...] = arranged(sums[:, :channels] + sum_over_atoms(tiles, far, both[0:channels, far]))
    split_by_core(total, keep_ref, send_ref)
    part_ref[...] = arranged(sums[:, channels:])


def adjoint_kernel(mask_ref, w_out_ref, part_ref, *rest, groups):
    tiles, cotangents = rest[:4], rest[4 : 4 + groups // 2]
    keep_ref, send_ref, adjoint_ref, total = rest[4 + groups // 2 :]
    for offset, cotangent in enumerate(cotangents):
        lanes, adjoint = adjoint_of(cotangent, groups // 2 + offset, mask_ref, w_out_ref)
        adjoint_ref[:, lanes] = adjoint
    _, far = halves_of_atoms(groups, adjoint_ref.shape[1])
    total[...] = part_ref[...] + arranged(sum_over_atoms(tiles, far, adjoint_ref[:, far]))
    split_by_core(total, keep_ref, send_ref)


def wave_kernel(pos_ref, packed_ref, width_ref, after_ref, *rest, atom_total):
    *gain_ref, cos, sin, cos_high, cos_low, sin_high, sin_low, k_ref, k_column = rest
    vectors = cos.shape[0]
    rows = vectors // 2
    core = lax.axis_index("atoms") % 2
    k_column[:, 0:3] = lattice_rows(packed_ref, width_ref.shape[1], vectors).T
    for flip in range(2):
        start = pl.multiple_of((core ^ flip) * rows, rows)
        k_ref[flip * rows : (flip + 1) * rows, :] = k_column[pl.ds(start, rows), :]
    if gain_ref:
        waves = [2.0 * math.pi * k_ref[0:rows, x : x + 1] for x in range(3)]
        square = waves[0] * waves[0] + waves[1] * waves[1] + waves[2] * waves[2]
        gain = jnp.exp(-square * width_ref[...]) * 40.0 / (square + 40.0) / math.sqrt(atom_total)
        gain_ref[0][...] = jnp.concatenate([gain, gain], axis=1)
    first = lax.axis_index("kvec") * cos.shape[1]
    trig_blocks(k_ref, pos_ref, first, (cos_high, cos_low, sin_high, sin_low), (cos, sin))


def coefficient_stack(sides, part):
    channels = sides[0].shape[2] // 2
    lanes = slice(part * channels, (part + 1) * channels)
    rows = [jnp.concatenate([side[0, :, lanes], side[1, :, lanes]], axis=1) for side in sides]
    high, low = halves(jnp.concatenate(rows, axis=0))
    return jnp.concatenate([high, low, high], axis=1)


def own_stack(own_ref, channels):
    high, low = halves(own_ref[0 : 2 * channels, :])
    return jnp.concatenate([high, high, low], axis=0)


def add_field(stack, tile_high, tile_low):
    width = stack.shape[1] // 3
    wide = dot16(stack[:, : 2 * width], tile_high, TN)
    return wide[:width] + wide[width:] + dot16(stack[:, :width], tile_low, TN)


def add_force(sums, wave, along, rows, first):
    step = 16
    cos, sin, _, _, _, _, k_ref = wave
    for start in range(0, rows.stop - rows.start, step):
        here = slice(rows.start + start, rows.start + start + step)
        there = slice(first + start, first + start + step)
        slope = cos[here, :] * along[1, there, :] - sin[here, :] * along[0, there, :]
        for x in range(3):
            term = k_ref[here, x : x + 1] * slope
            sums[x] = sums[x] + (term[0:8] + term[8:16])
    return sums


def fields(own_ref, refs, layout, channels, along, field, sums):
    entries = []
    for count, first in layout:
        wave, sides, refs = refs[:7], refs[7 : 7 + count], refs[7 + count :]
        rows = sides[0].shape[1]
        entries.append((wave, sides, slice(first * rows, (first + count) * rows)))
    stack = jnp.concatenate([coefficient_stack(sides, part) for part in range(2) for _, sides, _ in entries], axis=0)
    depth = stack.shape[0] // 2
    slopes = dot16(stack, own_stack(own_ref, channels), NN)
    for part in range(2):
        along[part] = slopes[part * depth : (part + 1) * depth]
    tiles = [
        jnp.concatenate([wave[at][rows, :] for at in kinds for wave, _, rows in entries], axis=0)
        for kinds in ((2, 4), (3, 5))
    ]
    added = add_field(stack, *tiles)
    field = added if field is None else field + added
    first = 0
    for wave, _, rows in entries:
        sums = add_force(sums, wave, along, rows, first)
        first += rows.stop - rows.start
    return field, sums


def partial_field_kernel(own_ref, *rest, layout, first):
    refs, field_ref, sums_ref, along = rest[:-3], *rest[-3:]
    share = own_ref.shape[1]
    if first:
        field, sums = None, [jnp.zeros((8, share), F32)] * 3
    else:
        refs, before = refs[:-2], refs[-2:]
        field, sums = before[0][...], [before[1][8 * x : 8 * x + 8, :] for x in range(3)]
    field, sums = fields(own_ref, refs, layout, field_ref.shape[0] // 2, along, field, sums)
    field_ref[...] = field
    for x in range(3):
        sums_ref[8 * x : 8 * x + 8, :] = sums[x]


def field_kernel(own_ref, w_out_ref, w_charge_ref, *rest, layout):
    refs, field_ref, sums_ref, message_ref, force_ref, grad_ref, along = rest[:-6], *rest[-6:]
    channels = w_out_ref.shape[0]
    sums = [sums_ref[8 * x : 8 * x + 8, :] for x in range(3)]
    field, sums = fields(own_ref, refs, layout, channels, along, field_ref[...], sums)
    field = own_ref[2 * channels : 2 * channels + 1, :] * field
    message_ref[...] = dot3(w_out_ref[...], field[:channels], TN)
    grad_ref[...] = dot3(w_charge_ref[...], field[channels:], NN)
    for x in range(3):
        force_ref[x : x + 1, :] = 2.0 * math.pi * jnp.sum(sums[x], axis=0, keepdims=True)


def swap(value, axis, offset):
    size = lax.axis_size(axis)
    return lax.ppermute(value, axis, [(place, place ^ offset) for place in range(size)])


def swap_along_z(value, even, odd):
    pairs = [(place, place ^ (odd if place % 2 else even)) for place in range(lax.axis_size("atoms"))]
    return lax.ppermute(value, "atoms", pairs)


def cost(work):
    return pl.CostEstimate(flops=work, bytes_accessed=0, transcendentals=0)


def on_device(
    positions, feats, species, pad_count, k_lattice, filter_width, w_charge, species_embed, w_out, grad_out,
):
    atom_count, group_count = lax.axis_size("atoms"), lax.axis_size("kvec")
    channels, atoms = feats.shape
    share = grad_out.shape[1]
    vectors = k_lattice.shape[1]
    half = vectors // 2
    both = 2 * channels
    f32 = lambda *shape: jax.ShapeDtypeStruct(shape, F32)
    bf16 = lambda *shape: jax.ShapeDtypeStruct(shape, BF16)

    def planes(value):
        return [swap(value, "kvec", m) for m in range(group_count - 1, 0, -1)][::-1]

    chunks = -(-vectors // share)
    below = -(-3 * chunks // 8) * 8
    packed = jnp.pad(grad_out, ((0, below), (0, 0)))
    for n in range(chunks):
        chunk = k_lattice[:, n * share : (n + 1) * share]
        first = channels + 3 * n
        packed += jnp.pad(chunk, ((first, channels + below - first - 3), (0, share - chunk.shape[1]))).astype(F32)

    packed = [packed] + planes(packed)

    tiles = []
    for part in range(2):
        tiles += pl.pallas_call(
            functools.partial(tile_kernel, channels=channels, vectors=vectors, first=part * half),
            out_shape=[bf16(vectors, atoms)] * 2,
            in_specs=[VMEM] * 2,
            out_specs=[VMEM] * 2,
            scratch_shapes=[pltpu.VMEM((half, 128), F32)],
            compiler_params=PARAMS,
            cost_estimate=cost(9000 * half * atoms),
            name="waves_of_own_vectors",
        )(positions, packed[0])

    middle = group_count // 2
    keep_h, send_h, own, mask, part = pl.pallas_call(
        functools.partial(charge_kernel, groups=group_count),
        out_shape=[f32(half, both)] * 2 + [f32(both + 8, share), f32(1, atoms), f32(vectors, both)],
        in_specs=[VMEM] * (10 + middle),
        out_specs=[VMEM] * 5,
        scratch_shapes=[pltpu.VMEM((both, atoms), F32), pltpu.VMEM((vectors, both), F32)],
        compiler_params=PARAMS,
        cost_estimate=cost(60 * vectors * atoms * channels),
        name="charge_sums",
    )(
        pad_count.reshape(1, -1), feats, species.reshape(1, atoms), w_charge, species_embed.T, w_out,
        *tiles, *packed[:middle],
    )

    wave_shapes = [f32(vectors, share)] * 2 + [bf16(vectors, share)] * 4 + [f32(vectors, 128)]

    def waves_of(group, after):
        shapes = ([f32(half, both)] if group == 0 else []) + wave_shapes
        made = pl.pallas_call(
            functools.partial(wave_kernel, atom_total=atoms * atom_count),
            out_shape=shapes,
            in_specs=[VMEM, VMEM, VMEM, ANY],
            out_specs=[VMEM] * len(shapes),
            scratch_shapes=[pltpu.VMEM((vectors, 128), F32)],
            compiler_params=PARAMS,
            cost_estimate=cost(20 * vectors * share),
            name="waves_of_own_atoms",
        )(positions, packed[group], filter_width.reshape(1, channels), after)
        return list(made)

    arrived_h = swap(send_h, "atoms", 1)
    keep_b, send_b = pl.pallas_call(
        functools.partial(adjoint_kernel, groups=group_count),
        out_shape=[f32(half, both)] * 2,
        in_specs=[VMEM] * (7 + middle),
        out_specs=[VMEM] * 2,
        scratch_shapes=[pltpu.VMEM((channels, atoms), F32), pltpu.VMEM((vectors, both), F32)],
        compiler_params=PARAMS,
        cost_estimate=cost(60 * vectors * atoms * channels),
        name="adjoint_sums",
    )(mask, w_out, part, *tiles, *packed[middle:])

    arrived_h, send_b = lax.optimization_barrier((arrived_h, send_b))
    arrived_b = swap(send_b, "atoms", 1)
    sum_h = keep_h + arrived_h
    steps = [2 << n for n in range((atom_count // 2).bit_length() - 1)]
    next_h = swap_along_z(sum_h, steps[0], steps[-1])
    arrived_b, sum_h = lax.optimization_barrier((arrived_b, sum_h))
    sum_b = keep_b + arrived_b
    next_b = swap_along_z(sum_b, steps[0], steps[-1])

    def more_waves(count, after):
        return [waves_of(group, after) for group in range(len(waves), min(len(waves) + count, group_count))]

    waves = []
    beside = more_waves(2, sum_b)
    next_h, next_b, beside = lax.optimization_barrier((next_h, next_b, beside))
    waves += beside
    total = jnp.stack([sum_h + next_h, sum_b + next_b])
    for at, step in enumerate(zip(steps[1:], steps[-2::-1])):
        arrived = swap_along_z(total, *step)
        beside = more_waves(group_count if at + 2 == len(steps) else 1, total)
        arrived, beside = lax.optimization_barrier((arrived, beside))
        waves += beside
        total = total + arrived
    gain, *waves[0] = waves[0]
    near = gain[None] * total
    plane = {0: near}
    for group in range(group_count - 1, 0, -1):
        plane[group] = swap(near, "kvec", group)
    far = {}

    def operands_of(parts):
        sides = [[plane[group], far.get(group)][first : first + count] for group, count, first in parts]
        return [ref for part, side in zip(parts, sides) for ref in list(waves[part[0]]) + side]

    def field_sizes(parts):
        layout = tuple(part[1:] for part in parts)
        return layout, pltpu.VMEM((2, sum(count for count, _ in layout) * half, share), F32)

    def partial_fields(parts, before):
        layout, scratch = field_sizes(parts)
        operands = [own, *operands_of(parts), *before]
        return pl.pallas_call(
            functools.partial(partial_field_kernel, layout=layout, first=not before),
            out_shape=[f32(both, share), f32(24, share)],
            in_specs=[VMEM] * len(operands),
            out_specs=[VMEM] * 2,
            scratch_shapes=[scratch],
            compiler_params=PARAMS,
            cost_estimate=cost(vectors * share),
            name="fields_of_some_groups",
        )(*operands)

    fields_so_far = partial_fields([(0, 1, 0)], [])
    late = [2, 1] if group_count > 3 else [1]
    early = [group for group in range(group_count - 1, 0, -1) if group not in late]
    for group in early:
        plane[group], near, fields_so_far = lax.optimization_barrier((plane[group], near, fields_so_far))
        if not far:
            far[0] = swap(near, "atoms", 1)
        far[group] = swap(plane[group], "atoms", 1)
    fields_so_far = partial_fields([(group, 1, 0) for group in early], fields_so_far)
    for group in late:
        plane[group], fields_so_far = lax.optimization_barrier((plane[group], fields_so_far))
        far[group] = swap(plane[group], "atoms", 1)
    parts = [(group, 1, 1) for group in [0] + early] + [(group, 1, 0) for group in late]
    fields_so_far = partial_fields(parts, fields_so_far)

    parts = [(group, 1, 1) for group in late]
    layout, scratch = field_sizes(parts)
    operands = [own, w_out, w_charge, *operands_of(parts), *fields_so_far]
    return tuple(
        pl.pallas_call(
            functools.partial(field_kernel, layout=layout),
            out_shape=[f32(channels, share), f32(3, share), f32(channels, share)],
            in_specs=[VMEM] * len(operands),
            out_specs=[VMEM] * 3,
            scratch_shapes=[scratch],
            compiler_params=PARAMS,
            cost_estimate=cost(vectors * share),
            name="fields_and_forces",
        )(*operands)
    )


def solution(mesh):
    shared = P(None, ("atoms", "kvec"))
    placed = (
        P(None, "atoms"), P(None, "atoms"), P("atoms"), P("atoms"), P(None, "kvec"),
        P(), P(), P(), P(), shared,
    )
    return jax.shard_map(
        on_device, mesh=mesh, in_specs=placed, out_specs=(shared, shared, shared), check_vma=False
    )
```

```python
import functools
import math

import jax
import jax.numpy as jnp
from jax import lax
from jax.experimental import pallas as pl
from jax.experimental.pallas import tpu as pltpu
from jax.sharding import PartitionSpec as P

F32, BF16 = jnp.float32, jnp.bfloat16
HALF_SIN = (4.442867755889893, -7.307443618774414, 3.594788074493408, -0.7843740582466125)
HALF_COS = (1.4142135381698608, -6.978850841522217, 5.7394609451293945, -1.8835630416870117, 0.31069818139076233)
VMEM = pl.BlockSpec(memory_space=pltpu.VMEM)
ANY = pl.BlockSpec(memory_space=pl.ANY)
PARAMS = pltpu.CompilerParams(vmem_limit_bytes=32 * 2**20)
NN, NT, TN = ((1,), (0,)), ((1,), (1,)), ((0,), (0,))


def halves(value):
    high = value.astype(BF16)
    return high, (value - high.astype(F32)).astype(BF16)


def dot16(left, right, dims):
    return lax.dot_general(left, right, (dims, ((), ())), preferred_element_type=F32)


def dot3(left, right, dims):
    left_high, left_low = halves(left)
    right_high, right_low = halves(right)
    free = 1 - dims[0][0]
    count = left.shape[free]
    wide = dot16(jnp.concatenate([left_high, left_low], axis=free), right_high, dims)
    return wide[:count] + wide[count:] + dot16(left_high, right_low, dims)


def horner(terms, square):
    total = terms[-1] * square + terms[-2]
    for term in terms[-3::-1]:
        total = total * square + term
    return total


def trig(columns, rows):
    turns = columns[0] * rows[0] + columns[1] * rows[1] + columns[2] * rows[2]
    turns = turns - jnp.round(turns)
    square = turns * turns
    half_sin = horner(HALF_SIN, square) * turns
    return 1.0 - half_sin * half_sin, half_sin * horner(HALF_COS, square)


def trig_blocks(k_ref, pos_ref, first, high_low, full=None):
    vectors, atoms = high_low[0].shape
    step = 32
    width = min(256, atoms)
    per_body = max(1, 2048 // atoms)
    per_body = min(per_body, vectors // step)

    def body(block, _):
        for inner in range(per_body):
            here = pl.ds(pl.multiple_of((block * per_body + inner) * step, step), step)
            columns = [k_ref[here, x : x + 1] for x in range(3)]
            for chunk in range(atoms // width):
                lanes = pl.ds(chunk * width, width)
                start = chunk * width if first is None else pl.multiple_of(first + chunk * width, 128)
                rows = [pos_ref[x : x + 1, pl.ds(start, width)] for x in range(3)]
                cos, sin = trig(columns, rows)
                high_low[0][here, lanes], high_low[1][here, lanes] = halves(cos)
                high_low[2][here, lanes], high_low[3][here, lanes] = halves(sin)
                if full is not None:
                    full[0][here, lanes], full[1][here, lanes] = cos, sin
        return 0

    lax.fori_loop(0, vectors // (step * per_body), body, 0)


def lattice_rows(packed, channels, vectors):
    share = packed.shape[1]
    width = min(share, vectors)
    chunks = [packed[channels + 3 * n : channels + 3 * n + 3, 0:width] for n in range(-(-vectors // share))]
    return jnp.concatenate(chunks, axis=1)


def tile_kernel(pos_ref, packed_ref, high_ref, low_ref, k_column, *, channels, vectors, first):
    rows = k_column.shape[0]
    k_column[:, 0:3] = lattice_rows(packed_ref, channels, vectors)[:, first : first + rows].T
    cos, sin = pl.ds(0, rows), pl.ds(rows, rows)
    trig_blocks(k_column, pos_ref, None, (high_ref.at[cos], low_ref.at[cos], high_ref.at[sin], low_ref.at[sin]))


def sum_over_atoms(tiles, lanes, value):
    count = value.shape[0]
    high, low = halves(value)
    tiles_high = jnp.concatenate([tile[:, lanes] for tile in tiles[::2]], axis=0)
    tiles_low = jnp.concatenate([tile[:, lanes] for tile in tiles[1::2]], axis=0)
    wide = dot16(tiles_high, jnp.concatenate([high, low], axis=0), NT)
    return wide[:, :count] + wide[:, count:] + dot16(tiles_low, high, NT)


def arranged(sums):
    rows = sums.shape[0] // 4
    parts = [sums[n * rows : (n + 1) * rows] for n in range(4)]
    return jnp.concatenate([jnp.concatenate(parts[:2], axis=1), jnp.concatenate(parts[2:], axis=1)], axis=0)


def split_by_core(total, keep_ref, send_ref):
    rows = keep_ref.shape[0]
    core = lax.axis_index("atoms") % 2
    for flip, out in enumerate((keep_ref, send_ref)):
        out[...] = total[pl.ds(pl.multiple_of((core ^ flip) * rows, rows), rows), :]


def halves_of_atoms(groups, atoms):
    side = lax.axis_index("kvec") // (groups // 2)
    span = atoms // 2
    return [pl.ds(pl.multiple_of(at * span, span), span) for at in (side, 1 - side)]


def adjoint_of(cotangent_ref, offset, mask_ref, w_out_ref):
    share = cotangent_ref.shape[1]
    lanes = pl.ds(pl.multiple_of((lax.axis_index("kvec") ^ offset) * share, share), share)
    return lanes, mask_ref[:, lanes] * dot3(w_out_ref[...], cotangent_ref[0 : w_out_ref.shape[0], :], NN)


def charge_kernel(pad_ref, feats_ref, species_ref, w_charge_ref, embed_ref, w_out_ref, *rest, groups):
    tiles, cotangents = rest[:4], rest[4 : 4 + groups // 2]
    keep_ref, send_ref, own_ref, mask_ref, part_ref, both, total = rest[4 + groups // 2 :]
    channels, atoms = feats_ref.shape
    embed_high, embed_low = halves(embed_ref[...])
    for block in range(atoms // 256):
        lanes = slice(block * 256, (block + 1) * 256)
        used = pad_ref[0:1, block : block + 1]
        mask = (lax.broadcasted_iota(jnp.int32, (1, 256), 1) < used).astype(F32)
        mask_ref[:, lanes] = mask
        species_at = lax.broadcasted_iota(jnp.int32, (embed_ref.shape[0], 256), 0)
        one_hot = (species_at == species_ref[:, lanes]).astype(BF16)
        both[0:channels, lanes] = mask * (
            dot3(w_charge_ref[...], feats_ref[:, lanes], TN)
            + dot16(embed_high, one_hot, TN)
            + dot16(embed_low, one_hot, TN)
        )
    for offset, cotangent in enumerate(cotangents):
        lanes, adjoint = adjoint_of(cotangent, offset, mask_ref, w_out_ref)
        both[channels:, lanes] = adjoint
        if offset == 0:
            own_ref[0:channels, :] = adjoint
            own_ref[channels : 2 * channels, :] = both[0:channels, lanes]
            own_ref[2 * channels :, :] = jnp.broadcast_to(mask_ref[:, lanes], (8, adjoint.shape[1]))
    near, far = halves_of_atoms(groups, atoms)
    sums = sum_over_atoms(tiles, near, both[:, near])
    total[...] = arranged(sums[:, :channels] + sum_over_atoms(tiles, far, both[0:channels, far]))
    split_by_core(total, keep_ref, send_ref)
    part_ref[...] = arranged(sums[:, channels:])


def adjoint_kernel(mask_ref, w_out_ref, part_ref, *rest, groups):
    tiles, cotangents = rest[:4], rest[4 : 4 + groups // 2]
    keep_ref, send_ref, adjoint_ref, total = rest[4 + groups // 2 :]
    for offset, cotangent in enumerate(cotangents):
        lanes, adjoint = adjoint_of(cotangent, groups // 2 + offset, mask_ref, w_out_ref)
        adjoint_ref[:, lanes] = adjoint
    _, far = halves_of_atoms(groups, adjoint_ref.shape[1])
    total[...] = part_ref[...] + arranged(sum_over_atoms(tiles, far, adjoint_ref[:, far]))
    split_by_core(total, keep_ref, send_ref)


def wave_kernel(pos_ref, packed_ref, width_ref, w_out_ref, w_charge_ref, after_ref, *rest, atom_total):
    *first_refs, cos, sin, cos_high, cos_low, sin_high, sin_low, k_ref, k_column = rest
    vectors = cos.shape[0]
    rows = vectors // 2
    core = lax.axis_index("atoms") % 2
    k_column[:, 0:3] = lattice_rows(packed_ref, width_ref.shape[1], vectors).T
    for flip in range(2):
        start = pl.multiple_of((core ^ flip) * rows, rows)
        k_ref[flip * rows : (flip + 1) * rows, :] = k_column[pl.ds(start, rows), :]
    if first_refs:
        gain_ref, project_ref = first_refs
        waves = [2.0 * math.pi * k_ref[0:rows, x : x + 1] for x in range(3)]
        square = waves[0] * waves[0] + waves[1] * waves[1] + waves[2] * waves[2]
        gain = jnp.exp(-square * width_ref[...]) * 40.0 / (square + 40.0) / math.sqrt(atom_total)
        gain_ref[...] = jnp.concatenate([gain, gain], axis=1)
        empty = jnp.zeros_like(w_charge_ref[...])
        blocks = (
            jnp.concatenate([w_out_ref[...].T, empty], axis=1),
            jnp.concatenate([empty, w_charge_ref[...]], axis=1),
        )
        project_ref[...] = jnp.concatenate(halves(jnp.concatenate(blocks, axis=0)), axis=0)
    first = lax.axis_index("kvec") * cos.shape[1]
    trig_blocks(k_ref, pos_ref, first, (cos_high, cos_low, sin_high, sin_low), (cos, sin))


def coefficient_stack(sides, part):
    channels = sides[0].shape[2] // 2
    lanes = slice(part * channels, (part + 1) * channels)
    rows = [jnp.concatenate([side[0, :, lanes], side[1, :, lanes]], axis=1) for side in sides]
    high, low = halves(jnp.concatenate(rows, axis=0))
    return jnp.concatenate([high, low, high], axis=1)


def own_stack(own_ref, channels):
    high, low = halves(own_ref[0 : 2 * channels, :])
    return jnp.concatenate([high, high, low], axis=0)


def add_field(stack, tile_high, tile_low):
    width = stack.shape[1] // 3
    wide = dot16(stack[:, : 2 * width], tile_high, TN)
    return wide[:width] + wide[width:] + dot16(stack[:, :width], tile_low, TN)


def add_force(sums, wave, along, rows, first):
    step = 16
    cos, sin, _, _, _, _, k_ref = wave
    for start in range(0, rows.stop - rows.start, step):
        here = slice(rows.start + start, rows.start + start + step)
        there = slice(first + start, first + start + step)
        slope = cos[here, :] * along[1, there, :] - sin[here, :] * along[0, there, :]
        for x in range(3):
            term = k_ref[here, x : x + 1] * slope
            sums[x] = sums[x] + (term[0:8] + term[8:16])
    return sums


def fields(own_ref, refs, layout, channels, along, field, sums):
    entries = []
    for count, first in layout:
        wave, sides, refs = refs[:7], refs[7 : 7 + count], refs[7 + count :]
        rows = sides[0].shape[1]
        entries.append((wave, sides, slice(first * rows, (first + count) * rows)))
    stack = jnp.concatenate([coefficient_stack(sides, part) for part in range(2) for _, sides, _ in entries], axis=0)
    depth = stack.shape[0] // 2
    slopes = dot16(stack, own_stack(own_ref, channels), NN)
    for part in range(2):
        along[part] = slopes[part * depth : (part + 1) * depth]
    tiles = [
        jnp.concatenate([wave[at][rows, :] for at in kinds for wave, _, rows in entries], axis=0)
        for kinds in ((2, 4), (3, 5))
    ]
    added = add_field(stack, *tiles)
    field = added if field is None else field + added
    first = 0
    for wave, _, rows in entries:
        sums = add_force(sums, wave, along, rows, first)
        first += rows.stop - rows.start
    return field, sums


def partial_field_kernel(own_ref, *rest, layout, first):
    refs, field_ref, sums_ref, along = rest[:-3], *rest[-3:]
    share = own_ref.shape[1]
    if first:
        field, sums = None, [jnp.zeros((8, share), F32)] * 3
    else:
        refs, before = refs[:-2], refs[-2:]
        field, sums = before[0][...], [before[1][8 * x : 8 * x + 8, :] for x in range(3)]
    field, sums = fields(own_ref, refs, layout, field_ref.shape[0] // 2, along, field, sums)
    field_ref[...] = field
    for x in range(3):
        sums_ref[8 * x : 8 * x + 8, :] = sums[x]


def field_kernel(own_ref, project_ref, *rest, layout):
    refs, field_ref, sums_ref, message_ref, force_ref, grad_ref, along = rest[:-6], *rest[-6:]
    channels = message_ref.shape[0]
    both = 2 * channels
    sums = [sums_ref[8 * x : 8 * x + 8, :] for x in range(3)]
    field, sums = fields(own_ref, refs, layout, channels, along, field_ref[...], sums)
    high, low = halves(own_ref[both : both + 1, :] * field)
    wide = dot16(project_ref[...], high, NN)
    projected = wide[:both] + wide[both:] + dot16(project_ref[0:both, :], low, NN)
    message_ref[...] = projected[:channels]
    grad_ref[...] = projected[channels:]
    for x in range(3):
        force_ref[x : x + 1, :] = 2.0 * math.pi * jnp.sum(sums[x], axis=0, keepdims=True)


def swap(value, axis, offset):
    size = lax.axis_size(axis)
    return lax.ppermute(value, axis, [(place, place ^ offset) for place in range(size)])


def swap_along_z(value, even, odd):
    pairs = [(place, place ^ (odd if place % 2 else even)) for place in range(lax.axis_size("atoms"))]
    return lax.ppermute(value, "atoms", pairs)


def cost(work):
    return pl.CostEstimate(flops=work, bytes_accessed=0, transcendentals=0)


def on_device(
    positions, feats, species, pad_count, k_lattice, filter_width, w_charge, species_embed, w_out, grad_out,
):
    atom_count, group_count = lax.axis_size("atoms"), lax.axis_size("kvec")
    channels, atoms = feats.shape
    share = grad_out.shape[1]
    vectors = k_lattice.shape[1]
    half = vectors // 2
    both = 2 * channels
    f32 = lambda *shape: jax.ShapeDtypeStruct(shape, F32)
    bf16 = lambda *shape: jax.ShapeDtypeStruct(shape, BF16)

    def planes(value):
        return [swap(value, "kvec", m) for m in range(group_count - 1, 0, -1)][::-1]

    chunks = -(-vectors // share)
    below = -(-3 * chunks // 8) * 8
    packed = jnp.pad(grad_out, ((0, below), (0, 0)))
    for n in range(chunks):
        chunk = k_lattice[:, n * share : (n + 1) * share]
        first = channels + 3 * n
        packed += jnp.pad(chunk, ((first, channels + below - first - 3), (0, share - chunk.shape[1]))).astype(F32)

    packed = [packed] + planes(packed)

    tiles = []
    for part in range(2):
        tiles += pl.pallas_call(
            functools.partial(tile_kernel, channels=channels, vectors=vectors, first=part * half),
            out_shape=[bf16(vectors, atoms)] * 2,
            in_specs=[VMEM] * 2,
            out_specs=[VMEM] * 2,
            scratch_shapes=[pltpu.VMEM((half, 128), F32)],
            compiler_params=PARAMS,
            cost_estimate=cost(9000 * half * atoms),
            name="waves_of_own_vectors",
        )(positions, packed[0])

    middle = group_count // 2
    keep_h, send_h, own, mask, part = pl.pallas_call(
        functools.partial(charge_kernel, groups=group_count),
        out_shape=[f32(half, both)] * 2 + [f32(both + 8, share), f32(1, atoms), f32(vectors, both)],
        in_specs=[VMEM] * (10 + middle),
        out_specs=[VMEM] * 5,
        scratch_shapes=[pltpu.VMEM((both, atoms), F32), pltpu.VMEM((vectors, both), F32)],
        compiler_params=PARAMS,
        cost_estimate=cost(60 * vectors * atoms * channels),
        name="charge_sums",
    )(
        pad_count.reshape(1, -1), feats, species.reshape(1, atoms), w_charge, species_embed.T, w_out,
        *tiles, *packed[:middle],
    )

    wave_shapes = [f32(vectors, share)] * 2 + [bf16(vectors, share)] * 4 + [f32(vectors, 128)]

    def waves_of(group, after):
        shapes = ([f32(half, both), bf16(2 * both, both)] if group == 0 else []) + wave_shapes
        made = pl.pallas_call(
            functools.partial(wave_kernel, atom_total=atoms * atom_count),
            out_shape=shapes,
            in_specs=[VMEM] * 5 + [ANY],
            out_specs=[VMEM] * len(shapes),
            scratch_shapes=[pltpu.VMEM((vectors, 128), F32)],
            compiler_params=PARAMS,
            cost_estimate=cost(20 * vectors * share),
            name="waves_of_own_atoms",
        )(positions, packed[group], filter_width.reshape(1, channels), w_out, w_charge, after)
        return list(made)

    arrived_h = swap(send_h, "atoms", 1)
    keep_b, send_b = pl.pallas_call(
        functools.partial(adjoint_kernel, groups=group_count),
        out_shape=[f32(half, both)] * 2,
        in_specs=[VMEM] * (7 + middle),
        out_specs=[VMEM] * 2,
        scratch_shapes=[pltpu.VMEM((channels, atoms), F32), pltpu.VMEM((vectors, both), F32)],
        compiler_params=PARAMS,
        cost_estimate=cost(60 * vectors * atoms * channels),
        name="adjoint_sums",
    )(mask, w_out, part, *tiles, *packed[middle:])

    arrived_h, send_b = lax.optimization_barrier((arrived_h, send_b))
    arrived_b = swap(send_b, "atoms", 1)
    sum_h = keep_h + arrived_h
    steps = [2 << n for n in range((atom_count // 2).bit_length() - 1)]
    next_h = swap_along_z(sum_h, steps[0], steps[-1])
    arrived_b, sum_h = lax.optimization_barrier((arrived_b, sum_h))
    sum_b = keep_b + arrived_b
    next_b = swap_along_z(sum_b, steps[0], steps[-1])

    def more_waves(count, after):
        return [waves_of(group, after) for group in range(len(waves), min(len(waves) + count, group_count))]

    waves = []
    beside = more_waves(2, sum_b)
    next_h, next_b, beside = lax.optimization_barrier((next_h, next_b, beside))
    waves += beside
    total = jnp.stack([sum_h + next_h, sum_b + next_b])
    for at, step in enumerate(zip(steps[1:], steps[-2::-1])):
        arrived = swap_along_z(total, *step)
        beside = more_waves(group_count if at + 2 == len(steps) else 1, total)
        arrived, beside = lax.optimization_barrier((arrived, beside))
        waves += beside
        total = total + arrived
    gain, project, *waves[0] = waves[0]
    near = gain[None] * total
    plane = {0: near}
    for group in range(group_count - 1, 0, -1):
        plane[group] = swap(near, "kvec", group)
    far = {}

    def operands_of(parts):
        sides = [[plane[group], far.get(group)][first : first + count] for group, count, first in parts]
        return [ref for part, side in zip(parts, sides) for ref in list(waves[part[0]]) + side]

    def field_sizes(parts):
        layout = tuple(part[1:] for part in parts)
        return layout, pltpu.VMEM((2, sum(count for count, _ in layout) * half, share), F32)

    def partial_fields(parts, before):
        layout, scratch = field_sizes(parts)
        operands = [own, *operands_of(parts), *before]
        return pl.pallas_call(
            functools.partial(partial_field_kernel, layout=layout, first=not before),
            out_shape=[f32(both, share), f32(24, share)],
            in_specs=[VMEM] * len(operands),
            out_specs=[VMEM] * 2,
            scratch_shapes=[scratch],
            compiler_params=PARAMS,
            cost_estimate=cost(vectors * share),
            name="fields_of_some_groups",
        )(*operands)

    fields_so_far = partial_fields([(0, 1, 0)], [])
    late = [2, 1] if group_count > 3 else [1]
    early = [group for group in range(group_count - 1, 0, -1) if group not in late]
    for group in early:
        plane[group], near, fields_so_far = lax.optimization_barrier((plane[group], near, fields_so_far))
        if not far:
            far[0] = swap(near, "atoms", 1)
        far[group] = swap(plane[group], "atoms", 1)
    fields_so_far = partial_fields([(group, 1, 0) for group in early], fields_so_far)
    for group in late:
        plane[group], fields_so_far = lax.optimization_barrier((plane[group], fields_so_far))
        far[group] = swap(plane[group], "atoms", 1)
    parts = [(group, 1, 1) for group in [0] + early] + [(group, 1, 0) for group in late]
    fields_so_far = partial_fields(parts, fields_so_far)

    parts = [(group, 1, 1) for group in late]
    layout, scratch = field_sizes(parts)
    operands = [own, project, *operands_of(parts), *fields_so_far]
    return tuple(
        pl.pallas_call(
            functools.partial(field_kernel, layout=layout),
            out_shape=[f32(channels, share), f32(3, share), f32(channels, share)],
            in_specs=[VMEM] * len(operands),
            out_specs=[VMEM] * 3,
            scratch_shapes=[scratch],
            compiler_params=PARAMS,
            cost_estimate=cost(vectors * share),
            name="fields_and_forces",
        )(*operands)
    )


def solution(mesh):
    shared = P(None, ("atoms", "kvec"))
    placed = (
        P(None, "atoms"), P(None, "atoms"), P("atoms"), P("atoms"), P(None, "kvec"),
        P(), P(), P(), P(), shared,
    )
    return jax.shard_map(
        on_device, mesh=mesh, in_specs=placed, out_specs=(shared, shared, shared), check_vma=False
    )
```

```python
import functools
import math

import jax
import jax.numpy as jnp
from jax import lax
from jax.experimental import pallas as pl
from jax.experimental.pallas import tpu as pltpu
from jax.sharding import PartitionSpec as P

F32, BF16 = jnp.float32, jnp.bfloat16
HALF_SIN = (4.442867755889893, -7.307443618774414, 3.594788074493408, -0.7843740582466125)
HALF_COS = (1.4142135381698608, -6.978850841522217, 5.7394609451293945, -1.8835630416870117, 0.31069818139076233)
VMEM = pl.BlockSpec(memory_space=pltpu.VMEM)
ANY = pl.BlockSpec(memory_space=pl.ANY)
PARAMS = pltpu.CompilerParams(vmem_limit_bytes=32 * 2**20)
NN, NT, TN = ((1,), (0,)), ((1,), (1,)), ((0,), (0,))


def halves(value):
    high = value.astype(BF16)
    return high, (value - high.astype(F32)).astype(BF16)


def dot16(left, right, dims):
    return lax.dot_general(left, right, (dims, ((), ())), preferred_element_type=F32)


def dot3(left, right, dims):
    left_high, left_low = halves(left)
    right_high, right_low = halves(right)
    return (
        dot16(left_high, right_high, dims)
        + dot16(left_low, right_high, dims)
        + dot16(left_high, right_low, dims)
    )


def horner(terms, square):
    total = terms[-1] * square + terms[-2]
    for term in terms[-3::-1]:
        total = total * square + term
    return total


def trig(columns, rows):
    turns = columns[0] * rows[0] + columns[1] * rows[1] + columns[2] * rows[2]
    turns = turns - jnp.round(turns)
    square = turns * turns
    half_sin = horner(HALF_SIN, square) * turns
    return 1.0 - half_sin * half_sin, half_sin * horner(HALF_COS, square)


def trig_blocks(k_ref, pos_ref, first, high_low, full=None):
    vectors, atoms = high_low[0].shape
    step = 32
    width = min(256, atoms)
    per_body = max(1, 4096 // atoms)
    per_body = min(per_body, vectors // step)

    def body(block, _):
        for inner in range(per_body):
            here = pl.ds(pl.multiple_of((block * per_body + inner) * step, step), step)
            columns = [k_ref[here, x : x + 1] for x in range(3)]
            for chunk in range(atoms // width):
                lanes = pl.ds(chunk * width, width)
                start = chunk * width if first is None else pl.multiple_of(first + chunk * width, 128)
                rows = [pos_ref[x : x + 1, pl.ds(start, width)] for x in range(3)]
                cos, sin = trig(columns, rows)
                high_low[0][here, lanes], high_low[1][here, lanes] = halves(cos)
                high_low[2][here, lanes], high_low[3][here, lanes] = halves(sin)
                if full is not None:
                    full[0][here, lanes], full[1][here, lanes] = cos, sin
        return 0

    lax.fori_loop(0, vectors // (step * per_body), body, 0)


def lattice_rows(packed, channels, vectors):
    share = packed.shape[1]
    width = min(share, vectors)
    chunks = [packed[channels + 3 * n : channels + 3 * n + 3, 0:width] for n in range(-(-vectors // share))]
    return jnp.concatenate(chunks, axis=1)


def tile_kernel(pos_ref, packed_ref, high_ref, low_ref, k_column, *, channels, vectors, first):
    rows = k_column.shape[0]
    k_column[:, 0:3] = lattice_rows(packed_ref, channels, vectors)[:, first : first + rows].T
    cos, sin = pl.ds(0, rows), pl.ds(rows, rows)
    trig_blocks(k_column, pos_ref, None, (high_ref.at[cos], low_ref.at[cos], high_ref.at[sin], low_ref.at[sin]))


def sum_over_atoms(tiles, lanes, value):
    count = value.shape[0]
    high, low = halves(value)
    tiles_high = jnp.concatenate([tile[:, lanes] for tile in tiles[::2]], axis=0)
    tiles_low = jnp.concatenate([tile[:, lanes] for tile in tiles[1::2]], axis=0)
    wide = dot16(tiles_high, jnp.concatenate([high, low], axis=0), NT)
    return wide[:, :count] + wide[:, count:] + dot16(tiles_low, high, NT)


def arranged(sums):
    rows = sums.shape[0] // 4
    parts = [sums[n * rows : (n + 1) * rows] for n in range(4)]
    return jnp.concatenate([jnp.concatenate(parts[:2], axis=1), jnp.concatenate(parts[2:], axis=1)], axis=0)


def split_by_core(total, keep_ref, send_ref):
    rows = keep_ref.shape[0]
    core = lax.axis_index("atoms") % 2
    for flip, out in enumerate((keep_ref, send_ref)):
        out[...] = total[pl.ds(pl.multiple_of((core ^ flip) * rows, rows), rows), :]


def halves_of_atoms(groups, atoms):
    side = lax.axis_index("kvec") // (groups // 2)
    span = atoms // 2
    return [pl.ds(pl.multiple_of(at * span, span), span) for at in (side, 1 - side)]


def adjoint_of(cotangent_ref, offset, mask_ref, w_out_ref):
    share = cotangent_ref.shape[1]
    lanes = pl.ds(pl.multiple_of((lax.axis_index("kvec") ^ offset) * share, share), share)
    return lanes, mask_ref[:, lanes] * dot3(w_out_ref[...], cotangent_ref[0 : w_out_ref.shape[0], :], NN)


def charge_kernel(pad_ref, feats_ref, species_ref, w_charge_ref, embed_ref, w_out_ref, *rest, groups):
    tiles, cotangents = rest[:4], rest[4 : 4 + groups // 2]
    keep_ref, send_ref, own_ref, mask_ref, part_ref, both, total = rest[4 + groups // 2 :]
    channels, atoms = feats_ref.shape
    embed_high, embed_low = halves(embed_ref[...])
    for block in range(atoms // 256):
        lanes = slice(block * 256, (block + 1) * 256)
        used = pad_ref[0:1, block : block + 1]
        mask = (lax.broadcasted_iota(jnp.int32, (1, 256), 1) < used).astype(F32)
        mask_ref[:, lanes] = mask
        species_at = lax.broadcasted_iota(jnp.int32, (embed_ref.shape[0], 256), 0)
        one_hot = (species_at == species_ref[:, lanes]).astype(BF16)
        both[0:channels, lanes] = mask * (
            dot3(w_charge_ref[...], feats_ref[:, lanes], TN)
            + dot16(embed_high, one_hot, TN)
            + dot16(embed_low, one_hot, TN)
        )
    for offset, cotangent in enumerate(cotangents):
        lanes, adjoint = adjoint_of(cotangent, offset, mask_ref, w_out_ref)
        both[channels:, lanes] = adjoint
        if offset == 0:
            own_ref[0:channels, :] = adjoint
            own_ref[channels : 2 * channels, :] = both[0:channels, lanes]
            own_ref[2 * channels :, :] = jnp.broadcast_to(mask_ref[:, lanes], (8, adjoint.shape[1]))
    near, far = halves_of_atoms(groups, atoms)
    sums = sum_over_atoms(tiles, near, both[:, near])
    total[...] = arranged(sums[:, :channels] + sum_over_atoms(tiles, far, both[0:channels, far]))
    split_by_core(total, keep_ref, send_ref)
    part_ref[...] = arranged(sums[:, channels:])


def adjoint_kernel(mask_ref, w_out_ref, part_ref, *rest, groups):
    tiles, cotangents = rest[:4], rest[4 : 4 + groups // 2]
    keep_ref, send_ref, adjoint_ref, total = rest[4 + groups // 2 :]
    for offset, cotangent in enumerate(cotangents):
        lanes, adjoint = adjoint_of(cotangent, groups // 2 + offset, mask_ref, w_out_ref)
        adjoint_ref[:, lanes] = adjoint
    _, far = halves_of_atoms(groups, adjoint_ref.shape[1])
    total[...] = part_ref[...] + arranged(sum_over_atoms(tiles, far, adjoint_ref[:, far]))
    split_by_core(total, keep_ref, send_ref)


def wave_kernel(pos_ref, packed_ref, width_ref, after_ref, *rest, atom_total):
    *gain_ref, cos, sin, cos_high, cos_low, sin_high, sin_low, k_ref, k_column = rest
    vectors = cos.shape[0]
    rows = vectors // 2
    core = lax.axis_index("atoms") % 2
    k_column[:, 0:3] = lattice_rows(packed_ref, width_ref.shape[1], vectors).T
    for flip in range(2):
        start = pl.multiple_of((core ^ flip) * rows, rows)
        k_ref[flip * rows : (flip + 1) * rows, :] = k_column[pl.ds(start, rows), :]
    if gain_ref:
        waves = [2.0 * math.pi * k_ref[0:rows, x : x + 1] for x in range(3)]
        square = waves[0] * waves[0] + waves[1] * waves[1] + waves[2] * waves[2]
        gain = jnp.exp(-square * width_ref[...]) * 40.0 / (square + 40.0) / math.sqrt(atom_total)
        gain_ref[0][...] = jnp.concatenate([gain, gain], axis=1)
    first = lax.axis_index("kvec") * cos.shape[1]
    trig_blocks(k_ref, pos_ref, first, (cos_high, cos_low, sin_high, sin_low), (cos, sin))


def coefficient_stack(sides, part):
    channels = sides[0].shape[2] // 2
    lanes = slice(part * channels, (part + 1) * channels)
    rows = [jnp.concatenate([side[0, :, lanes], side[1, :, lanes]], axis=1) for side in sides]
    high, low = halves(jnp.concatenate(rows, axis=0))
    return jnp.concatenate([high, low, high], axis=1)


def own_stack(own_ref, channels):
    high, low = halves(own_ref[0 : 2 * channels, :])
    return jnp.concatenate([high, high, low], axis=0)


def add_field(stack, tile_high, tile_low):
    width = stack.shape[1] // 3
    wide = dot16(stack[:, : 2 * width], tile_high, TN)
    return wide[:width] + wide[width:] + dot16(stack[:, :width], tile_low, TN)


def add_force(sums, wave, along, rows, first):
    step = 16
    cos, sin, _, _, _, _, k_ref = wave
    for start in range(0, rows.stop - rows.start, step):
        here = slice(rows.start + start, rows.start + start + step)
        there = slice(first + start, first + start + step)
        slope = cos[here, :] * along[1, there, :] - sin[here, :] * along[0, there, :]
        for x in range(3):
            term = k_ref[here, x : x + 1] * slope
            sums[x] = sums[x] + (term[0:8] + term[8:16])
    return sums


def fields(own_ref, refs, layout, channels, along, field, sums):
    entries = []
    for count, first in layout:
        wave, sides, refs = refs[:7], refs[7 : 7 + count], refs[7 + count :]
        rows = sides[0].shape[1]
        entries.append((wave, sides, slice(first * rows, (first + count) * rows)))
    stack = jnp.concatenate([coefficient_stack(sides, part) for part in range(2) for _, sides, _ in entries], axis=0)
    depth = stack.shape[0] // 2
    slopes = dot16(stack, own_stack(own_ref, channels), NN)
    for part in range(2):
        along[part] = slopes[part * depth : (part + 1) * depth]
    tiles = [
        jnp.concatenate([wave[at][rows, :] for at in kinds for wave, _, rows in entries], axis=0)
        for kinds in ((2, 4), (3, 5))
    ]
    added = add_field(stack, *tiles)
    field = added if field is None else field + added
    first = 0
    for wave, _, rows in entries:
        sums = add_force(sums, wave, along, rows, first)
        first += rows.stop - rows.start
    return field, sums


def partial_field_kernel(own_ref, *rest, layout, first):
    refs, field_ref, sums_ref, along = rest[:-3], *rest[-3:]
    share = own_ref.shape[1]
    if first:
        field, sums = None, [jnp.zeros((8, share), F32)] * 3
    else:
        refs, before = refs[:-2], refs[-2:]
        field, sums = before[0][...], [before[1][8 * x : 8 * x + 8, :] for x in range(3)]
    field, sums = fields(own_ref, refs, layout, field_ref.shape[0] // 2, along, field, sums)
    field_ref[...] = field
    for x in range(3):
        sums_ref[8 * x : 8 * x + 8, :] = sums[x]


def field_kernel(own_ref, w_out_ref, w_charge_ref, *rest, layout):
    refs, field_ref, sums_ref, message_ref, force_ref, grad_ref, along = rest[:-6], *rest[-6:]
    channels = w_out_ref.shape[0]
    sums = [sums_ref[8 * x : 8 * x + 8, :] for x in range(3)]
    field, sums = fields(own_ref, refs, layout, channels, along, field_ref[...], sums)
    field = own_ref[2 * channels : 2 * channels + 1, :] * field
    message_ref[...] = dot3(w_out_ref[...], field[:channels], TN)
    grad_ref[...] = dot3(w_charge_ref[...], field[channels:], NN)
    for x in range(3):
        force_ref[x : x + 1, :] = 2.0 * math.pi * jnp.sum(sums[x], axis=0, keepdims=True)


def swap(value, axis, offset):
    size = lax.axis_size(axis)
    return lax.ppermute(value, axis, [(place, place ^ offset) for place in range(size)])


def swap_along_z(value, even, odd):
    pairs = [(place, place ^ (odd if place % 2 else even)) for place in range(lax.axis_size("atoms"))]
    return lax.ppermute(value, "atoms", pairs)


def cost(work):
    return pl.CostEstimate(flops=work, bytes_accessed=0, transcendentals=0)


def on_device(
    positions, feats, species, pad_count, k_lattice, filter_width, w_charge, species_embed, w_out, grad_out,
):
    atom_count, group_count = lax.axis_size("atoms"), lax.axis_size("kvec")
    channels, atoms = feats.shape
    share = grad_out.shape[1]
    vectors = k_lattice.shape[1]
    half = vectors // 2
    both = 2 * channels
    f32 = lambda *shape: jax.ShapeDtypeStruct(shape, F32)
    bf16 = lambda *shape: jax.ShapeDtypeStruct(shape, BF16)

    def planes(value):
        return [swap(value, "kvec", m) for m in range(group_count - 1, 0, -1)][::-1]

    chunks = -(-vectors // share)
    below = -(-3 * chunks // 8) * 8
    packed = jnp.pad(grad_out, ((0, below), (0, 0)))
    for n in range(chunks):
        chunk = k_lattice[:, n * share : (n + 1) * share]
        first = channels + 3 * n
        packed += jnp.pad(chunk, ((first, channels + below - first - 3), (0, share - chunk.shape[1]))).astype(F32)

    packed = [packed] + planes(packed)

    tiles = []
    for part in range(2):
        tiles += pl.pallas_call(
            functools.partial(tile_kernel, channels=channels, vectors=vectors, first=part * half),
            out_shape=[bf16(vectors, atoms)] * 2,
            in_specs=[VMEM] * 2,
            out_specs=[VMEM] * 2,
            scratch_shapes=[pltpu.VMEM((half, 128), F32)],
            compiler_params=PARAMS,
            cost_estimate=cost(9000 * half * atoms),
            name="waves_of_own_vectors",
        )(positions, packed[0])

    middle = group_count // 2
    keep_h, send_h, own, mask, part = pl.pallas_call(
        functools.partial(charge_kernel, groups=group_count),
        out_shape=[f32(half, both)] * 2 + [f32(both + 8, share), f32(1, atoms), f32(vectors, both)],
        in_specs=[VMEM] * (10 + middle),
        out_specs=[VMEM] * 5,
        scratch_shapes=[pltpu.VMEM((both, atoms), F32), pltpu.VMEM((vectors, both), F32)],
        compiler_params=PARAMS,
        cost_estimate=cost(60 * vectors * atoms * channels),
        name="charge_sums",
    )(
        pad_count.reshape(1, -1), feats, species.reshape(1, atoms), w_charge, species_embed.T, w_out,
        *tiles, *packed[:middle],
    )

    wave_shapes = [f32(vectors, share)] * 2 + [bf16(vectors, share)] * 4 + [f32(vectors, 128)]

    def waves_of(group, after):
        shapes = ([f32(half, both)] if group == 0 else []) + wave_shapes
        made = pl.pallas_call(
            functools.partial(wave_kernel, atom_total=atoms * atom_count),
            out_shape=shapes,
            in_specs=[VMEM, VMEM, VMEM, ANY],
            out_specs=[VMEM] * len(shapes),
            scratch_shapes=[pltpu.VMEM((vectors, 128), F32)],
            compiler_params=PARAMS,
            cost_estimate=cost(20 * vectors * share),
            name="waves_of_own_atoms",
        )(positions, packed[group], filter_width.reshape(1, channels), after)
        return list(made)

    arrived_h = swap(send_h, "atoms", 1)
    keep_b, send_b = pl.pallas_call(
        functools.partial(adjoint_kernel, groups=group_count),
        out_shape=[f32(half, both)] * 2,
        in_specs=[VMEM] * (7 + middle),
        out_specs=[VMEM] * 2,
        scratch_shapes=[pltpu.VMEM((channels, atoms), F32), pltpu.VMEM((vectors, both), F32)],
        compiler_params=PARAMS,
        cost_estimate=cost(60 * vectors * atoms * channels),
        name="adjoint_sums",
    )(mask, w_out, part, *tiles, *packed[middle:])

    arrived_h, send_b = lax.optimization_barrier((arrived_h, send_b))
    arrived_b = swap(send_b, "atoms", 1)
    sum_h = keep_h + arrived_h
    steps = [2 << n for n in range((atom_count // 2).bit_length() - 1)]
    next_h = swap_along_z(sum_h, steps[0], steps[-1])
    arrived_b, sum_h = lax.optimization_barrier((arrived_b, sum_h))
    sum_b = keep_b + arrived_b
    next_b = swap_along_z(sum_b, steps[0], steps[-1])

    def more_waves(count, after):
        return [waves_of(group, after) for group in range(len(waves), min(len(waves) + count, group_count))]

    waves = []
    beside = more_waves(2, sum_b)
    next_h, next_b, beside = lax.optimization_barrier((next_h, next_b, beside))
    waves += beside
    total = jnp.stack([sum_h + next_h, sum_b + next_b])
    for at, step in enumerate(zip(steps[1:], steps[-2::-1])):
        arrived = swap_along_z(total, *step)
        beside = more_waves(group_count if at + 2 == len(steps) else 1, total)
        arrived, beside = lax.optimization_barrier((arrived, beside))
        waves += beside
        total = total + arrived
    gain, *waves[0] = waves[0]
    near = gain[None] * total
    plane = {0: near}
    for group in range(group_count - 1, 0, -1):
        plane[group] = swap(near, "kvec", group)
    far = {}

    def operands_of(parts):
        sides = [[plane[group], far.get(group)][first : first + count] for group, count, first in parts]
        return [ref for part, side in zip(parts, sides) for ref in list(waves[part[0]]) + side]

    def field_sizes(parts):
        layout = tuple(part[1:] for part in parts)
        return layout, pltpu.VMEM((2, sum(count for count, _ in layout) * half, share), F32)

    def partial_fields(parts, before):
        layout, scratch = field_sizes(parts)
        operands = [own, *operands_of(parts), *before]
        return pl.pallas_call(
            functools.partial(partial_field_kernel, layout=layout, first=not before),
            out_shape=[f32(both, share), f32(24, share)],
            in_specs=[VMEM] * len(operands),
            out_specs=[VMEM] * 2,
            scratch_shapes=[scratch],
            compiler_params=PARAMS,
            cost_estimate=cost(vectors * share),
            name="fields_of_some_groups",
        )(*operands)

    fields_so_far = partial_fields([(0, 1, 0)], [])
    late = [2, 1] if group_count > 3 else [1]
    early = [group for group in range(group_count - 1, 0, -1) if group not in late]
    for group in early:
        plane[group], near, fields_so_far = lax.optimization_barrier((plane[group], near, fields_so_far))
        if not far:
            far[0] = swap(near, "atoms", 1)
        far[group] = swap(plane[group], "atoms", 1)
    fields_so_far = partial_fields([(group, 1, 0) for group in early], fields_so_far)
    for group in late:
        plane[group], fields_so_far = lax.optimization_barrier((plane[group], fields_so_far))
        far[group] = swap(plane[group], "atoms", 1)
    parts = [(group, 1, 1) for group in [0] + early] + [(group, 1, 0) for group in late]
    fields_so_far = partial_fields(parts, fields_so_far)

    parts = [(group, 1, 1) for group in late]
    layout, scratch = field_sizes(parts)
    operands = [own, w_out, w_charge, *operands_of(parts), *fields_so_far]
    return tuple(
        pl.pallas_call(
            functools.partial(field_kernel, layout=layout),
            out_shape=[f32(channels, share), f32(3, share), f32(channels, share)],
            in_specs=[VMEM] * len(operands),
            out_specs=[VMEM] * 3,
            scratch_shapes=[scratch],
            compiler_params=PARAMS,
            cost_estimate=cost(vectors * share),
            name="fields_and_forces",
        )(*operands)
    )


def solution(mesh):
    shared = P(None, ("atoms", "kvec"))
    placed = (
        P(None, "atoms"), P(None, "atoms"), P("atoms"), P("atoms"), P(None, "kvec"),
        P(), P(), P(), P(), shared,
    )
    return jax.shard_map(
        on_device, mesh=mesh, in_specs=placed, out_specs=(shared, shared, shared), check_vma=False
    )
```
